32 devices in a mesh: dp: 4 (over x, core), seq: 8 (over z, y).
Axes of the slice: x: 2, y: 2, z: 4, core: 2. Of those that a mesh axis runs over, the one named last changes fastest.
Arguments:
- inputs: bfloat16 [8, 2048, 512], P('dp', 'seq'), may hold values from -6 to 6
- encoder: bfloat16 [8, 2048, 512], P('dp', 'seq'), may hold values from -6 to 6
- tgt_seg: int32 [8, 2048], P('dp'), may hold values from 0 to 7, never falling along the last dimension, each value on 1 to 1024 neighbouring positions
- src_len: int32 [8, 8], P('dp'), may hold values from 1 to 1024, 2048 in all within a row
- cotangent: bfloat16 [8, 2048, 512], P('dp', 'seq'), may hold values from -6 to 6
- self_in: bfloat16 [512, 1536], P(('dp', 'seq')), may hold values from -0.25 to 0.25
- self_out: bfloat16 [512, 512], P(('dp', 'seq')), may hold values from -0.5 to 0.5
- cross_q: bfloat16 [512, 512], P(('dp', 'seq')), may hold values from -0.25 to 0.25
- cross_kv: bfloat16 [512, 1024], P(('dp', 'seq')), may hold values from -0.25 to 0.25
- cross_out: bfloat16 [512, 512], P(('dp', 'seq')), may hold values from -0.5 to 0.5
- ffn_in: bfloat16 [512, 2048], P(('dp', 'seq')), may hold values from -0.25 to 0.25
- ffn_out: bfloat16 [2048, 512], P(('dp', 'seq')), may hold values from -0.125 to 0.125
- norm_params: bfloat16 [512, 6], P(('dp', 'seq')), may hold values from -1 to 1.25, as said below
Outputs:
- outputs: float32 [8, 2048, 512], P('dp', 'seq')
- grad_inputs: float32 [8, 2048, 512], P('dp', 'seq')
- grad_encoder: float32 [8, 2048, 512], P('dp', 'seq')
- grad_self_in: float32 [512, 1536], P(('dp', 'seq'))
- grad_self_out: float32 [512, 512], P(('dp', 'seq'))
- grad_cross_q: float32 [512, 512], P(('dp', 'seq'))
- grad_cross_kv: float32 [512, 1024], P(('dp', 'seq'))
- grad_cross_out: float32 [512, 512], P(('dp', 'seq'))
- grad_ffn_in: float32 [512, 2048], P(('dp', 'seq'))
- grad_ffn_out: float32 [2048, 512], P(('dp', 'seq'))
- grad_norm_params: float32 [512, 6], P(('dp', 'seq'))
The draws below stay inside these ranges and needn't reach their ends.
Inputs may be any that keep to these rules, and one draw needn't show every extreme that they name: `tgt_seg`: ids never fall along a sequence; each document has 1 to 1024 tokens. `src_len`: each row sums to 2048. `norm_params`: columns 0, 2, 4 are gains, columns 1, 3, 5 shifts.
All inputs are finite; a program needn't handle non-finite values.
Results may differ from the reference program's by a relative error of at most 0.018.
Values may be sent and summed in bfloat16 or wider, within the bound.
No kernel may reach another device: no remote copies, remote signals or barrier semaphores. Data moves between devices by JAX's collectives and lax.ppermute only.
A program may use at most 192 MiB of HBM per device.

```python
import math
import jax
import jax.numpy as jnp
import numpy as np
from jax import lax

D = 512
HEADS = 8
FF = 2048
HEAD_DIM = 64
LEN = 2048
SRC_LEN = 2048
DOCS = 8
NSEQ = 8


def draw_norm_params(key, part):
    first_key, second_key = jax.random.split(jax.random.fold_in(key, 11))
    gains = jax.random.uniform(first_key, (D, 3), jnp.float32, 0.75, 1.25)
    shifts = jnp.clip(0.3 * jax.random.normal(second_key, (D, 3), jnp.float32), -1.0, 1.0)
    return jnp.stack([gains, shifts], axis=2).reshape(D, 6).astype(jnp.bfloat16)


def steps_of(stream_key, dims, cuts, smallest, high):
    factor_of = 1.0
    for position, parts in cuts:
        steps = jax.random.uniform(jax.random.fold_in(jax.random.fold_in(stream_key, 6), position), (parts,), jnp.float32, smallest / len(cuts), high / len(cuts))
        factor_of = factor_of * jnp.repeat(jnp.exp(steps), dims[position] // parts).reshape((-1,) + (1,) * (len(dims) - 1 - position))
    return factor_of


def profile(number_of, total, most, lean):
    portions = [(1 << 20) // math.isqrt(rank ** lean) + 1 for rank in range(2, number_of + 1)]
    surplus, given = total - most - (number_of - 1), [1] * (number_of - 1)
    while surplus > 0:
        candidates = [i for i in range(number_of - 1) if given[i] < most]
        pool, budget = sum([portions[i] for i in candidates]), surplus
        for i in candidates:
            extra = min(most - given[i], max(1, budget * portions[i] // pool), surplus)
            given[i] = given[i] + extra
            surplus = surplus - extra
    return np.array([most] + given)


def ragged(key, number_of, total, bound, slope):
    if number_of == 2:
        one = jax.random.randint(key, (), max(1, total - bound), min(bound, total - 1) + 1)
        return jnp.stack([one, total - one])
    sizes = jnp.asarray(profile(number_of, total, bound, slope), jnp.int32)
    pairs = (number_of - 1) // 2
    source_of, receiver = sizes[1:1 + 2 * pairs:2], sizes[2:2 + 2 * pairs:2]
    room = jnp.minimum(source_of - 1, bound - receiver)
    passed = jax.random.randint(jax.random.fold_in(key, 1), (pairs,), 0, 1 << 20) % (room + 1)
    sizes = sizes.at[1:1 + 2 * pairs:2].set(source_of - passed).at[2:2 + 2 * pairs:2].set(receiver + passed)
    return sizes[jax.random.permutation(jax.random.fold_in(key, 2), number_of)]


def bell_draw(own_key, extent, deviation, limit, cuts=(), kind=jnp.bfloat16):
    drawn = jax.random.normal(own_key, extent, jnp.float32) * deviation
    if len(cuts) > 0:
        drawn = steps_of(own_key, extent, cuts, -0.22, 0.18) * drawn
    return jnp.clip(drawn, min=-limit, max=limit).astype(kind)


def setup_inputs(seed: int = 0) -> dict:
    keys = jax.random.split(jax.random.key(seed), 14)
    inputs = bell_draw(keys[0], (NSEQ, LEN, D), 1.0, 6.0, ((0, 4), (1, 8)))
    encoder = bell_draw(keys[1], (NSEQ, SRC_LEN, D), 1.0, 6.0, ((0, 4), (1, 8)))
    tgt_seg = jax.vmap(lambda own: jnp.searchsorted(jnp.cumsum(ragged(own, DOCS, LEN, LEN // 2, 2)), jnp.arange(LEN), side="right"))(jax.random.split(keys[2], NSEQ)).reshape((NSEQ, LEN)).astype(jnp.int32)
    src_len = jax.vmap(lambda own: ragged(own, DOCS, SRC_LEN, SRC_LEN // 2, 2))(jax.random.split(keys[3], NSEQ)).reshape((NSEQ, DOCS)).astype(jnp.int32)
    cotangent = bell_draw(keys[4], (NSEQ, LEN, D), 1.0, 6.0, ((0, 4), (1, 8)))
    self_in = bell_draw(keys[5], (D, 3 * D), D ** -0.5, 0.25, ((0, 32),))
    self_out = bell_draw(keys[6], (D, D), (D // 4) ** -0.5, 0.5, ((0, 32),))
    cross_q = bell_draw(keys[7], (D, D), D ** -0.5, 0.25, ((0, 32),))
    cross_kv = bell_draw(keys[8], (D, 2 * D), D ** -0.5, 0.25, ((0, 32),))
    cross_out = bell_draw(keys[9], (D, D), (D // 4) ** -0.5, 0.5, ((0, 32),))
    ffn_in = bell_draw(keys[10], (D, FF), D ** -0.5, 0.25, ((0, 32),))
    ffn_out = bell_draw(keys[11], (FF, D), FF ** -0.5, 0.125, ((0, 32),))
    norm_params = draw_norm_params(jax.random.fold_in(keys[13], 71), 0)
    return {"inputs": inputs, "encoder": encoder, "tgt_seg": tgt_seg, "src_len": src_len, "cotangent": cotangent, "self_in": self_in, "self_out": self_out, "cross_q": cross_q, "cross_kv": cross_kv, "cross_out": cross_out, "ffn_in": ffn_in, "ffn_out": ffn_out, "norm_params": norm_params}


@jax.custom_vjp
def low(v):
    return lax.optimization_barrier(v.astype(jnp.bfloat16)).astype(jnp.float32)

@jax.custom_vjp
def low_back(v):
    return v

def low_keep(v):
    return (low(v), None)

def low_pass(kept, grad):
    return (grad,)

def back_keep(v):
    return (v, None)

def back_low(kept, grad):
    return (low(grad),)
low.defvjp(low_keep, low_pass)
low_back.defvjp(back_keep, back_low)

def round_both(array_in):
    return low_back(low(array_in))

def matmul_high(left, right):
    return jnp.dot(left, right, precision=lax.Precision.HIGHEST, preferred_element_type=jnp.float32)

def split_heads(array_in):
    return array_in.reshape(array_in.shape[0], HEADS, HEAD_DIM)

def attention(queries, keys_in, values_in, allowed):
    scores = jnp.einsum('rhd,khd->hrk', split_heads(queries), split_heads(keys_in), precision=lax.Precision.HIGHEST) * HEAD_DIM ** (-0.5)
    scores = low_back(scores)
    scores = jnp.where(allowed[None], scores, -1e+30)
    weights = low(jax.nn.softmax(scores, axis=-1))
    mixed_out = jnp.einsum('hrk,khd->rhd', weights, split_heads(values_in), precision=lax.Precision.HIGHEST)
    return round_both(mixed_out.reshape(queries.shape[0], D))

def layer_norm(resid, gain, shift):
    centered = resid - lax.optimization_barrier(jnp.mean(resid, axis=-1, keepdims=True))
    spread = lax.optimization_barrier(jnp.mean(centered * centered, axis=-1, keepdims=True))
    return centered * lax.rsqrt(spread + 1e-05) * gain + shift

def source_ids(lengths):
    ends = jnp.cumsum(lengths.astype(jnp.int32), dtype=jnp.int32).astype(jnp.int32)
    positions = jnp.arange(SRC_LEN, dtype=jnp.int32)
    return lax.optimization_barrier(jnp.sum((positions[:, None] >= ends[None, :]).astype(jnp.int32), axis=1, dtype=jnp.int32)).astype(jnp.int32)

def decoder_layer(tokens_now, source_now, target_ids, source_ids_now, params_now):
    w_self_in, w_self_out, w_cross_q, w_cross_kv, w_cross_out, w_ffn_in, w_ffn_out, norm_table = params_now
    projected = matmul_high(tokens_now, w_self_in)
    queries = round_both(projected[:, :D])
    keys_self = round_both(projected[:, D:2 * D])
    values_self = round_both(projected[:, 2 * D:])
    mixed_self = attention(queries, keys_self, values_self, target_ids[:, None] == target_ids[None, :])
    resid_one = tokens_now + low_back(matmul_high(mixed_self, w_self_out))
    normed_one = layer_norm(resid_one, norm_table[:, 0], norm_table[:, 1])
    queries_cross = round_both(matmul_high(low(normed_one), w_cross_q))
    source_pairs = matmul_high(source_now, w_cross_kv)
    keys_cross = round_both(source_pairs[:, :D])
    values_cross = round_both(source_pairs[:, D:])
    mixed_cross = attention(queries_cross, keys_cross, values_cross, target_ids[:, None] == source_ids_now[None, :])
    resid_two = normed_one + low_back(matmul_high(mixed_cross, w_cross_out))
    normed_two = layer_norm(resid_two, norm_table[:, 2], norm_table[:, 3])
    hidden_pre = low_back(matmul_high(low(normed_two), w_ffn_in))
    hidden = low(jax.nn.gelu(hidden_pre, approximate=True))
    resid_three = normed_two + low_back(matmul_high(hidden, w_ffn_out))
    return layer_norm(resid_three, norm_table[:, 4], norm_table[:, 5])

def reference(inputs, encoder, tgt_seg, src_len, cotangent, self_in, self_out, cross_q, cross_kv, cross_out, ffn_in, ffn_out, norm_params):
    params = tuple((weight_now.astype(jnp.float32) for weight_now in (self_in, self_out, cross_q, cross_kv, cross_out, ffn_in, ffn_out, norm_params)))
    source_all = jax.vmap(source_ids)(src_len)

    def whole_batch(tokens_all, sources_all, params_now):

        def per_sequence(pieces):
            return decoder_layer(pieces[0], pieces[1], pieces[2], pieces[3], params_now)
        return lax.map(jax.checkpoint(per_sequence), (tokens_all, sources_all, tgt_seg.astype(jnp.int32), source_all))
    outputs, pullback = jax.vjp(whole_batch, inputs.astype(jnp.float32), encoder.astype(jnp.float32), params)
    grad_inputs, grad_encoder, grad_params = pullback(cotangent.astype(jnp.float32))
    return (outputs, grad_inputs, grad_encoder, grad_params[0], grad_params[1], grad_params[2], grad_params[3], grad_params[4], grad_params[5], grad_params[6], grad_params[7])
```

```python
import functools

import jax
import jax.numpy as jnp
from jax import lax
from jax.experimental import pallas as pl
from jax.experimental.pallas import tpu as pltpu
from jax.sharding import PartitionSpec as P

HEAD_DIM = 64
GROUP = 4
LANES = GROUP * HEAD_DIM
BF = jnp.bfloat16
F32 = jnp.float32
VMEM_LIMIT = 56 * 2**20


def dot_f32(left, right):
    return jnp.dot(left, right, preferred_element_type=F32)


def dot_nt(left, right):
    return lax.dot_general(left, right, (((1,), (1,)), ((), ())), preferred_element_type=F32)


def dot_tn(left, right):
    return lax.dot_general(left, right, (((0,), (0,)), ((), ())), preferred_element_type=F32)


def head_of_lane(rows):
    return lax.broadcasted_iota(jnp.int32, (rows, LANES), 1) // HEAD_DIM


def stack_heads(tile):
    head = head_of_lane(tile.shape[0])
    zero = jnp.zeros_like(tile)
    return jnp.concatenate([jnp.where(head == h, tile, zero) for h in range(GROUP)], axis=0)


def unstack_heads(tile):
    rows = tile.shape[0] // GROUP
    head = head_of_lane(rows)
    out = tile[:rows]
    for h in range(1, GROUP):
        out = jnp.where(head == h, tile[h * rows : (h + 1) * rows], out)
    return out


def row_of(column):
    wide = jnp.broadcast_to(column, (column.shape[0], 128))
    return jnp.transpose(wide)[0:1, :]


def attend_kernel(place_ref, q_ref, kv_ref, qseg_ref, kseg_ref, o_ref, lse_ref, s_ref, m_ref, acc_ref):
    width = q_ref.shape[1]
    blocks = qseg_ref.shape[0]
    rows = q_ref.shape[0] // blocks
    keys = kseg_ref.shape[1]
    me = place_ref[2, 0]

    def block(k, carry):
        lo, hi = place_ref[0, k], place_ref[1, k]
        q_rows = pl.ds(pl.multiple_of(k * rows, rows), rows)
        qseg = qseg_ref[k]
        qseg = jnp.concatenate([qseg] * GROUP, axis=0)
        for g in range(width // LANES):
            cols = slice(g * LANES, (g + 1) * LANES)
            v_cols = slice(width + g * LANES, width + (g + 1) * LANES)
            stacked = stack_heads(q_ref[q_rows, cols])
            m_ref[...] = jnp.full(m_ref.shape, -3e38, F32)

            def first(b, carry):
                k_rows = pl.ds(pl.multiple_of((b ^ me) * keys, keys), keys)
                scores = dot_nt(stacked, kv_ref[k_rows, cols])
                scores = jnp.where(qseg == kseg_ref[pl.ds(b, 1), :], scores, -1e30)
                s_ref[b] = scores
                m_ref[...] = jnp.maximum(m_ref[...], scores)
                return carry

            lax.fori_loop(lo, hi, first, 0)
            top = jnp.max(m_ref[...], axis=1, keepdims=True)
            m_ref[...] = jnp.zeros(m_ref.shape, F32)
            acc_ref[...] = jnp.zeros(acc_ref.shape, F32)

            def second(b, carry):
                k_rows = pl.ds(pl.multiple_of((b ^ me) * keys, keys), keys)
                weights = jnp.exp(s_ref[b] - top)
                m_ref[...] += weights
                acc_ref[...] += dot_f32(weights.astype(BF), kv_ref[k_rows, v_cols])
                return carry

            lax.fori_loop(lo, hi, second, 0)
            total = jnp.sum(m_ref[...], axis=1, keepdims=True)
            o_ref[q_rows, cols] = unstack_heads(acc_ref[...] / total).astype(BF)
            lse_ref[k * (width // LANES) + g] = row_of(top + jnp.log(total))
        return carry

    lax.fori_loop(0, blocks, block, 0)


def attend_back_kernel(
    place_ref, q_ref, do_ref, o_ref, lse_ref, kv_ref, qseg_ref, kseg_ref, dq_ref, dkv_ref, sum_ref, dqt_ref
):
    width = q_ref.shape[1]
    blocks = qseg_ref.shape[0]
    rows = q_ref.shape[0] // blocks
    total = kv_ref.shape[0]
    me = place_ref[2, 0]
    keys = place_keys(total, blocks, place_ref)
    sum_ref[...] = jnp.zeros(sum_ref.shape, F32)

    def block(k, carry):
        lo, hi = place_ref[0, k], place_ref[1, k]
        q_rows = pl.ds(pl.multiple_of(k * rows, rows), rows)
        qseg = qseg_ref[k]
        qseg = jnp.concatenate([qseg] * GROUP, axis=1)
        for g in range(width // LANES):
            cols = slice(g * LANES, (g + 1) * LANES)
            v_cols = slice(width + g * LANES, width + (g + 1) * LANES)
            q_st = stack_heads(q_ref[q_rows, cols])
            do_tile = do_ref[q_rows, cols]
            do_st = stack_heads(do_tile)
            prod = do_tile.astype(F32) * o_ref[q_rows, cols].astype(F32)
            delta = row_of(jnp.sum(stack_heads(prod), axis=1, keepdims=True))
            lse = lse_ref[k * (width // LANES) + g]
            dqt_ref[...] = jnp.zeros(dqt_ref.shape, F32)

            def step(b, carry):
                k_rows = pl.ds(pl.multiple_of((b ^ me) * keys, keys), keys)
                k_tile = kv_ref[k_rows, cols]
                kseg = kseg_ref[pl.ds(pl.multiple_of(b * keys, keys), keys), :]
                scores = dot_nt(k_tile, q_st)
                soft = jnp.where(kseg == qseg, jnp.exp(scores - lse), 0.0)
                d_soft = dot_nt(kv_ref[k_rows, v_cols], do_st)
                d_scores = (soft * (d_soft - delta)).astype(BF)
                sum_ref[k_rows, cols] += dot_f32(d_scores, q_st)
                sum_ref[k_rows, v_cols] += dot_f32(soft.astype(BF), do_st)
                dqt_ref[...] += dot_tn(k_tile, d_scores)
                return carry

            lax.fori_loop(lo, hi, step, 0)
            dq_ref[q_rows, cols] = unstack_heads(jnp.transpose(dqt_ref[...]) * HEAD_DIM**-0.5).astype(BF)
        return carry

    lax.fori_loop(0, blocks, block, 0)
    dkv_ref[...] = sum_ref[...].astype(BF)


def place_keys(total, blocks, place_ref):
    return total // place_ref.shape[1]


SMEM = pl.BlockSpec(memory_space=pltpu.SMEM)
VMEM = pl.BlockSpec(memory_space=pltpu.VMEM)


def attend(place, queries, pairs, qseg, kseg):
    own, width = queries.shape
    blocks = qseg.shape[0]
    rows = own // blocks
    count, keys = kseg.shape
    groups = width // LANES
    return pl.pallas_call(
        attend_kernel,
        out_shape=(
            jax.ShapeDtypeStruct((own, width), BF),
            jax.ShapeDtypeStruct((blocks * groups, 1, GROUP * rows), F32),
        ),
        in_specs=[SMEM] + [VMEM] * 4,
        out_specs=(VMEM, VMEM),
        scratch_shapes=[
            pltpu.VMEM((count, GROUP * rows, keys), F32),
            pltpu.VMEM((GROUP * rows, keys), F32),
            pltpu.VMEM((GROUP * rows, LANES), F32),
        ],
        compiler_params=pltpu.CompilerParams(vmem_limit_bytes=VMEM_LIMIT),
        cost_estimate=pl.CostEstimate(
            flops=8 * own * count * keys * width // 4, bytes_accessed=6 * 2**20, transcendentals=own * count * keys * 8 // 4
        ),
    )(place, queries, pairs, qseg[:, :, None], kseg)


def attend_back(place, queries, d_mixed, mixed, lse, pairs, qseg, kseg):
    own, width = queries.shape
    blocks = qseg.shape[0]
    rows = own // blocks
    count, keys = kseg.shape
    return pl.pallas_call(
        attend_back_kernel,
        out_shape=(
            jax.ShapeDtypeStruct((own, width), BF),
            jax.ShapeDtypeStruct(pairs.shape, BF),
        ),
        in_specs=[SMEM] + [VMEM] * 7,
        out_specs=(VMEM, VMEM),
        scratch_shapes=[
            pltpu.VMEM(pairs.shape, F32),
            pltpu.VMEM((LANES, GROUP * rows), F32),
        ],
        compiler_params=pltpu.CompilerParams(vmem_limit_bytes=VMEM_LIMIT),
        cost_estimate=pl.CostEstimate(
            flops=20 * own * count * keys * width // 4, bytes_accessed=8 * 2**20, transcendentals=own * count * keys * 8 // 4
        ),
    )(place, queries, d_mixed, mixed, lse, pairs, qseg[:, None, :], kseg.reshape(-1, 1))


def layer_norm(resid, gain, shift):
    centered = resid - jnp.mean(resid, axis=-1, keepdims=True)
    inv_std = lax.rsqrt(jnp.mean(centered * centered, axis=-1, keepdims=True) + 1e-05)
    normed = centered * inv_std
    return (normed * gain + shift, normed, inv_std)


def norm_back(upstream, normed, inv_std, gain):
    scaled_grad = upstream * gain
    centered_grad = (
        scaled_grad
        - jnp.mean(scaled_grad, axis=-1, keepdims=True)
        - normed * jnp.mean(scaled_grad * normed, axis=-1, keepdims=True)
    )
    return (centered_grad * inv_std, jnp.sum(upstream * normed, axis=0), jnp.sum(upstream, axis=0))


def smooth_gate(values_in):
    return jax.nn.gelu(values_in, approximate=True)


def unxor(parts, place):
    out = jnp.zeros((len(parts),) + parts[0].shape, parts[0].dtype)
    for k, part in enumerate(parts):
        out = lax.dynamic_update_index_in_dim(out, part, place ^ k, 0)
    return out


def body(
    inputs,
    encoder,
    tgt_seg,
    src_len,
    cotangent,
    self_in,
    self_out,
    cross_q,
    cross_kv,
    cross_out,
    ffn_in,
    ffn_out,
    norm_params,
):
    held, local_rows, width = inputs.shape
    half = local_rows // 2
    dp_count, seq_count = lax.axis_size("dp"), lax.axis_size("seq")
    length = local_rows * seq_count
    x_count = dp_count // 2
    z_count = 2 * held
    y_count = seq_count // z_count
    dp_place, seq_place = lax.axis_index("dp"), lax.axis_index("seq")
    x_place, c_place = dp_place // 2, dp_place % 2
    z_place, y_place = seq_place // y_count, seq_place % y_count

    def over_core(v):
        return lax.ppermute(v, "dp", [(i, i ^ 1) for i in range(dp_count)])

    def over_x(v, k):
        return v if k == 0 else lax.ppermute(v, "dp", [(i, i ^ (2 * k)) for i in range(dp_count)])

    def over_y(v, k):
        return v if k == 0 else lax.ppermute(v, "seq", [(i, i ^ k) for i in range(seq_count)])

    def over_z(v, k):
        return v if k == 0 else lax.ppermute(v, "seq", [(i, i ^ (k * y_count)) for i in range(seq_count)])

    def pick(v, place):
        return lax.dynamic_index_in_dim(v, place, 0, keepdims=False)

    def to_work(v):
        halves = v.reshape(held, 2, half, width)
        mine = lax.dynamic_index_in_dim(halves, c_place, 1, keepdims=False)
        other = over_core(lax.dynamic_index_in_dim(halves, 1 - c_place, 1, keepdims=False))
        both = jnp.concatenate([mine, other], axis=0)
        return [over_z(pick(both, (z_place ^ k) ^ (held * c_place)), k) for k in range(z_count)]

    def gather_sequence(parts):
        out = []
        for part in parts:
            for l in range(y_count):
                moved = over_y(part, l)
                out += [moved, over_core(moved)]
        return jnp.concatenate(out, axis=0)

    def reduce_sequence(v):
        blocks = v.reshape(z_count, y_count, 2, half, width)
        kept = blocks[:, :, 0] + over_core(blocks[:, :, 1].astype(BF)).astype(F32)
        total = []
        for k in range(z_count):
            part = kept[k, 0]
            for l in range(1, y_count):
                part = part + over_y(kept[k, l].astype(BF), l).astype(F32)
            total.append(part)
        return total

    def to_home(parts):
        moved = unxor([over_z(part.astype(BF), k) for k, part in enumerate(parts)], z_place)
        moved = moved.reshape(2, held, half, width)
        mine = pick(moved, c_place)
        other = over_core(pick(moved, 1 - c_place))
        out = unxor([mine, other], c_place)
        return out.transpose(1, 0, 2, 3).reshape(held, local_rows, width).astype(F32)

    def gather_rows(shard):
        rows, columns = shard.shape
        chunk = unxor([over_z(shard, k) for k in range(z_count)], z_place)
        chunk = unxor([over_y(chunk, l) for l in range(y_count)], y_place)
        chunk = chunk.transpose(1, 0, 2, 3).reshape(seq_count * rows, columns)
        chips = [over_x(chunk, k) for k in range(x_count)]
        cores = [unxor([part, over_core(part)], c_place) for part in chips]
        return unxor(cores, x_place).reshape(dp_count * seq_count * rows, columns)

    def scatter_rows(grad):
        columns = grad.shape[1]
        rows = grad.shape[0] // (dp_count * seq_count)
        parts = grad.reshape(x_count, 2, seq_count * rows, columns)
        kept = lax.dynamic_index_in_dim(parts, c_place, 1, keepdims=False) + over_core(
            lax.dynamic_index_in_dim(parts, 1 - c_place, 1, keepdims=False).astype(BF)
        ).astype(F32)
        total = pick(kept, x_place)
        for k in range(1, x_count):
            total = total + over_x(pick(kept, x_place ^ k).astype(BF), k).astype(F32)
        parts = total.reshape(z_count, y_count, rows, columns)
        kept = lax.dynamic_index_in_dim(parts, y_place, 1, keepdims=False)
        for l in range(1, y_count):
            kept = kept + over_y(
                lax.dynamic_index_in_dim(parts, y_place ^ l, 1, keepdims=False).astype(BF), l
            ).astype(F32)
        total = pick(kept, z_place)
        for k in range(1, z_count):
            total = total + over_z(pick(kept, z_place ^ k).astype(BF), k).astype(F32)
        return total

    def sum_everywhere(v):
        v = v + over_core(v)
        for k in (1 << i for i in range(x_count.bit_length() - 1)):
            v = v + over_x(v, k)
        for k in (1 << i for i in range(y_count.bit_length() - 1)):
            v = v + over_y(v, k)
        for k in (1 << i for i in range(z_count.bit_length() - 1)):
            v = v + over_z(v, k)
        return v

    both_seg = jnp.concatenate([tgt_seg, over_core(tgt_seg)], axis=0)
    target_all = pick(both_seg, z_place ^ (held * c_place))
    both_len = jnp.concatenate([src_len, over_core(src_len)], axis=0)
    lengths = pick(both_len, z_place ^ (held * c_place))
    docs = lengths.shape[0]
    upto = lax.broadcasted_iota(jnp.int32, (docs, docs), 0) <= lax.broadcasted_iota(jnp.int32, (docs, docs), 1)
    ends = jnp.sum(jnp.where(upto, lengths[:, None], 0), axis=0, dtype=jnp.int32)
    positions = jnp.arange(length, dtype=jnp.int32)
    source_all = jnp.sum((positions[:, None] >= ends[None, :]).astype(jnp.int32), axis=1, dtype=jnp.int32)
    place = seq_place * 2 + c_place
    by_block = target_all.reshape(-1, half)
    qseg = jnp.stack([pick(by_block, place ^ (k * 2 * y_count)) for k in range(z_count)])
    keys = 2 * half

    def in_order(segments):
        pairs = segments.reshape(-1, 2, half)
        return jnp.where(c_place == 0, pairs, pairs[:, ::-1]).reshape(-1, keys)

    def visits(segments):
        low = jnp.sum((segments[None, :] < qseg[:, :1]).astype(jnp.int32), axis=1, dtype=jnp.int32)
        high = jnp.sum((segments[None, :] <= qseg[:, -1:]).astype(jnp.int32), axis=1, dtype=jnp.int32)
        rest = length // keys - z_count
        table = jnp.stack([low // keys, (high + keys - 1) // keys, jnp.zeros_like(low) + seq_place])
        return jnp.pad(table, ((0, 0), (0, rest)))

    self_kseg, cross_kseg = in_order(target_all), in_order(source_all)
    self_visits, cross_visits = visits(target_all), visits(source_all)

    x_parts = to_work(inputs)
    x_own = jnp.concatenate(x_parts, axis=0)
    x_all = gather_sequence(x_parts)
    w_self_in = gather_rows(self_in)
    w_self_out = gather_rows(self_out)
    norm_wide = jnp.pad(norm_params, ((0, 0), (0, 128 - norm_params.shape[1])))
    norm_table = gather_rows(norm_wide).astype(F32)
    source_parts = to_work(encoder)
    source_everything = gather_sequence(source_parts)
    w_cross_kv = gather_rows(cross_kv)
    w_cross_q = gather_rows(cross_q)
    w_cross_out = gather_rows(cross_out)
    w_ffn_in = gather_rows(ffn_in)
    w_ffn_out = gather_rows(ffn_out)
    upstream = jnp.concatenate(to_work(cotangent), axis=0).astype(F32)
    scaling = HEAD_DIM**-0.5

    queries = (dot_f32(x_own, w_self_in[:, :width]) * scaling).astype(BF)
    self_pairs = dot_f32(x_all, w_self_in[:, width:]).astype(BF)
    mixed_self, self_lse = attend(self_visits, queries, self_pairs, qseg, self_kseg)
    resid_one = x_own.astype(F32) + dot_f32(mixed_self, w_self_out)
    normed_one, hat_one, inv_one = layer_norm(resid_one, norm_table[:, 0], norm_table[:, 1])
    low_one = normed_one.astype(BF)
    queries_cross = (dot_f32(low_one, w_cross_q) * scaling).astype(BF)
    cross_pairs = dot_f32(source_everything, w_cross_kv).astype(BF)
    mixed_cross, cross_lse = attend(cross_visits, queries_cross, cross_pairs, qseg, cross_kseg)
    resid_two = normed_one + dot_f32(mixed_cross, w_cross_out)
    normed_two, hat_two, inv_two = layer_norm(resid_two, norm_table[:, 2], norm_table[:, 3])
    low_two = normed_two.astype(BF)
    hidden_pre = dot_f32(low_two, w_ffn_in)
    hidden = smooth_gate(hidden_pre).astype(BF)
    resid_three = normed_two + dot_f32(hidden, w_ffn_out)
    layer_out, hat_three, inv_three = layer_norm(resid_three, norm_table[:, 4], norm_table[:, 5])
    out_tokens = to_home(list(layer_out.reshape(z_count, half, width)))

    d_resid_three, gain_three, shift_three = norm_back(upstream, hat_three, inv_three, norm_table[:, 4])
    d_branch_ffn = d_resid_three.astype(BF)
    g_ffn_out = scatter_rows(dot_tn(hidden, d_branch_ffn))
    d_hidden = dot_nt(d_branch_ffn, w_ffn_out)
    gate_pull = jax.vjp(smooth_gate, hidden_pre)[1]
    d_pre = gate_pull(d_hidden)[0].astype(BF)
    g_ffn_in = scatter_rows(dot_tn(low_two, d_pre))
    d_normed_two = d_resid_three + dot_nt(d_pre, w_ffn_in)
    d_resid_two, gain_two, shift_two = norm_back(d_normed_two, hat_two, inv_two, norm_table[:, 2])
    d_branch_cross = d_resid_two.astype(BF)
    g_cross_out = scatter_rows(dot_tn(mixed_cross, d_branch_cross))
    d_mixed_cross = dot_nt(d_branch_cross, w_cross_out).astype(BF)
    d_queries_cross, d_cross_pairs = attend_back(
        cross_visits, queries_cross, d_mixed_cross, mixed_cross, cross_lse, cross_pairs, qseg, cross_kseg
    )
    g_cross_kv = scatter_rows(dot_tn(source_everything, d_cross_pairs))
    grad_source = to_home(reduce_sequence(dot_nt(d_cross_pairs, w_cross_kv)))
    g_cross_q = scatter_rows(dot_tn(low_one, d_queries_cross))
    d_normed_one = d_resid_two + dot_nt(d_queries_cross, w_cross_q)
    d_resid_one, gain_one, shift_one = norm_back(d_normed_one, hat_one, inv_one, norm_table[:, 0])
    sums = jnp.stack([gain_one, shift_one, gain_two, shift_two, gain_three, shift_three], axis=0)
    sums = sum_everywhere(jnp.pad(sums, ((0, 2), (0, 0))))
    shard_rows = norm_params.shape[0]
    g_norm = lax.dynamic_slice_in_dim(sums, (dp_place * seq_count + seq_place) * shard_rows, shard_rows, 1)[:6].T
    d_branch_self = d_resid_one.astype(BF)
    g_self_out = scatter_rows(dot_tn(mixed_self, d_branch_self))
    d_mixed_self = dot_nt(d_branch_self, w_self_out).astype(BF)
    d_queries, d_self_pairs = attend_back(
        self_visits, queries, d_mixed_self, mixed_self, self_lse, self_pairs, qseg, self_kseg
    )
    g_self_in = scatter_rows(
        jnp.concatenate([dot_tn(x_own, d_queries), dot_tn(x_all, d_self_pairs)], axis=1)
    )
    summed = reduce_sequence(dot_nt(d_self_pairs, w_self_in[:, width:]))
    kept = d_resid_one + dot_nt(d_queries, w_self_in[:, :width])
    grad_tokens = to_home([a + b for a, b in zip(summed, list(kept.reshape(z_count, half, width)))])
    return (
        out_tokens,
        grad_tokens,
        grad_source,
        g_self_in,
        g_self_out,
        g_cross_q,
        g_cross_kv,
        g_cross_out,
        g_ffn_in,
        g_ffn_out,
        g_norm,
    )


def solution(mesh):
    tokens, rows = P("dp", "seq", None), P(("dp", "seq"), None)
    return jax.shard_map(
        body,
        mesh=mesh,
        in_specs=(tokens, tokens, P("dp", None), P("dp", None), tokens) + (rows,) * 8,
        out_specs=(tokens,) * 3 + (rows,) * 8,
        check_vma=False,
    )
```

```python
import functools

import jax
import jax.numpy as jnp
from jax import lax
from jax.experimental import pallas as pl
from jax.experimental.pallas import tpu as pltpu
from jax.sharding import PartitionSpec as P

HEAD_DIM = 64
GROUP = 4
LANES = GROUP * HEAD_DIM
BF = jnp.bfloat16
F32 = jnp.float32
VMEM_LIMIT = 56 * 2**20


def dot_f32(left, right):
    return jnp.dot(left, right, preferred_element_type=F32)


def dot_nt(left, right):
    return lax.dot_general(left, right, (((1,), (1,)), ((), ())), preferred_element_type=F32)


def dot_tn(left, right):
    return lax.dot_general(left, right, (((0,), (0,)), ((), ())), preferred_element_type=F32)


def head_of_lane(rows):
    return lax.broadcasted_iota(jnp.int32, (rows, LANES), 1) // HEAD_DIM


def stack_heads(tile):
    head = head_of_lane(tile.shape[0])
    zero = jnp.zeros_like(tile)
    return jnp.concatenate([jnp.where(head == h, tile, zero) for h in range(GROUP)], axis=0)


def unstack_heads(tile):
    rows = tile.shape[0] // GROUP
    head = head_of_lane(rows)
    out = tile[:rows]
    for h in range(1, GROUP):
        out = jnp.where(head == h, tile[h * rows : (h + 1) * rows], out)
    return out


def row_of(column):
    wide = jnp.broadcast_to(column, (column.shape[0], 128))
    return jnp.transpose(wide)[0:1, :]


def key_rows(b, place_ref, y_count, rows, total):
    r = b ^ place_ref[2, 0]
    z_count = total // (2 * rows * y_count)
    at = pl.multiple_of((lax.rem(r, y_count) * z_count + lax.div(r, y_count)) * rows, rows)
    return pl.ds(at, rows), pl.ds(pl.multiple_of(at + total // 2, rows), rows)


def both_halves(ref, spots, cols):
    return jnp.concatenate([ref[spot, cols] for spot in spots], axis=0)


def attend_kernel(y_count, place_ref, q_ref, kv_ref, qseg_ref, kseg_ref, o_ref, lse_ref, s_ref, m_ref, acc_ref):
    width = q_ref.shape[1]
    blocks = qseg_ref.shape[0]
    rows = q_ref.shape[0] // blocks
    keys = kseg_ref.shape[1]
    total_keys = kv_ref.shape[0]

    def block(k, carry):
        lo, hi = place_ref[0, k], place_ref[1, k]
        q_rows = pl.ds(pl.multiple_of(k * rows, rows), rows)
        qseg = qseg_ref[k]
        qseg = jnp.concatenate([qseg] * GROUP, axis=0)
        for g in range(width // LANES):
            cols = slice(g * LANES, (g + 1) * LANES)
            v_cols = slice(width + g * LANES, width + (g + 1) * LANES)
            stacked = stack_heads(q_ref[q_rows, cols])
            m_ref[...] = jnp.full(m_ref.shape, -3e38, F32)

            def first(b, carry):
                spots = key_rows(b, place_ref, y_count, keys // 2, total_keys)
                scores = dot_nt(stacked, both_halves(kv_ref, spots, cols))
                scores = jnp.where(qseg == kseg_ref[pl.ds(b, 1), :], scores, -1e30)
                s_ref[b] = scores
                m_ref[...] = jnp.maximum(m_ref[...], scores)
                return carry

            lax.fori_loop(lo, hi, first, 0)
            top = jnp.max(m_ref[...], axis=1, keepdims=True)
            m_ref[...] = jnp.zeros(m_ref.shape, F32)
            acc_ref[...] = jnp.zeros(acc_ref.shape, F32)

            def second(b, carry):
                spots = key_rows(b, place_ref, y_count, keys // 2, total_keys)
                weights = jnp.exp(s_ref[b] - top)
                m_ref[...] += weights
                acc_ref[...] += dot_f32(weights.astype(BF), both_halves(kv_ref, spots, v_cols))
                return carry

            lax.fori_loop(lo, hi, second, 0)
            total = jnp.sum(m_ref[...], axis=1, keepdims=True)
            o_ref[q_rows, cols] = unstack_heads(acc_ref[...] / total).astype(BF)
            lse_ref[k * (width // LANES) + g] = row_of(top + jnp.log(total))
        return carry

    lax.fori_loop(0, blocks, block, 0)


def attend_back_kernel(
    y_count, place_ref, q_ref, do_ref, o_ref, lse_ref, kv_ref, qseg_ref, kseg_ref, dq_ref, dkv_ref, sum_ref, dqt_ref
):
    width = q_ref.shape[1]
    blocks = qseg_ref.shape[0]
    rows = q_ref.shape[0] // blocks
    total = kv_ref.shape[0]
    keys = total // place_ref.shape[1]
    sum_ref[...] = jnp.zeros(sum_ref.shape, F32)

    def block(k, carry):
        lo, hi = place_ref[0, k], place_ref[1, k]
        q_rows = pl.ds(pl.multiple_of(k * rows, rows), rows)
        qseg = qseg_ref[k]
        qseg = jnp.concatenate([qseg] * GROUP, axis=1)
        for g in range(width // LANES):
            cols = slice(g * LANES, (g + 1) * LANES)
            v_cols = slice(width + g * LANES, width + (g + 1) * LANES)
            q_st = stack_heads(q_ref[q_rows, cols])
            do_tile = do_ref[q_rows, cols]
            do_st = stack_heads(do_tile)
            prod = do_tile.astype(F32) * o_ref[q_rows, cols].astype(F32)
            delta = row_of(jnp.sum(stack_heads(prod), axis=1, keepdims=True))
            lse = lse_ref[k * (width // LANES) + g]
            dqt_ref[...] = jnp.zeros(dqt_ref.shape, F32)

            def step(b, carry):
                spots = key_rows(b, place_ref, y_count, keys // 2, total)
                k_tile = both_halves(kv_ref, spots, cols)
                kseg = kseg_ref[pl.ds(pl.multiple_of(b * keys, keys), keys), :]
                scores = dot_nt(k_tile, q_st)
                soft = jnp.where(kseg == qseg, jnp.exp(scores - lse), 0.0)
                d_soft = dot_nt(both_halves(kv_ref, spots, v_cols), do_st)
                d_scores = (soft * (d_soft - delta)).astype(BF)
                d_keys = dot_f32(d_scores, q_st)
                d_values = dot_f32(soft.astype(BF), do_st)
                for e, spot in enumerate(spots):
                    part = slice(e * keys // 2, (e + 1) * keys // 2)
                    sum_ref[spot, cols] += d_keys[part]
                    sum_ref[spot, v_cols] += d_values[part]
                dqt_ref[...] += dot_tn(k_tile, d_scores)
                return carry

            lax.fori_loop(lo, hi, step, 0)
            dq_ref[q_rows, cols] = unstack_heads(jnp.transpose(dqt_ref[...]) * HEAD_DIM**-0.5).astype(BF)
        return carry

    lax.fori_loop(0, blocks, block, 0)
    dkv_ref[...] = sum_ref[...].astype(BF)


def assemble_kernel(pieces, place_ref, *refs):
    *parts, out_ref, sem = refs
    place = place_ref[0]
    piece = out_ref.shape[0] // pieces
    copies = []
    done = 0
    for part in parts:
        for i in range(part.shape[0] // piece):
            at = pl.multiple_of(((done + i) ^ place) * piece, piece)
            copies.append(
                pltpu.make_async_copy(part.at[pl.ds(i * piece, piece)], out_ref.at[pl.ds(at, piece)], sem.at[done + i])
            )
        done += part.shape[0] // piece
    for copy in copies:
        copy.start()
    for copy in copies:
        copy.wait()


def assemble(parts, pieces, place):
    rows = sum(part.shape[0] for part in parts)
    return pl.pallas_call(
        functools.partial(assemble_kernel, pieces),
        out_shape=jax.ShapeDtypeStruct((rows, parts[0].shape[1]), parts[0].dtype),
        in_specs=[SMEM] + [pl.BlockSpec(memory_space=pl.ANY)] * len(parts),
        out_specs=pl.BlockSpec(memory_space=pl.ANY),
        scratch_shapes=[pltpu.SemaphoreType.DMA((pieces,))],
        compiler_params=pltpu.CompilerParams(vmem_limit_bytes=2**20),
    )(place.reshape(1), *parts)


def assemble_pieces_kernel(rows, z_count, y_count, place_ref, *refs):
    *parts, out_ref, sem = refs
    dp_place, z_place, y_place = place_ref[0], place_ref[1], place_ref[2]
    copies = []
    for d, part in enumerate(parts):
        for l in range(y_count):
            for k in range(z_count):
                at = ((dp_place ^ d) * z_count + (z_place ^ k)) * y_count + (y_place ^ l)
                at = pl.multiple_of(at * rows, rows)
                copies.append(
                    pltpu.make_async_copy(
                        part.at[pl.ds((l * z_count + k) * rows, rows)], out_ref.at[pl.ds(at, rows)], sem.at[len(copies)]
                    )
                )
    for copy in copies:
        copy.start()
    for copy in copies:
        copy.wait()


def assemble_pieces(parts, rows, dp_place, z_place, y_place, z_count, y_count):
    pieces = len(parts) * z_count * y_count
    return pl.pallas_call(
        functools.partial(assemble_pieces_kernel, rows, z_count, y_count),
        out_shape=jax.ShapeDtypeStruct((pieces * rows, parts[0].shape[1]), parts[0].dtype),
        in_specs=[SMEM] + [pl.BlockSpec(memory_space=pl.ANY)] * len(parts),
        out_specs=pl.BlockSpec(memory_space=pl.ANY),
        scratch_shapes=[pltpu.SemaphoreType.DMA((pieces,))],
        compiler_params=pltpu.CompilerParams(vmem_limit_bytes=2**20),
    )(jnp.stack([dp_place, z_place, y_place]).astype(jnp.int32), *parts)


def tie(value, *after):
    return lax.optimization_barrier((value, after))[0]


SMEM = pl.BlockSpec(memory_space=pltpu.SMEM)
VMEM = pl.BlockSpec(memory_space=pltpu.VMEM)


def attend(y_count, place, queries, pairs, qseg, kseg):
    own, width = queries.shape
    blocks = qseg.shape[0]
    rows = own // blocks
    count, keys = kseg.shape
    groups = width // LANES
    return pl.pallas_call(
        functools.partial(attend_kernel, y_count),
        out_shape=(
            jax.ShapeDtypeStruct((own, width), BF),
            jax.ShapeDtypeStruct((blocks * groups, 1, GROUP * rows), F32),
        ),
        in_specs=[SMEM] + [VMEM] * 4,
        out_specs=(VMEM, VMEM),
        scratch_shapes=[
            pltpu.VMEM((count, GROUP * rows, keys), F32),
            pltpu.VMEM((GROUP * rows, keys), F32),
            pltpu.VMEM((GROUP * rows, LANES), F32),
        ],
        compiler_params=pltpu.CompilerParams(vmem_limit_bytes=VMEM_LIMIT),
        cost_estimate=pl.CostEstimate(
            flops=16 * own * count * keys * width * 2, bytes_accessed=6 * 2**20, transcendentals=own * count * keys * 8 // 4
        ),
    )(place, queries, pairs, qseg[:, :, None], kseg)


def attend_back(y_count, place, queries, d_mixed, mixed, lse, pairs, qseg, kseg):
    own, width = queries.shape
    blocks = qseg.shape[0]
    rows = own // blocks
    count, keys = kseg.shape
    return pl.pallas_call(
        functools.partial(attend_back_kernel, y_count),
        out_shape=(
            jax.ShapeDtypeStruct((own, width), BF),
            jax.ShapeDtypeStruct(pairs.shape, BF),
        ),
        in_specs=[SMEM] + [VMEM] * 7,
        out_specs=(VMEM, VMEM),
        scratch_shapes=[
            pltpu.VMEM(pairs.shape, F32),
            pltpu.VMEM((LANES, GROUP * rows), F32),
        ],
        compiler_params=pltpu.CompilerParams(vmem_limit_bytes=VMEM_LIMIT),
        cost_estimate=pl.CostEstimate(
            flops=24 * own * count * keys * width * 2, bytes_accessed=8 * 2**20, transcendentals=own * count * keys * 8 // 4
        ),
    )(place, queries, d_mixed, mixed, lse, pairs, qseg[:, None, :], kseg.reshape(-1, 1))


def layer_norm(resid, gain, shift):
    centered = resid - jnp.mean(resid, axis=-1, keepdims=True)
    inv_std = lax.rsqrt(jnp.mean(centered * centered, axis=-1, keepdims=True) + 1e-05)
    normed = centered * inv_std
    return (normed * gain + shift, normed, inv_std)


def norm_back(upstream, normed, inv_std, gain):
    scaled_grad = upstream * gain
    centered_grad = (
        scaled_grad
        - jnp.mean(scaled_grad, axis=-1, keepdims=True)
        - normed * jnp.mean(scaled_grad * normed, axis=-1, keepdims=True)
    )
    return (centered_grad * inv_std, jnp.sum(upstream * normed, axis=0), jnp.sum(upstream, axis=0))


def smooth_gate(values_in):
    return jax.nn.gelu(values_in, approximate=True)


def unxor(parts, place):
    out = jnp.zeros((len(parts),) + parts[0].shape, parts[0].dtype)
    for k, part in enumerate(parts):
        out = lax.dynamic_update_index_in_dim(out, part, place ^ k, 0)
    return out


def body(
    inputs,
    encoder,
    tgt_seg,
    src_len,
    cotangent,
    self_in,
    self_out,
    cross_q,
    cross_kv,
    cross_out,
    ffn_in,
    ffn_out,
    norm_params,
):
    held, local_rows, width = inputs.shape
    half = local_rows // 2
    dp_count, seq_count = lax.axis_size("dp"), lax.axis_size("seq")
    length = local_rows * seq_count
    x_count = dp_count // 2
    z_count = 2 * held
    y_count = seq_count // z_count
    dp_place, seq_place = lax.axis_index("dp"), lax.axis_index("seq")
    x_place, c_place = dp_place // 2, dp_place % 2
    z_place, y_place = seq_place // y_count, seq_place % y_count

    def over_core(v):
        return lax.ppermute(v, "dp", [(i, i ^ 1) for i in range(dp_count)])

    def over_x(v, k):
        return v if k == 0 else lax.ppermute(v, "dp", [(i, i ^ (2 * k)) for i in range(dp_count)])

    def over_y(v, k):
        return v if k == 0 else lax.ppermute(v, "seq", [(i, i ^ k) for i in range(seq_count)])

    def over_z(v, k):
        return v if k == 0 else lax.ppermute(v, "seq", [(i, i ^ (k * y_count)) for i in range(seq_count)])

    def pick(v, place):
        return lax.dynamic_index_in_dim(v, place, 0, keepdims=False)

    def swap_halves(v):
        halves = v.reshape(held, 2, half, width)
        mine = lax.dynamic_index_in_dim(halves, c_place, 1, keepdims=False)
        other = over_core(lax.dynamic_index_in_dim(halves, 1 - c_place, 1, keepdims=False))
        return jnp.concatenate([mine, other], axis=0)

    def to_work(*swapped):
        picked = [
            jnp.concatenate([pick(v, (z_place ^ k) ^ (held * c_place)) for v in swapped], axis=0) for k in range(z_count)
        ]
        return [over_z(v, k) for k, v in enumerate(picked)]

    def core_sum(v):
        blocks = v.reshape(2, y_count, z_count, half, width)
        return blocks[0] + over_core(blocks[1].astype(BF)).astype(F32)

    def y_sum(kept):
        total = kept[0]
        for l in range(1, y_count):
            total = total + over_y(kept[l].astype(BF), l).astype(F32)
        return total

    def z_home(blocks):
        return [over_z(blocks[k].astype(BF), k) for k in range(z_count)]

    def core_home(parts):
        moved = unxor(parts, z_place).reshape(2, held, half, width)
        mine = pick(moved, c_place)
        other = over_core(pick(moved, 1 - c_place))
        out = unxor([mine, other], c_place)
        return out.transpose(1, 0, 2, 3).reshape(held, local_rows, width).astype(F32)

    def z_gather(shard):
        return [over_z(shard, k) for k in range(z_count)]

    def y_gather(parts):
        if parts[0].shape[0] % 16:
            parts = [unxor(parts, z_place).reshape(-1, parts[0].shape[1])]
        near = jnp.concatenate(parts, axis=0)
        return jnp.concatenate([over_y(near, l) for l in range(y_count)], axis=0)

    def x_gather(chunk):
        return [over_x(chunk, k) for k in range(x_count)]

    def core_gather(chips, rows):
        if rows % 16:
            columns = chips[0].shape[1]

            def ordered(v):
                v = v.reshape(y_count, z_count, rows, columns)
                return unxor(list(v), y_place).transpose(1, 0, 2, 3).reshape(-1, columns)

            chips = [ordered(v) for v in chips]
        parts = [half_of for chip in chips for half_of in (chip, over_core(chip))]
        if rows % 16:
            return assemble(parts, dp_count, dp_place)
        return assemble_deep(parts, rows)

    def assemble_deep(parts, rows):
        return assemble_pieces(parts, rows, dp_place, z_place, y_place, z_count, y_count)

    def core_scatter(grad):
        parts = grad.reshape(x_count, 2, -1, grad.shape[1])
        return lax.dynamic_index_in_dim(parts, c_place, 1, keepdims=False) + over_core(
            lax.dynamic_index_in_dim(parts, 1 - c_place, 1, keepdims=False).astype(BF)
        ).astype(F32)

    def x_scatter(kept):
        total = pick(kept, x_place)
        for k in range(1, x_count):
            total = total + over_x(pick(kept, x_place ^ k).astype(BF), k).astype(F32)
        return total

    def y_scatter(kept):
        columns = kept.shape[1]
        parts = kept.reshape(z_count, y_count, -1, columns)
        total = lax.dynamic_index_in_dim(parts, y_place, 1, keepdims=False)
        for l in range(1, y_count):
            total = total + over_y(
                lax.dynamic_index_in_dim(parts, y_place ^ l, 1, keepdims=False).astype(BF), l
            ).astype(F32)
        return total

    def z_scatter(kept):
        total = pick(kept, z_place)
        for k in range(1, z_count):
            total = total + over_z(pick(kept, z_place ^ k).astype(BF), k).astype(F32)
        return total

    notes = jnp.concatenate([tgt_seg, src_len], axis=1)
    notes = pick(jnp.concatenate([notes, over_core(notes)], axis=0), z_place ^ (held * c_place))
    target_all, lengths = notes[:length], notes[length:]
    docs = lengths.shape[0]
    upto = lax.broadcasted_iota(jnp.int32, (docs, docs), 0) <= lax.broadcasted_iota(jnp.int32, (docs, docs), 1)
    ends = jnp.sum(jnp.where(upto, lengths[:, None], 0), axis=0, dtype=jnp.int32)
    positions = jnp.arange(length, dtype=jnp.int32)
    source_all = jnp.sum((positions[:, None] >= ends[None, :]).astype(jnp.int32), axis=1, dtype=jnp.int32)
    place = seq_place * 2 + c_place
    by_block = target_all.reshape(-1, half)
    qseg = jnp.stack([pick(by_block, place ^ (k * 2 * y_count)) for k in range(z_count)])
    keys = 2 * half

    def in_order(segments):
        pairs = segments.reshape(-1, 2, half)
        return jnp.where(c_place == 0, pairs, pairs[:, ::-1]).reshape(-1, keys)

    def visits(segments):
        low = jnp.sum((segments[None, :] < qseg[:, :1]).astype(jnp.int32), axis=1, dtype=jnp.int32)
        high = jnp.sum((segments[None, :] <= qseg[:, -1:]).astype(jnp.int32), axis=1, dtype=jnp.int32)
        rest = length // keys - z_count
        table = jnp.stack([low // keys, (high + keys - 1) // keys, jnp.zeros_like(low) + seq_place])
        return jnp.pad(table, ((0, 0), (0, rest)))

    self_kseg, cross_kseg = in_order(target_all), in_order(source_all)
    self_visits, cross_visits = visits(target_all), visits(source_all)

    rows = self_in.shape[0]
    norm_wide = jnp.pad(norm_params, ((0, 0), (0, 128 - norm_params.shape[1])))
    near_swap = swap_halves(inputs)
    w1 = z_gather(jnp.concatenate([self_in, self_out, norm_wide], axis=1))
    x_parts = to_work(near_swap)
    w1 = y_gather(w1)
    far_swap = [swap_halves(v) for v in tie((encoder, cotangent), near_swap)]
    x_own = jnp.concatenate(x_parts, axis=0)
    x_near = jnp.concatenate([x_own] + [over_y(x_own, l) for l in range(1, y_count)], axis=0)
    w1 = x_gather(w1)
    far = to_work(*tie(far_swap, x_own))
    w2 = z_gather(tie(jnp.concatenate([cross_kv, cross_q, cross_out], axis=1), x_own))
    x_all = jnp.concatenate([x_near, over_core(x_near)], axis=0)
    w1 = core_gather(w1, rows)
    w_self_in, w_self_out = w1[:, : 3 * width], w1[:, 3 * width : 4 * width]
    norm_table = w1[:, 4 * width :].astype(F32)
    scaling = HEAD_DIM**-0.5
    x_all, far, w2 = lax.optimization_barrier((x_all, far, w2))
    source_own = jnp.concatenate([v[:half] for v in far], axis=0)
    upstream = jnp.concatenate([v[half:] for v in far], axis=0).astype(F32)
    source_near = jnp.concatenate([source_own] + [over_y(source_own, l) for l in range(1, y_count)], axis=0)
    w2 = y_gather(w2)
    queries = (dot_f32(x_own, w_self_in[:, :width]) * scaling).astype(BF)
    self_pairs = dot_f32(x_all, w_self_in[:, width:]).astype(BF)

    queries, source_near, w2 = lax.optimization_barrier((queries, source_near, w2))
    source_all_rows = jnp.concatenate([source_near, over_core(source_near)], axis=0)
    w2 = x_gather(w2)
    w3, w4 = z_gather(tie(ffn_in, queries)), z_gather(tie(ffn_out, queries))
    mixed_self, self_lse = attend(y_count, self_visits, queries, self_pairs, qseg, self_kseg)
    mixed_self, source_all_rows, w2, w3, w4 = lax.optimization_barrier((mixed_self, source_all_rows, w2, w3, w4))
    w2 = core_gather(w2, rows)
    w_cross_kv, w_cross_q, w_cross_out = w2[:, : 2 * width], w2[:, 2 * width : 3 * width], w2[:, 3 * width :]
    w3, w4 = y_gather(w3), y_gather(w4)
    resid_one = x_own.astype(F32) + dot_f32(mixed_self, w_self_out)
    normed_one, hat_one, inv_one = layer_norm(resid_one, norm_table[:, 0], norm_table[:, 1])
    low_one = normed_one.astype(BF)
    cross_pairs = dot_f32(source_all_rows, w_cross_kv).astype(BF)
    queries_cross = (dot_f32(low_one, w_cross_q) * scaling).astype(BF)
    queries_cross, w3, w4 = lax.optimization_barrier((queries_cross, w3, w4))
    w3, w4 = x_gather(w3), x_gather(w4)
    mixed_cross, cross_lse = attend(y_count, cross_visits, queries_cross, cross_pairs, qseg, cross_kseg)
    mixed_cross, w3, w4 = lax.optimization_barrier((mixed_cross, w3, w4))
    w_ffn_in, w_ffn_out = core_gather(w3, rows), core_gather(w4, ffn_out.shape[0])
    resid_two = normed_one + dot_f32(mixed_cross, w_cross_out)
    normed_two, hat_two, inv_two = layer_norm(resid_two, norm_table[:, 2], norm_table[:, 3])
    low_two = normed_two.astype(BF)
    hidden_pre = dot_f32(low_two, w_ffn_in)
    hidden = smooth_gate(hidden_pre).astype(BF)
    resid_three = normed_two + dot_f32(hidden, w_ffn_out)
    layer_out, hat_three, inv_three = layer_norm(resid_three, norm_table[:, 4], norm_table[:, 5])
    out_low = layer_out.astype(BF)

    d_resid_three, gain_three, shift_three = norm_back(upstream, hat_three, inv_three, norm_table[:, 4])
    d_branch_ffn = d_resid_three.astype(BF)
    d_branch_ffn, out_low = lax.optimization_barrier((d_branch_ffn, out_low))
    out_parts = z_home(out_low.reshape(z_count, half, width))
    g_ffn_out = dot_tn(hidden, d_branch_ffn)
    d_hidden = dot_nt(d_branch_ffn, w_ffn_out)
    gate_pull = jax.vjp(smooth_gate, hidden_pre)[1]
    d_pre = gate_pull(d_hidden)[0].astype(BF)
    g_ffn_in = dot_tn(low_two, d_pre)
    d_pre, g_ffn_in, g_ffn_out = lax.optimization_barrier((d_pre, g_ffn_in, g_ffn_out))
    g_ffn_in, g_ffn_out = core_scatter(g_ffn_in), core_scatter(g_ffn_out)
    d_normed_two = d_resid_three + dot_nt(d_pre, w_ffn_in)
    d_resid_two, gain_two, shift_two = norm_back(d_normed_two, hat_two, inv_two, norm_table[:, 2])
    d_branch_cross = d_resid_two.astype(BF)
    g_cross_out = dot_tn(mixed_cross, d_branch_cross)
    d_mixed_cross = dot_nt(d_branch_cross, w_cross_out).astype(BF)
    d_mixed_cross, g_ffn_in, g_ffn_out, out_parts = lax.optimization_barrier(
        (d_mixed_cross, g_ffn_in, g_ffn_out, out_parts)
    )
    g_ffn_in, g_ffn_out = x_scatter(g_ffn_in), x_scatter(g_ffn_out)
    out_tokens = core_home(out_parts)
    d_queries_cross, d_cross_pairs = attend_back(
        y_count, cross_visits, queries_cross, d_mixed_cross, mixed_cross, cross_lse, cross_pairs, qseg, cross_kseg
    )
    d_cross_pairs = tie(d_cross_pairs, out_tokens)
    d_source = core_sum(dot_nt(d_cross_pairs, w_cross_kv))
    g_cross_kv = dot_tn(source_all_rows, d_cross_pairs)
    g_cross_q = dot_tn(low_one, d_queries_cross)
    d_normed_one = d_resid_two + dot_nt(d_queries_cross, w_cross_q)
    d_resid_one, gain_one, shift_one = norm_back(d_normed_one, hat_one, inv_one, norm_table[:, 0])
    sums = jnp.stack([gain_one, shift_one, gain_two, shift_two, gain_three, shift_three], axis=0)
    sums = jnp.pad(sums, ((0, 2), (0, 0)))
    d_branch_self = d_resid_one.astype(BF)
    g_self_out = dot_tn(mixed_self, d_branch_self)
    g_cross = core_scatter(jnp.concatenate([g_cross_kv, g_cross_q, g_cross_out, g_self_out], axis=1))
    sums = sums + over_core(sums)
    d_mixed_self = dot_nt(d_branch_self, w_self_out).astype(BF)
    d_mixed_self, g_ffn_in, g_ffn_out, d_source, g_cross, sums = lax.optimization_barrier(
        (d_mixed_self, g_ffn_in, g_ffn_out, d_source, g_cross, sums)
    )
    g_ffn_in, g_ffn_out = y_scatter(g_ffn_in), y_scatter(g_ffn_out)
    d_source = y_sum(d_source)
    g_cross = x_scatter(g_cross)
    for k in (1 << i for i in range(x_count.bit_length() - 1)):
        sums = sums + over_x(sums, k)
    d_queries, d_self_pairs = attend_back(
        y_count, self_visits, queries, d_mixed_self, mixed_self, self_lse, self_pairs, qseg, self_kseg
    )
    d_self_pairs, g_ffn_in, g_ffn_out, d_source, g_cross, sums = lax.optimization_barrier(
        (d_self_pairs, g_ffn_in, g_ffn_out, d_source, g_cross, sums)
    )
    source_parts = z_home(d_source)
    g_cross = y_scatter(g_cross)
    for k in (1 << i for i in range(y_count.bit_length() - 1)):
        sums = sums + over_y(sums, k)
    summed = core_sum(dot_nt(d_self_pairs, w_self_in[:, width:]))
    g_self_in = jnp.concatenate([dot_tn(x_own, d_queries), dot_tn(x_all, d_self_pairs)], axis=1)
    kept = d_resid_one + dot_nt(d_queries, w_self_in[:, :width])
    kept, g_self_in, source_parts, g_cross, sums, summed = lax.optimization_barrier(
        (kept, g_self_in, source_parts, g_cross, sums, summed)
    )
    summed = y_sum(summed)
    g_self_in = core_scatter(g_self_in)
    g_ffn_in, g_ffn_out = z_scatter(g_ffn_in), z_scatter(g_ffn_out)
    g_self_in = x_scatter(g_self_in)
    grad_source = core_home(source_parts)
    tokens_parts = z_home(summed + kept.reshape(z_count, half, width))
    g_cross = z_scatter(g_cross)
    for k in (1 << i for i in range(z_count.bit_length() - 1)):
        sums = sums + over_z(sums, k)
    g_self_in = z_scatter(y_scatter(g_self_in))
    grad_tokens = core_home(tokens_parts)
    g_norm = lax.dynamic_slice_in_dim(sums, (dp_place * seq_count + seq_place) * rows, rows, 1)[:6].T
    g_cross_kv, g_cross_q = g_cross[:, : 2 * width], g_cross[:, 2 * width : 3 * width]
    g_cross_out, g_self_out = g_cross[:, 3 * width : 4 * width], g_cross[:, 4 * width :]
    return (
        out_tokens,
        grad_tokens,
        grad_source,
        g_self_in,
        g_self_out,
        g_cross_q,
        g_cross_kv,
        g_cross_out,
        g_ffn_in,
        g_ffn_out,
        g_norm,
    )


def solution(mesh):
    tokens, rows = P("dp", "seq", None), P(("dp", "seq"), None)
    return jax.shard_map(
        body,
        mesh=mesh,
        in_specs=(tokens, tokens, P("dp", None), P("dp", None), tokens) + (rows,) * 8,
        out_specs=(tokens,) * 3 + (rows,) * 8,
        check_vma=False,
    )
```

```python
import dataclasses
import functools
import math

import jax
import jax.numpy as jnp
from jax import lax
from jax.experimental import pallas as pl
from jax.experimental.pallas import tpu as pltpu
from jax.sharding import PartitionSpec as P

HEAD_DIM = 64
GROUP = 4
LANES = GROUP * HEAD_DIM
CHUNK = 256
LOG2E = 1.4426950408889634
LN2 = 0.6931471805599453
GELU_A = 0.7978845608028654
GELU_B = 0.044715
BF = jnp.bfloat16
F32 = jnp.float32
SMEM = pl.BlockSpec(memory_space=pltpu.SMEM)
VMEM = pl.BlockSpec(memory_space=pltpu.VMEM)
ANY = pl.BlockSpec(memory_space=pl.ANY)


def dot_f32(left, right):
    return jnp.dot(left, right, preferred_element_type=F32)


def dot_nt(left, right):
    return lax.dot_general(left, right, (((1,), (1,)), ((), ())), preferred_element_type=F32)


def padded_bytes(dims, dtype):
    dims = (1,) * (2 - len(dims)) + tuple(dims)
    lead = math.prod(dims[:-2])
    return lead * (-(-dims[-2] // 16) * 16) * (-(-dims[-1] // 128) * 128) * jnp.dtype(dtype).itemsize


def kernel_call(kernel, *, out_shape, in_specs, out_specs, scratch_shapes=(), spare=4):
    def call(*operands):
        need = spare * 2**20
        for operand, spec in zip(operands, in_specs):
            need += padded_bytes(operand.shape, operand.dtype) if spec is VMEM else 0
        for result in jax.tree.leaves(out_shape):
            need += padded_bytes(result.shape, result.dtype)
        for scratch in scratch_shapes:
            if getattr(scratch, "memory_space", None) == pltpu.VMEM:
                need += padded_bytes(scratch.shape, scratch.dtype)
        return pl.pallas_call(
            kernel,
            out_shape=out_shape,
            in_specs=in_specs,
            out_specs=out_specs,
            scratch_shapes=scratch_shapes,
            compiler_params=pltpu.CompilerParams(vmem_limit_bytes=need),
            cost_estimate=pl.CostEstimate(flops=10**6, bytes_accessed=2**10, transcendentals=0),
        )(*operands)

    return call


def shape(dims, dtype=BF):
    return jax.ShapeDtypeStruct(dims, dtype)


def chunk(i):
    return pl.ds(pl.multiple_of(i * CHUNK, CHUNK), CHUNK)


@dataclasses.dataclass(frozen=True)
class Size:
    half: int
    length: int
    own: int
    z_count: int
    x_count: int
    pieces: int
    tile_rows: int
    hidden: int
    first: int


def stack_heads(tile):
    head = lax.broadcasted_iota(jnp.int32, tile.shape, 1) // HEAD_DIM
    zero = jnp.zeros_like(tile)
    return jnp.concatenate([jnp.where(head == h, tile, zero) for h in range(GROUP)], axis=0)


def row_of(column):
    return jnp.transpose(jnp.broadcast_to(column, (column.shape[0], 128)))[0:1, :]


def key_rows(b, keys, total):
    half = keys // 2
    at = pl.multiple_of(b * half, half)
    return pl.ds(at, half), pl.ds(pl.multiple_of(at + total // 2, half), half)


def both_rows(ref, spots, cols):
    return jnp.concatenate([ref[spot, cols] for spot in spots], axis=0)


def attend_kernel(visit_ref, q_ref, kv_ref, qseg_ref, kseg_ref, o_ref, lse_ref, acc_ref, qst_ref):
    width = q_ref.shape[1]
    blocks = qseg_ref.shape[0]
    rows = q_ref.shape[0] // blocks
    total = kv_ref.shape[0]
    keys = total // visit_ref.shape[1]
    groups = width // LANES

    def block(k, carry):
        lo, hi = visit_ref[0, k], visit_ref[1, k]
        q_rows = pl.ds(pl.multiple_of(k * rows, rows), rows)
        qseg = jnp.concatenate([qseg_ref[k]] * GROUP, axis=1)
        for g in range(groups):
            qst_ref[g] = stack_heads(q_ref[q_rows, g * LANES : (g + 1) * LANES])
        acc_ref[...] = jnp.zeros(acc_ref.shape, F32)

        def step(b, carry):
            spots = key_rows(b, keys, total)
            same = kseg_ref[pl.ds(pl.multiple_of(b * keys, keys), keys), :] == qseg
            scores = [
                dot_nt(both_rows(kv_ref, spots, slice(g * LANES, (g + 1) * LANES)), qst_ref[g]) for g in range(groups)
            ]
            out, lows, fades = [], [], []
            for g in range(groups):
                top, tot = carry[g]
                masked = jnp.where(same, scores[g], -1e30)
                new = jnp.maximum(top, jnp.max(masked, axis=0, keepdims=True))
                soft = jnp.exp2(masked - new)
                fade = jnp.exp2(top - new)
                out.append((new, tot * fade + jnp.sum(soft, axis=0, keepdims=True)))
                lows.append(soft.astype(BF))
                fades.append(fade)
            for g in range(groups):
                turned = jnp.transpose(both_rows(kv_ref, spots, slice(width + g * LANES, width + (g + 1) * LANES)))
                for h in range(GROUP):
                    at = g * LANES + h * HEAD_DIM
                    cols = slice(h * rows, (h + 1) * rows)
                    values = turned[h * HEAD_DIM : (h + 1) * HEAD_DIM]
                    acc_ref[at : at + HEAD_DIM] = acc_ref[at : at + HEAD_DIM] * fades[g][:, cols] + dot_f32(
                        values, lows[g][:, cols]
                    )
            return tuple(out)

        start = (jnp.full((1, GROUP * rows), -3e38, F32), jnp.zeros((1, GROUP * rows), F32))
        end = lax.fori_loop(lo, hi, step, (start,) * groups)
        for g in range(groups):
            top, tot = end[g]
            inv = 1.0 / tot
            mixed = [
                acc_ref[g * LANES + h * HEAD_DIM : g * LANES + (h + 1) * HEAD_DIM] * inv[:, h * rows : (h + 1) * rows]
                for h in range(GROUP)
            ]
            o_ref[q_rows, g * LANES : (g + 1) * LANES] = jnp.transpose(jnp.concatenate(mixed, axis=0)).astype(BF)
            lse_ref[k * groups + g] = top + jnp.log2(tot)
        return carry

    lax.fori_loop(0, blocks, block, 0)


def attend_back_kernel(
    visit_ref,
    q_ref,
    do_ref,
    o_ref,
    lse_ref,
    kv_ref,
    qseg_ref,
    kseg_ref,
    dq_ref,
    dkv_ref,
    sum_ref,
    dqt_ref,
    qst_ref,
    dst_ref,
    delta_ref,
):
    width = q_ref.shape[1]
    blocks = qseg_ref.shape[0]
    rows = q_ref.shape[0] // blocks
    total = kv_ref.shape[0]
    keys = total // visit_ref.shape[1]
    groups = width // LANES
    sum_ref[...] = jnp.zeros(sum_ref.shape, F32)

    def block(k, carry):
        lo, hi = visit_ref[0, k], visit_ref[1, k]
        q_rows = pl.ds(pl.multiple_of(k * rows, rows), rows)
        qseg = jnp.concatenate([qseg_ref[k]] * GROUP, axis=1)
        for g in range(groups):
            cols = slice(g * LANES, (g + 1) * LANES)
            qst_ref[g] = stack_heads(q_ref[q_rows, cols])
            d_mixed = do_ref[q_rows, cols]
            dst_ref[g] = stack_heads(d_mixed)
            prod = d_mixed.astype(F32) * o_ref[q_rows, cols].astype(F32)
            delta_ref[g] = row_of(jnp.sum(stack_heads(prod), axis=1, keepdims=True))
        dqt_ref[...] = jnp.zeros(dqt_ref.shape, F32)

        def step(b, carry):
            spots = key_rows(b, keys, total)
            same = kseg_ref[pl.ds(pl.multiple_of(b * keys, keys), keys), :] == qseg
            k_cols = [slice(g * LANES, (g + 1) * LANES) for g in range(groups)]
            v_cols = [slice(width + g * LANES, width + (g + 1) * LANES) for g in range(groups)]
            scores = [dot_nt(both_rows(kv_ref, spots, k_cols[g]), qst_ref[g]) for g in range(groups)]
            d_soft = [dot_nt(both_rows(kv_ref, spots, v_cols[g]), dst_ref[g]) for g in range(groups)]
            softs, d_scores = [], []
            for g in range(groups):
                soft = jnp.where(same, jnp.exp2(scores[g] - lse_ref[k * groups + g]), 0.0)
                d_scores.append((soft * (d_soft[g] - delta_ref[g])).astype(BF))
                softs.append(soft.astype(BF))
            for g in range(groups):
                d_keys, d_values = dot_f32(d_scores[g], qst_ref[g]), dot_f32(softs[g], dst_ref[g])
                for e, spot in enumerate(spots):
                    part = slice(e * keys // 2, (e + 1) * keys // 2)
                    sum_ref[spot, k_cols[g]] += d_keys[part]
                    sum_ref[spot, v_cols[g]] += d_values[part]
                turned = jnp.transpose(both_rows(kv_ref, spots, k_cols[g]))
                for h in range(GROUP):
                    at = slice(g * LANES + h * HEAD_DIM, g * LANES + (h + 1) * HEAD_DIM)
                    keys_t = turned[h * HEAD_DIM : (h + 1) * HEAD_DIM]
                    dqt_ref[at] += dot_f32(keys_t, d_scores[g][:, h * rows : (h + 1) * rows])
            return carry

        lax.fori_loop(lo, hi, step, 0)
        for g in range(groups):
            cols = slice(g * LANES, (g + 1) * LANES)
            dq_ref[q_rows, cols] = (jnp.transpose(dqt_ref[cols]) * HEAD_DIM**-0.5).astype(BF)
        return carry

    lax.fori_loop(0, blocks, block, 0)
    dkv_ref[:, :width] = (sum_ref[:, :width] * LN2).astype(BF)
    dkv_ref[:, width:] = sum_ref[:, width:].astype(BF)


def attend(visits, queries, pairs, qseg, kseg):
    own, width = queries.shape
    blocks = qseg.shape[0]
    rows = own // blocks
    groups = width // LANES
    return kernel_call(
        attend_kernel,
        out_shape=(shape((own, width)), shape((blocks * groups, 1, GROUP * rows), F32)),
        in_specs=[SMEM] + [VMEM] * 4,
        out_specs=(VMEM, VMEM),
        scratch_shapes=[pltpu.VMEM((width, rows), F32), pltpu.VMEM((groups, GROUP * rows, LANES), BF)],
    )(visits, queries, pairs, qseg[:, None, :], kseg.reshape(-1, 1))


def attend_back(visits, queries, d_mixed, mixed, lse, pairs, qseg, kseg):
    own, width = queries.shape
    blocks = qseg.shape[0]
    rows = own // blocks
    groups = width // LANES
    return kernel_call(
        attend_back_kernel,
        out_shape=(shape((own, width)), shape(pairs.shape)),
        in_specs=[SMEM] + [VMEM] * 7,
        out_specs=(VMEM, VMEM),
        scratch_shapes=[
            pltpu.VMEM(pairs.shape, F32),
            pltpu.VMEM((width, rows), F32),
            pltpu.VMEM((groups, GROUP * rows, LANES), BF),
            pltpu.VMEM((groups, GROUP * rows, LANES), BF),
            pltpu.VMEM((groups, 1, GROUP * rows), F32),
        ],
    )(visits, queries, d_mixed, mixed, lse, pairs, qseg[:, None, :], kseg.reshape(-1, 1))


def norm_of(resid):
    centered = resid - jnp.mean(resid, axis=-1, keepdims=True)
    inv = lax.rsqrt(jnp.mean(centered * centered, axis=-1, keepdims=True) + 1e-05)
    return centered * inv, inv


def norm_pull(upstream, hat, inv, gain):
    scaled = upstream * gain
    return inv * (
        scaled - jnp.mean(scaled, axis=-1, keepdims=True) - hat * jnp.mean(scaled * hat, axis=-1, keepdims=True)
    )


def fetch_tiles(place_ref, parts, first, tiles, rows, x_count, whole_ref, sem):
    copies = []
    for e, part in enumerate(parts):
        pieces = part.shape[0]
        for k in range(x_count):
            dp = (place_ref[0] ^ k) * 2 + (place_ref[1] ^ e)
            at = pl.ds(pl.multiple_of(dp * pieces, pieces), pieces)
            for t in range(tiles):
                source = part.at[:, pl.ds(first + (k * tiles + t) * rows, rows)]
                copies.append(pltpu.make_async_copy(source, whole_ref.at[t, at], sem.at[len(copies)]))
    for copy in copies:
        copy.start()
    return copies


def tile_of(ref, t):
    tile = ref[t]
    return tile.reshape(-1, tile.shape[-1])


def own_tokens(near_ref, place_ref, half, z_count):
    y_count = near_ref.shape[0] // z_count
    return jnp.concatenate([near_ref[z * y_count + place_ref[3], :half, :] for z in range(z_count)], axis=0)


def sequence_rows(ref, i, half):
    count = CHUNK // half
    return jnp.concatenate([ref[i * count + j, :half, :] for j in range(count)], axis=0)


def put_pairs(near_ref, far_ref, half, w_k, w_v, kv_ref):
    width = w_k.shape[1]
    count = near_ref.shape[0] * half // CHUNK
    for e, ref in enumerate((near_ref, far_ref)):

        def step(i, carry):
            rows = sequence_rows(ref, i, half)
            at = chunk(i + e * count)
            kv_ref[at, :width] = dot_f32(rows, w_k).astype(BF)
            kv_ref[at, width:] = dot_f32(rows, w_v).astype(BF)
            return carry

        lax.fori_loop(0, count, step, 0)


def grad_rows(place_ref, left_ref, dp_count, e):
    rows = left_ref.shape[0] // dp_count
    out = []
    for k in range(dp_count // 2):
        dp = (place_ref[0] ^ k) * 2 + (place_ref[1] ^ e)
        out.append(left_ref[pl.ds(pl.multiple_of(dp * rows, rows), rows), :])
    return jnp.concatenate(out, axis=0)


def put_grad(target, value, tile, tile_rows):
    x_count, pieces, _, width = target.shape
    rows = value.shape[0] // x_count
    for k in range(x_count):
        part = value[k * rows : (k + 1) * rows].astype(target.dtype)
        target[k, :, tile * tile_rows : (tile + 1) * tile_rows, :] = part.reshape(pieces, tile_rows, width)


def project_kernel(size, place_ref, w_near_ref, w_far_ref, near_ref, far_ref, q_ref, kv_ref, whole_ref, sem):
    copies = fetch_tiles(
        place_ref, (w_near_ref, w_far_ref), size.first, 3, size.tile_rows, size.x_count, whole_ref, sem
    )
    own = own_tokens(near_ref, place_ref, size.half, size.z_count)
    for copy in copies:
        copy.wait()
    q_ref[...] = (dot_f32(own, tile_of(whole_ref, 0)) * (HEAD_DIM**-0.5 * LOG2E)).astype(BF)
    put_pairs(near_ref, far_ref, size.half, tile_of(whole_ref, 1), tile_of(whole_ref, 2), kv_ref)


def project(size, place, weights, near, far):
    width = near.shape[2]
    return kernel_call(
        functools.partial(project_kernel, size),
        out_shape=(
            shape((size.own, width)),
            shape((size.length, 2 * width)),
            shape((3, 2 * size.x_count * size.pieces, size.tile_rows, width)),
        ),
        in_specs=[SMEM, ANY, ANY, VMEM, VMEM],
        out_specs=(VMEM,) * 3,
        scratch_shapes=[pltpu.SemaphoreType.DMA((2 * size.x_count * 3,))],
    )(place, *weights, near, far)


def bridge_kernel(
    size,
    place_ref,
    w_near_ref,
    w_far_ref,
    near_ref,
    source_near_ref,
    source_far_ref,
    mixed_ref,
    q_ref,
    kv_ref,
    whole_ref,
    hat_ref,
    inv_ref,
    norm_ref,
    sem,
):
    copies = fetch_tiles(
        place_ref, (w_near_ref, w_far_ref), size.first, 6, size.tile_rows, size.x_count, whole_ref, sem
    )
    own = own_tokens(near_ref, place_ref, size.half, size.z_count)
    for copy in copies:
        copy.wait()
    norm_ref[...] = jnp.transpose(tile_of(whole_ref, 5)[:, :128].astype(F32))[: norm_ref.shape[0]]
    hat, inv = norm_of(own.astype(F32) + dot_f32(mixed_ref[...], tile_of(whole_ref, 0)))
    hat_ref[...] = hat
    inv_ref[...] = inv
    low = (hat * norm_ref[0:1, :] + norm_ref[1:2, :]).astype(BF)
    q_ref[...] = (dot_f32(low, tile_of(whole_ref, 1)) * (HEAD_DIM**-0.5 * LOG2E)).astype(BF)
    put_pairs(
        source_near_ref, source_far_ref, size.half, tile_of(whole_ref, 2), tile_of(whole_ref, 3), kv_ref
    )


def bridge(size, place, weights, near, source_near, source_far, mixed):
    width = near.shape[2]
    return kernel_call(
        functools.partial(bridge_kernel, size),
        out_shape=(
            shape((size.own, width)),
            shape((size.length, 2 * width)),
            shape((6, 2 * size.x_count * size.pieces, size.tile_rows, width)),
            shape((size.own, width), F32),
            shape((size.own, 1), F32),
            shape((8, width), F32),
        ),
        in_specs=[SMEM, ANY, ANY] + [VMEM] * 4,
        out_specs=(VMEM,) * 6,
        scratch_shapes=[pltpu.SemaphoreType.DMA((2 * size.x_count * 6,))],
    )(place, *weights, near, source_near, source_far, mixed)


def feed_kernel(
    size,
    place_ref,
    w_near_ref,
    w_far_ref,
    mixed_ref,
    whole_two_ref,
    hat_one_ref,
    norm_ref,
    cot_ref,
    out_ref,
    d_two_ref,
    d_mixed_ref,
    sums_ref,
    low_t_ref,
    dz_ref,
    hid_ref,
    down_ref,
    mixed_t_ref,
    w_in_ref,
    w_out_ref,
    z_ref,
    low_ref,
    hat_two_ref,
    inv_two_ref,
    sem,
):
    own, width = hat_one_ref.shape
    hidden = z_ref.shape[1]
    tiles = hidden // width
    tile_rows = size.tile_rows
    copies = []
    for e, part in enumerate((w_near_ref, w_far_ref)):
        pieces, total = part.shape[0], part.shape[1] // size.x_count
        for k in range(size.x_count):
            dp = (place_ref[0] ^ k) * 2 + (place_ref[1] ^ e)
            at = pl.ds(pl.multiple_of(dp * pieces, pieces), pieces)
            for t in range(tiles):
                source = part.at[:, pl.ds(k * total + t * tile_rows, tile_rows)]
                copies.append(pltpu.make_async_copy(source, w_in_ref.at[t, at], sem.at[len(copies)]))
            source = part.at[:, pl.ds(k * total + tiles * tile_rows, total - tiles * tile_rows)]
            copies.append(pltpu.make_async_copy(source, w_out_ref.at[at], sem.at[len(copies)]))
    for copy in copies:
        copy.start()
    mixed_t_ref[...] = jnp.transpose(mixed_ref[...])
    sums_ref[...] = jnp.zeros(sums_ref.shape, F32)
    cross_out = whole_two_ref[4]
    for copy in copies:
        copy.wait()
    per_tile = w_out_ref.shape[0] // tiles

    def w_down(t):
        return w_out_ref[t * per_tile : (t + 1) * per_tile].reshape(width, width)

    def forward(i, carry):
        at = chunk(i)
        one = hat_one_ref[at, :] * norm_ref[0:1, :] + norm_ref[1:2, :]
        hat, inv = norm_of(one + dot_f32(mixed_ref[at, :], cross_out))
        hat_two_ref[at, :] = hat
        inv_two_ref[at, :] = inv
        two = hat * norm_ref[2:3, :] + norm_ref[3:4, :]
        low = two.astype(BF)
        low_ref[at, :] = low
        total = two
        for t in range(tiles):
            cols = slice(t * width, (t + 1) * width)
            z = dot_f32(low, tile_of(w_in_ref, t))
            z_ref[at, cols] = z
            turn = jnp.tanh(GELU_A * (z + GELU_B * (z * z * z)))
            hid = (0.5 * z * (1.0 + turn)).astype(BF)
            hid_ref[at, cols] = hid
            total = total + dot_f32(hid, w_down(t))
        hat, inv = norm_of(total)
        gain = norm_ref[4:5, :]
        out_ref[at, :] = (hat * gain + norm_ref[5:6, :]).astype(BF)
        upstream = sequence_rows(cot_ref, i, size.half).astype(F32)
        sums_ref[4:5, :] += jnp.sum(upstream * hat, axis=0, keepdims=True)
        sums_ref[5:6, :] += jnp.sum(upstream, axis=0, keepdims=True)
        down = norm_pull(upstream, hat, inv, gain)
        low_down = down.astype(BF)
        down_ref[at, :] = low_down
        back = down
        for t in range(tiles):
            cols = slice(t * width, (t + 1) * width)
            d_hid = dot_nt(low_down, w_down(t))
            z = z_ref[at, cols]
            turn = jnp.tanh(GELU_A * (z + GELU_B * (z * z * z)))
            slope = 0.5 * (1.0 + turn) + (0.5 * GELU_A) * z * (1.0 - turn * turn) * (1.0 + (3.0 * GELU_B) * z * z)
            dz = (d_hid * slope).astype(BF)
            dz_ref[at, cols] = dz
            back = back + dot_nt(dz, tile_of(w_in_ref, t))
        hat, inv = hat_two_ref[at, :], inv_two_ref[at, :]
        sums_ref[2:3, :] += jnp.sum(back * hat, axis=0, keepdims=True)
        sums_ref[3:4, :] += jnp.sum(back, axis=0, keepdims=True)
        d_two = norm_pull(back, hat, inv, norm_ref[2:3, :])
        d_two_ref[at, :] = d_two
        d_mixed_ref[at, :] = dot_nt(d_two.astype(BF), cross_out).astype(BF)
        return carry

    lax.fori_loop(0, own // CHUNK, forward, 0)
    low_t_ref[...] = jnp.transpose(low_ref[...])


def feed(size, place, weights, mixed, whole_two, hat_one, norms, cot):
    own, width = hat_one.shape
    hidden = size.hidden
    devices = 2 * size.x_count * size.pieces
    return kernel_call(
        functools.partial(feed_kernel, size),
        out_shape=(
            shape((own, width)),
            shape((own, width), F32),
            shape((own, width)),
            shape((8, width), F32),
            shape((width, own)),
            shape((own, hidden)),
            shape((own, hidden)),
            shape((own, width)),
            shape((width, own)),
        ),
        in_specs=[SMEM, ANY, ANY] + [VMEM] * 5,
        out_specs=(VMEM,) * 9,
        scratch_shapes=[
            pltpu.VMEM((hidden // width, devices, size.tile_rows, width), BF),
            pltpu.VMEM((devices, hidden // devices, width), BF),
            pltpu.VMEM((own, hidden), F32),
            pltpu.VMEM((own, width), BF),
            pltpu.VMEM((own, width), F32),
            pltpu.VMEM((own, 1), F32),
            pltpu.SemaphoreType.DMA((2 * size.x_count * (hidden // width + 1),)),
        ],
    )(place, *weights, mixed, whole_two, hat_one, norms, cot)


def feed_grads_kernel(
    size, e, place_ref, low_t_ref, dz_ref, hid_ref, down_ref, mixed_t_ref, d_two_ref, target
):
    width = low_t_ref.shape[0]
    hidden = dz_ref.shape[1]
    tiles = hidden // width
    lefts = grad_rows(place_ref, low_t_ref, 2 * size.x_count, e)
    for t in range(tiles):
        put_grad(target, dot_f32(lefts, dz_ref[:, t * width : (t + 1) * width]), t, size.tile_rows)
    value = dot_f32(grad_rows(place_ref, mixed_t_ref, 2 * size.x_count, e), d_two_ref[...].astype(BF))
    put_grad(target, value, tiles, size.tile_rows)
    rows = hidden // (2 * size.x_count)
    for k in range(size.x_count):
        dp = (place_ref[0] ^ k) * 2 + (place_ref[1] ^ e)
        cols = pl.ds(pl.multiple_of(dp * rows, rows), rows)
        value = dot_f32(jnp.transpose(hid_ref[:, cols]), down_ref[...]).astype(target.dtype)
        target[k, :, (tiles + 1) * size.tile_rows :, :] = value.reshape(size.pieces, rows // size.pieces, width)


def feed_grads(size, e, place, low_t, dz, hid, down, mixed_t, d_two):
    width = low_t.shape[0]
    tiles = size.hidden // width
    rows = (tiles + 1) * size.tile_rows + size.hidden // (2 * size.x_count * size.pieces)
    return kernel_call(
        functools.partial(feed_grads_kernel, size, e),
        out_shape=shape((size.x_count, size.pieces, rows, width)),
        in_specs=[SMEM] + [VMEM] * 6,
        out_specs=VMEM,
    )(place, low_t, dz, hid, down, mixed_t, d_two)


def back_pairs(size, d_kv_ref, w_k, w_v, kept_ref, send_ref):
    width = w_k.shape[1]
    count = size.length // (2 * CHUNK)
    for e, target in enumerate((kept_ref, send_ref)):

        def step(i, carry):
            at = chunk(i + e * count)
            value = dot_nt(d_kv_ref[at, :width], w_k) + dot_nt(d_kv_ref[at, width:], w_v)
            target[chunk(i), :] = value.astype(target.dtype)
            return carry

        lax.fori_loop(0, count, step, 0)


def turn_rows(size, near_ref, far_ref, left_ref):
    count = size.length // (2 * CHUNK)
    for e, ref in enumerate((near_ref, far_ref)):

        def step(i, carry):
            left_ref[:, chunk(i + e * count)] = jnp.transpose(sequence_rows(ref, i, size.half))
            return carry

        lax.fori_loop(0, count, step, 0)


def back_cross_kernel(
    size,
    place_ref,
    d_kv_ref,
    d_q_ref,
    whole_ref,
    hat_ref,
    inv_ref,
    norm_ref,
    d_two_ref,
    sums_in_ref,
    kept_rows_ref,
    send_rows_ref,
    d_one_ref,
    d_mixed_ref,
    sums_ref,
    low_t_ref,
):
    hat, inv, gain = hat_ref[...], inv_ref[...], norm_ref[0:1, :]
    upstream = d_two_ref[...] + dot_nt(d_q_ref[...], whole_ref[1])
    sums_ref[...] = sums_in_ref[...]
    sums_ref[0:1, :] = jnp.sum(upstream * hat, axis=0, keepdims=True)
    sums_ref[1:2, :] = jnp.sum(upstream, axis=0, keepdims=True)
    d_one = norm_pull(upstream, hat, inv, gain)
    d_one_ref[...] = d_one
    d_mixed_ref[...] = dot_nt(d_one.astype(BF), whole_ref[0]).astype(BF)
    low_t_ref[...] = jnp.transpose((hat * gain + norm_ref[1:2, :]).astype(BF))
    back_pairs(size, d_kv_ref, whole_ref[2], whole_ref[3], kept_rows_ref, send_rows_ref)


def back_cross(size, place, d_kv, d_q, whole, hat, inv, norms, d_two, sums):
    own, width = hat.shape
    return kernel_call(
        functools.partial(back_cross_kernel, size),
        out_shape=(
            shape((size.length // 2, width)),
            shape((size.length // 2, width)),
            shape((own, width), F32),
            shape((own, width)),
            shape((8, width), F32),
            shape((width, own)),
        ),
        in_specs=[SMEM] + [VMEM] * 8,
        out_specs=(VMEM,) * 6,
    )(place, d_kv, d_q, whole, hat, inv, norms, d_two, sums)


def cross_grads_kernel(
    size,
    place_ref,
    near_ref,
    far_ref,
    d_kv_ref,
    d_q_ref,
    low_t_ref,
    mixed_self_ref,
    d_one_ref,
    sums_ref,
    kept_ref,
    send_ref,
    left_ref,
    self_t_ref,
    cols_ref,
):
    width = d_one_ref.shape[1]
    dp_count = 2 * size.x_count
    self_t_ref[...] = jnp.transpose(mixed_self_ref[...])
    pad = jnp.zeros((128 - sums_ref.shape[0], width), F32)
    cols_ref[...] = jnp.zeros(cols_ref.shape, F32)
    cols_ref[:, :128] = jnp.transpose(jnp.concatenate([sums_ref[...], pad], axis=0))
    turn_rows(size, near_ref, far_ref, left_ref)
    for e, target in enumerate((kept_ref, send_ref)):
        value = dot_f32(grad_rows(place_ref, self_t_ref, dp_count, e), d_one_ref[...].astype(BF))
        put_grad(target, value, 0, size.tile_rows)
        put_grad(target, dot_f32(grad_rows(place_ref, low_t_ref, dp_count, e), d_q_ref[...]), 1, size.tile_rows)
        lefts = grad_rows(place_ref, left_ref, dp_count, e)
        for t in range(2):
            put_grad(target, dot_f32(lefts, d_kv_ref[:, t * width : (t + 1) * width]), 2 + t, size.tile_rows)
        put_grad(target, grad_rows(place_ref, cols_ref, dp_count, e), 4, size.tile_rows)


def cross_grads(size, place, near, far, d_kv, d_q, low_t, mixed_self, d_one, sums):
    own, width = d_one.shape
    group = (size.x_count, size.pieces, 5 * size.tile_rows, width)
    return kernel_call(
        functools.partial(cross_grads_kernel, size),
        out_shape=(shape(group), shape(group)),
        in_specs=[SMEM] + [VMEM] * 8,
        out_specs=(VMEM,) * 2,
        scratch_shapes=[
            pltpu.VMEM((width, size.length), BF),
            pltpu.VMEM((width, own), BF),
            pltpu.VMEM((width, width), F32),
        ],
    )(place, near, far, d_kv, d_q, low_t, mixed_self, d_one, sums)


def self_grads_kernel(size, place_ref, near_ref, far_ref, d_kv_ref, d_q_ref, kept_ref, send_ref, left_ref, own_t_ref):
    width = d_q_ref.shape[1]
    dp_count = 2 * size.x_count
    turn_rows(size, near_ref, far_ref, left_ref)
    own_t_ref[...] = jnp.transpose(own_tokens(near_ref, place_ref, size.half, size.z_count))
    for e, target in enumerate((kept_ref, send_ref)):
        put_grad(target, dot_f32(grad_rows(place_ref, own_t_ref, dp_count, e), d_q_ref[...]), 0, size.tile_rows)
        lefts = grad_rows(place_ref, left_ref, dp_count, e)
        for t in range(2):
            put_grad(target, dot_f32(lefts, d_kv_ref[:, t * width : (t + 1) * width]), 1 + t, size.tile_rows)


def self_grads(size, place, near, far, d_kv, d_q):
    own, width = d_q.shape
    group = (size.x_count, size.pieces, 3 * size.tile_rows, width)
    return kernel_call(
        functools.partial(self_grads_kernel, size),
        out_shape=(shape(group), shape(group)),
        in_specs=[SMEM] + [VMEM] * 4,
        out_specs=(VMEM,) * 2,
        scratch_shapes=[pltpu.VMEM((width, size.length), BF), pltpu.VMEM((width, own), BF)],
    )(place, near, far, d_kv, d_q)


def back_self_kernel(size, place_ref, d_kv_ref, d_q_ref, whole_ref, d_one_ref, kept_rows_ref, send_rows_ref):
    back_pairs(size, d_kv_ref, whole_ref[1], whole_ref[2], kept_rows_ref, send_rows_ref)
    mine = d_one_ref[...] + dot_nt(d_q_ref[...], whole_ref[0])
    half = size.half
    y_count = size.length // (2 * half * size.z_count)
    for z in range(size.z_count):
        at = pl.ds(pl.multiple_of((z * y_count + place_ref[3]) * half, half), half)
        total = kept_rows_ref[at, :].astype(F32) + mine[z * half : (z + 1) * half]
        kept_rows_ref[at, :] = total.astype(kept_rows_ref.dtype)


def back_self(size, place, d_kv, d_q, whole, d_one):
    width = d_one.shape[1]
    return kernel_call(
        functools.partial(back_self_kernel, size),
        out_shape=(shape((size.length // 2, width)), shape((size.length // 2, width))),
        in_specs=[SMEM] + [VMEM] * 4,
        out_specs=(VMEM,) * 2,
    )(place, d_kv, d_q, whole, d_one)


def together(*values):
    return lax.optimization_barrier(values)


def unxor(parts, place):
    if len(parts) == 2:
        return jnp.where(place == 0, jnp.stack(parts), jnp.stack(parts[::-1]))
    out = jnp.zeros((len(parts),) + parts[0].shape, parts[0].dtype)
    for k, part in enumerate(parts):
        out = lax.dynamic_update_index_in_dim(out, part, place ^ k, 0)
    return out


def body(
    inputs,
    encoder,
    tgt_seg,
    src_len,
    cotangent,
    self_in,
    self_out,
    cross_q,
    cross_kv,
    cross_out,
    ffn_in,
    ffn_out,
    norm_params,
):
    held, local_rows, width = inputs.shape
    half = local_rows // 2
    dp_count, seq_count = lax.axis_size("dp"), lax.axis_size("seq")
    length = local_rows * seq_count
    x_count = dp_count // 2
    z_count = 2 * held
    y_count = seq_count // z_count
    dp_place, seq_place = lax.axis_index("dp"), lax.axis_index("seq")
    x_place, c_place = dp_place // 2, dp_place % 2
    z_place, y_place = seq_place // y_count, seq_place % y_count
    place = jnp.stack([x_place, c_place, z_place, y_place]).astype(jnp.int32)
    rows = self_in.shape[0]
    fine = rows % 16 == 0
    pieces = seq_count if fine else 1
    tile_rows = rows * seq_count // pieces

    def over_core(v):
        return lax.ppermute(v, "dp", [(i, i ^ 1) for i in range(dp_count)])

    def over_x(v, k):
        return v if k == 0 else lax.ppermute(v, "dp", [(i, i ^ (2 * k)) for i in range(dp_count)])

    def over_y(v, k):
        return v if k == 0 else lax.ppermute(v, "seq", [(i, i ^ k) for i in range(seq_count)])

    def over_z(v, k):
        return v if k == 0 else lax.ppermute(v, "seq", [(i, i ^ (k * y_count)) for i in range(seq_count)])

    def pick(v, at, axis=0):
        return lax.dynamic_index_in_dim(v, at, axis, keepdims=False)

    def by_core(mine, other, axis=0):
        return jnp.where(
            c_place == 0, jnp.concatenate([mine, other], axis=axis), jnp.concatenate([other, mine], axis=axis)
        )

    def exchange(v):
        return lax.all_to_all(v, "seq", 0, 0, tiled=True)

    def exchange_z(v):
        groups = [[z * y_count + y for z in range(z_count)] for y in range(y_count)]
        return lax.all_to_all(v, "seq", 0, 0, tiled=True, axis_index_groups=groups)

    def tiles_of(v):
        return v.reshape(rows, -1, width).transpose(1, 0, 2).reshape(-1, width)

    def y_gather(v):
        return y_order(y_moves(v))

    def y_moves(v):
        return [over_y(v, k) for k in range(y_count)]

    def y_order(moves):
        return unxor(moves, y_place).swapaxes(0, 1).reshape((seq_count,) + moves[0].shape[1:])

    def with_weights(blocks, weights):
        weights = weights.reshape(-1, width)
        return jnp.concatenate([blocks, jnp.broadcast_to(weights, (z_count,) + weights.shape)], axis=1)

    def coarse_parts(v, outer):
        whole = lax.all_gather(v, ("dp", "seq"), axis=0).reshape((x_count, 2, seq_count) + v.shape)
        inner = whole[:, :, :, : v.shape[0] - outer].reshape(x_count, 2, seq_count, -1, rows, width)
        inner = inner.swapaxes(2, 3).reshape(x_count, 2, -1, width)
        whole = jnp.concatenate([inner, whole[:, :, :, v.shape[0] - outer :].reshape(x_count, 2, -1, width)], axis=2)
        out = []
        for e in range(2):
            mine = pick(whole, c_place ^ e, 1)
            out.append(jnp.concatenate([pick(mine, x_place ^ k) for k in range(x_count)])[None])
        return out

    def x_sum(kept, came):
        total = kept[0].astype(F32) + came[0]
        for k in range(1, x_count):
            total = total + over_x((kept[k].astype(F32) + came[k]).astype(BF), k)
        return total

    def by_owner(v, outer):
        if fine:
            return v
        inner = v[0, : v.shape[1] - outer].reshape(-1, seq_count, rows, width).swapaxes(0, 1)
        inner = inner.reshape(seq_count, -1, width)
        return jnp.concatenate([inner, v[0, v.shape[1] - outer :].reshape(seq_count, -1, width)], axis=1)

    def y_sum(v):
        v = v.reshape((z_count, y_count) + v.shape[1:])
        total = pick(v, y_place, 1)
        for k in range(1, y_count):
            total = total + over_y(pick(v, y_place ^ k, 1).astype(BF), k)
        return total

    def untiled(v):
        return v.reshape(-1, rows, width).transpose(1, 0, 2).reshape(rows, -1)

    def home(v):
        v = v.astype(BF).reshape(2, held, half, width)
        mine, other = pick(v, c_place), over_core(pick(v, 1 - c_place))
        mine, other = mine[:, None], other[:, None]
        return by_core(mine, other, 1).reshape(held, local_rows, width).astype(F32)

    notes = jnp.concatenate([tgt_seg, src_len], axis=1)
    notes = pick(by_core(notes, over_core(notes)), z_place)
    target_all, lengths = notes[:length], notes[length:]
    docs = lengths.shape[0]
    upto = lax.broadcasted_iota(jnp.int32, (docs, docs), 0) <= lax.broadcasted_iota(jnp.int32, (docs, docs), 1)
    ends = jnp.sum(jnp.where(upto, lengths[:, None], 0), axis=0, dtype=jnp.int32)
    positions = jnp.arange(length, dtype=jnp.int32)
    source_all = jnp.sum((positions[:, None] >= ends[None, :]).astype(jnp.int32), axis=1, dtype=jnp.int32)
    qseg = pick(target_all.reshape(z_count, y_count * 2, half), y_place * 2 + c_place, 1)
    keys = 2 * half

    def in_order(segments):
        pairs = segments.reshape(-1, 2, half)
        return jnp.where(c_place == 0, pairs, pairs[:, ::-1]).reshape(-1, keys)

    def visits(segments):
        low = jnp.sum((segments[None, :] < qseg[:, :1]).astype(jnp.int32), axis=1, dtype=jnp.int32)
        high = jnp.sum((segments[None, :] <= qseg[:, -1:]).astype(jnp.int32), axis=1, dtype=jnp.int32)
        table = jnp.stack([low // keys, (high + keys - 1) // keys])
        return jnp.pad(table, ((0, 0), (0, length // keys - z_count)))

    self_kseg, cross_kseg = in_order(target_all), in_order(source_all)
    self_visits, cross_visits = visits(target_all), visits(source_all)

    hidden = ffn_in.shape[1]
    outer = ffn_out.shape[0]
    norm_wide = jnp.pad(norm_params, ((0, 0), (0, width - norm_params.shape[1])))
    first_tiles = tiles_of(self_in)
    rest_tiles = tiles_of(jnp.concatenate([self_out, cross_q, cross_kv, cross_out, norm_wide, ffn_in], axis=1))
    rest_tiles = jnp.concatenate([rest_tiles, ffn_out], axis=0)
    mid = 6 * rows
    size = Size(
        half=half,
        length=length,
        own=z_count * half,
        z_count=z_count,
        x_count=x_count,
        pieces=pieces,
        tile_rows=tile_rows,
        hidden=hidden,
        first=half if fine else 0,
    )
    streams = jnp.stack([inputs, encoder, cotangent]).reshape(3, held, 2, half, width)
    mine = pick(streams, c_place, 2)
    other = over_core(pick(streams, 1 - c_place, 2))
    streams = by_core(mine, other, 1)
    x_blocks, source_blocks, cot = streams[0], streams[1], streams[2]
    if fine:
        w1 = jnp.stack([over_x(first_tiles, k) for k in range(x_count)])
        rest = jnp.stack([over_x(rest_tiles, k) for k in range(x_count)])
        x_blocks = with_weights(x_blocks, w1)
        source_blocks = with_weights(source_blocks, rest[:, :mid])
        cot = with_weights(cot, rest[:, mid:])
    x_near = exchange_z(x_blocks)
    x_near, source_blocks = together(x_near, source_blocks)
    x_near = y_gather(x_near)
    source_near = exchange_z(source_blocks)
    x_far = over_core(x_near)
    weights = (x_near, x_far) if fine else coarse_parts(first_tiles, 0)

    queries, pairs, whole_one = project(size, place, weights, x_near, x_far)
    whole_one = whole_one.reshape(3, width, width)
    queries, source_near, cot = together(queries, source_near, cot)
    source_near = y_gather(source_near)
    cot = exchange_z(cot)
    mixed_self, self_lse = attend(self_visits, queries, pairs, qseg, self_kseg)
    mixed_self, source_near, cot = together(mixed_self, source_near, cot)
    source_far = over_core(source_near)
    mixed_self, source_far = together(mixed_self, source_far)
    w3 = y_moves(cot[:, half:]) if fine else None
    weights = (source_near, source_far) if fine else coarse_parts(rest_tiles[:mid], 0)
    queries_c, pairs_c, whole_two, hat_one, inv_one, norms = bridge(
        size, place, weights, x_near, source_near, source_far, mixed_self
    )
    whole_two = whole_two.reshape(6, width, width)
    mixed_cross, cross_lse = attend(cross_visits, queries_c, pairs_c, qseg, cross_kseg)
    if fine:
        mixed_cross, w3 = together(mixed_cross, w3)
        w3 = y_order(w3)
        weights = (w3, over_core(w3))
    else:
        weights = coarse_parts(rest_tiles[mid:], outer)
    out_low, d_two, d_mixed_c, sums, low_t, dz, hid, down, mixed_ct = feed(
        size, place, weights, mixed_cross, whole_two, hat_one, norms, cot
    )

    out_parts = exchange_z(out_low.reshape(z_count, half, width))
    f_send = feed_grads(size, 1, place, low_t, dz, hid, down, mixed_ct, d_two)
    f_came = over_core(f_send)
    low_t, f_send = together(low_t, f_send)
    f_kept = feed_grads(size, 0, place, low_t, dz, hid, down, mixed_ct, d_two)
    d_mixed_c, f_kept, f_came = together(d_mixed_c, f_kept, f_came)
    f_sum = x_sum(f_kept, f_came)
    d_queries_c, d_pairs_c = attend_back(
        cross_visits, queries_c, d_mixed_c, mixed_cross, cross_lse, pairs_c, qseg, cross_kseg
    )
    s_kept, s_send, d_one, d_mixed, sums, low_one_t = back_cross(
        size, place, d_pairs_c, d_queries_c, whole_two, hat_one, inv_one, norms, d_two, sums
    )
    d_one, f_sum, s_send, s_kept, out_parts = together(d_one, f_sum, s_send, s_kept, out_parts)
    s_came = over_core(s_send)
    f_sum = y_sum(by_owner(f_sum, hidden // dp_count))
    c_kept, c_send = cross_grads(
        size, place, source_near, source_far, d_pairs_c, d_queries_c, low_one_t, mixed_self, d_one, sums
    )
    d_mixed, s_came, c_send, f_sum = together(d_mixed, s_came, c_send, f_sum)
    c_came = over_core(c_send)
    s_sum = y_sum((s_kept.astype(F32) + s_came).reshape(seq_count, half, width))
    f_sum = exchange_z(f_sum.astype(BF))
    d_queries, d_pairs = attend_back(
        self_visits, queries, d_mixed, mixed_self, self_lse, pairs, qseg, self_kseg
    )
    d_pairs, s_sum, c_came, f_sum = together(d_pairs, s_sum, c_came, f_sum)
    s_parts = exchange_z(s_sum.astype(BF))
    c_sum = x_sum(c_kept, c_came)
    x_kept, x_send = back_self(size, place, d_pairs, d_queries, whole_one, d_one)
    x_came = over_core(x_send)
    d_pairs, x_send = together(d_pairs, x_send)
    i_kept, i_send = self_grads(size, place, x_near, x_far, d_pairs, d_queries)
    i_came = over_core(i_send)
    x_came, x_kept, i_send, s_parts = together(x_came, x_kept, i_send, s_parts)
    x_total = (x_kept.astype(F32) + x_came).astype(BF)
    x_parts = exchange(x_total.reshape(seq_count, half, width))
    x_total, i_came, i_kept = together(x_total, i_came, i_kept)
    i_sum = x_sum(i_kept, i_came)
    i_kept, s_parts, out_parts, f_sum = together(i_kept, s_parts, out_parts, f_sum)
    grad_source = home(s_parts)
    out_tokens = home(out_parts)
    f_own = jnp.sum(f_sum.astype(F32), axis=0)
    w_sum = y_sum(jnp.concatenate([by_owner(c_sum, 0), by_owner(i_sum, 0)], axis=1))
    w_own = pick(w_sum, z_place)
    for k in range(1, z_count):
        w_own = w_own + over_z(pick(w_sum, z_place ^ k).astype(BF), k)
    c_own, i_own = w_own[: 5 * rows], w_own[5 * rows :]
    grad_tokens = home(jnp.sum(x_parts.reshape(z_count, y_count, half, width).astype(F32), axis=1))
    f_in = hidden // width * rows
    c_own = c_own.reshape(5, rows, width)
    return (
        out_tokens,
        grad_tokens,
        grad_source,
        untiled(i_own),
        c_own[0],
        c_own[1],
        untiled(c_own[2:4]),
        f_own[f_in : f_in + rows],
        untiled(f_own[:f_in]),
        f_own[f_in + rows :],
        c_own[4][:, : norm_params.shape[1]],
    )


def solution(mesh):
    tokens, rows = P("dp", "seq", None), P(("dp", "seq"), None)
    return jax.shard_map(
        body,
        mesh=mesh,
        in_specs=(tokens, tokens, P("dp", None), P("dp", None), tokens) + (rows,) * 8,
        out_specs=(tokens,) * 3 + (rows,) * 8,
        check_vma=False,
    )
```

```python
import dataclasses
import functools
import math

import jax
import jax.numpy as jnp
from jax import lax
from jax.experimental import pallas as pl
from jax.experimental.pallas import tpu as pltpu
from jax.sharding import PartitionSpec as P

HEAD_DIM = 64
GROUP = 4
LANES = GROUP * HEAD_DIM
PACE = 1.15e9 * 0.1
CHUNK = 256
LOG2E = 1.4426950408889634
LN2 = 0.6931471805599453
GELU_A = 0.7978845608028654
GELU_B = 0.044715
BF = jnp.bfloat16
F32 = jnp.float32
SMEM = pl.BlockSpec(memory_space=pltpu.SMEM)
VMEM = pl.BlockSpec(memory_space=pltpu.VMEM)
ANY = pl.BlockSpec(memory_space=pl.ANY)


def dot_f32(left, right):
    return jnp.dot(left, right, preferred_element_type=F32)


def dot_nt(left, right):
    return lax.dot_general(left, right, (((1,), (1,)), ((), ())), preferred_element_type=F32)


def padded_bytes(dims, dtype):
    dims = (1,) * (2 - len(dims)) + tuple(dims)
    lead = math.prod(dims[:-2])
    return lead * (-(-dims[-2] // 16) * 16) * (-(-dims[-1] // 128) * 128) * jnp.dtype(dtype).itemsize


def kernel_call(kernel, *, out_shape, in_specs, out_specs, scratch_shapes=(), spare=3, us=2):
    def call(*operands):
        need = spare * 2**20
        for operand, spec in zip(operands, in_specs):
            need += padded_bytes(operand.shape, operand.dtype) if spec is VMEM else 0
        for result in jax.tree.leaves(out_shape):
            need += padded_bytes(result.shape, result.dtype)
        for scratch in scratch_shapes:
            if getattr(scratch, "memory_space", None) == pltpu.VMEM:
                need += padded_bytes(scratch.shape, scratch.dtype)
        return pl.pallas_call(
            kernel,
            out_shape=out_shape,
            in_specs=in_specs,
            out_specs=out_specs,
            scratch_shapes=scratch_shapes,
            compiler_params=pltpu.CompilerParams(vmem_limit_bytes=need),
            cost_estimate=pl.CostEstimate(flops=int(us * PACE), bytes_accessed=2**10, transcendentals=0),
        )(*operands)

    return call


def shape(dims, dtype=BF):
    return jax.ShapeDtypeStruct(dims, dtype)


def chunk(i):
    return pl.ds(pl.multiple_of(i * CHUNK, CHUNK), CHUNK)


@dataclasses.dataclass(frozen=True)
class Size:
    half: int
    length: int
    own: int
    z_count: int
    x_count: int
    pieces: int
    tile_rows: int
    hidden: int
    feed_rows: int
    first_one: tuple
    first_two: tuple
    first_three: tuple


def stack_heads(tile):
    head = lax.broadcasted_iota(jnp.int32, tile.shape, 1) // HEAD_DIM
    zero = jnp.zeros_like(tile)
    return jnp.concatenate([jnp.where(head == h, tile, zero) for h in range(GROUP)], axis=0)


def row_of(column):
    return jnp.transpose(jnp.broadcast_to(column, (column.shape[0], 128)))[0:1, :]


def key_rows(b, keys, total):
    half = keys // 2
    at = pl.multiple_of(b * half, half)
    return pl.ds(at, half), pl.ds(pl.multiple_of(at + total // 2, half), half)


def both_rows(ref, spots, cols):
    return jnp.concatenate([ref[spot, cols] for spot in spots], axis=0)


def turn_segments(kseg_ref, seg_ref):
    count, _, keys = kseg_ref.shape
    for b in range(count):
        row = kseg_ref[b].astype(F32)
        seg_ref[b * keys : (b + 1) * keys, :] = jnp.transpose(jnp.broadcast_to(row, (128, keys)))[:, :1]


def attend_part(visit_ref, q_ref, kv_ref, qseg_ref, seg_ref, o_ref, lse_ref, acc_ref, qst_ref):
    width = q_ref.shape[1]
    blocks = qseg_ref.shape[0]
    rows = q_ref.shape[0] // blocks
    total = kv_ref.shape[0]
    keys = total // visit_ref.shape[1]
    groups = width // LANES

    def block(k, carry):
        lo, hi = visit_ref[0, k], visit_ref[1, k]
        q_rows = pl.ds(pl.multiple_of(k * rows, rows), rows)
        qseg = jnp.concatenate([qseg_ref[k].astype(F32)] * GROUP, axis=1)
        for g in range(groups):
            qst_ref[g] = stack_heads(q_ref[q_rows, g * LANES : (g + 1) * LANES])
        acc_ref[...] = jnp.zeros(acc_ref.shape, F32)

        def step(b, carry):
            spots = key_rows(b, keys, total)
            same = seg_ref[pl.ds(pl.multiple_of(b * keys, keys), keys), :] == qseg
            scores = [
                dot_nt(both_rows(kv_ref, spots, slice(g * LANES, (g + 1) * LANES)), qst_ref[g]) for g in range(groups)
            ]
            out, lows, fades = [], [], []
            for g in range(groups):
                top, tot = carry[g]
                masked = jnp.where(same, scores[g], -1e30)
                new = jnp.maximum(top, jnp.max(masked, axis=0, keepdims=True))
                soft = jnp.exp2(masked - new)
                fade = jnp.exp2(top - new)
                out.append((new, tot * fade + jnp.sum(soft, axis=0, keepdims=True)))
                lows.append(soft.astype(BF))
                fades.append(fade)
            for g in range(groups):
                turned = jnp.transpose(both_rows(kv_ref, spots, slice(width + g * LANES, width + (g + 1) * LANES)))
                for h in range(GROUP):
                    at = g * LANES + h * HEAD_DIM
                    cols = slice(h * rows, (h + 1) * rows)
                    values = turned[h * HEAD_DIM : (h + 1) * HEAD_DIM]
                    acc_ref[at : at + HEAD_DIM] = acc_ref[at : at + HEAD_DIM] * fades[g][:, cols] + dot_f32(
                        values, lows[g][:, cols]
                    )
            return tuple(out)

        start = (jnp.full((1, GROUP * rows), -3e38, F32), jnp.zeros((1, GROUP * rows), F32))
        end = lax.fori_loop(lo, hi, step, (start,) * groups)
        for g in range(groups):
            top, tot = end[g]
            inv = 1.0 / tot
            mixed = [
                acc_ref[g * LANES + h * HEAD_DIM : g * LANES + (h + 1) * HEAD_DIM] * inv[:, h * rows : (h + 1) * rows]
                for h in range(GROUP)
            ]
            o_ref[q_rows, g * LANES : (g + 1) * LANES] = jnp.transpose(jnp.concatenate(mixed, axis=0)).astype(BF)
            lse_ref[k * groups + g] = top + jnp.log2(tot)
        return carry

    lax.fori_loop(0, blocks, block, 0)


def attend_back_part(
    visit_ref,
    q_ref,
    do_ref,
    o_ref,
    lse_ref,
    kv_ref,
    qseg_ref,
    seg_ref,
    dq_ref,
    dkv_ref,
    sum_ref,
    dqt_ref,
    qst_ref,
    dst_ref,
    delta_ref,
):
    width = q_ref.shape[1]
    blocks = qseg_ref.shape[0]
    rows = q_ref.shape[0] // blocks
    total = kv_ref.shape[0]
    keys = total // visit_ref.shape[1]
    groups = width // LANES
    sum_ref[...] = jnp.zeros(sum_ref.shape, F32)

    def block(k, carry):
        lo, hi = visit_ref[0, k], visit_ref[1, k]
        q_rows = pl.ds(pl.multiple_of(k * rows, rows), rows)
        qseg = jnp.concatenate([qseg_ref[k].astype(F32)] * GROUP, axis=1)
        for g in range(groups):
            cols = slice(g * LANES, (g + 1) * LANES)
            qst_ref[g] = stack_heads(q_ref[q_rows, cols])
            d_mixed = do_ref[q_rows, cols]
            dst_ref[g] = stack_heads(d_mixed)
            prod = d_mixed.astype(F32) * o_ref[q_rows, cols].astype(F32)
            delta_ref[g] = row_of(jnp.sum(stack_heads(prod), axis=1, keepdims=True))
        dqt_ref[...] = jnp.zeros(dqt_ref.shape, F32)

        def step(b, carry):
            spots = key_rows(b, keys, total)
            same = seg_ref[pl.ds(pl.multiple_of(b * keys, keys), keys), :] == qseg
            k_cols = [slice(g * LANES, (g + 1) * LANES) for g in range(groups)]
            v_cols = [slice(width + g * LANES, width + (g + 1) * LANES) for g in range(groups)]
            scores = [dot_nt(both_rows(kv_ref, spots, k_cols[g]), qst_ref[g]) for g in range(groups)]
            d_soft = [dot_nt(both_rows(kv_ref, spots, v_cols[g]), dst_ref[g]) for g in range(groups)]
            softs, d_scores = [], []
            for g in range(groups):
                soft = jnp.where(same, jnp.exp2(scores[g] - lse_ref[k * groups + g]), 0.0)
                d_scores.append((soft * (d_soft[g] - delta_ref[g])).astype(BF))
                softs.append(soft.astype(BF))
            for g in range(groups):
                d_keys, d_values = dot_f32(d_scores[g], qst_ref[g]), dot_f32(softs[g], dst_ref[g])
                for e, spot in enumerate(spots):
                    part = slice(e * keys // 2, (e + 1) * keys // 2)
                    sum_ref[spot, k_cols[g]] += d_keys[part]
                    sum_ref[spot, v_cols[g]] += d_values[part]
                turned = jnp.transpose(both_rows(kv_ref, spots, k_cols[g]))
                for h in range(GROUP):
                    at = slice(g * LANES + h * HEAD_DIM, g * LANES + (h + 1) * HEAD_DIM)
                    keys_t = turned[h * HEAD_DIM : (h + 1) * HEAD_DIM]
                    dqt_ref[at] += dot_f32(keys_t, d_scores[g][:, h * rows : (h + 1) * rows])
            return carry

        lax.fori_loop(lo, hi, step, 0)
        for g in range(groups):
            cols = slice(g * LANES, (g + 1) * LANES)
            dq_ref[q_rows, cols] = (jnp.transpose(dqt_ref[cols]) * HEAD_DIM**-0.5).astype(BF)
        return carry

    lax.fori_loop(0, blocks, block, 0)
    dkv_ref[:, :width] = (sum_ref[:, :width] * LN2).astype(BF)
    dkv_ref[:, width:] = sum_ref[:, width:].astype(BF)


def norm_of(resid):
    centered = resid - jnp.mean(resid, axis=-1, keepdims=True)
    inv = lax.rsqrt(jnp.mean(centered * centered, axis=-1, keepdims=True) + 1e-05)
    return centered * inv, inv


def norm_pull(upstream, hat, inv, gain):
    scaled = upstream * gain
    return inv * (
        scaled - jnp.mean(scaled, axis=-1, keepdims=True) - hat * jnp.mean(scaled * hat, axis=-1, keepdims=True)
    )


def weight_rows(size, weights, total, firsts):
    out = []
    per = len(weights) // 2
    for e in range(2):
        for k in range(size.x_count):
            a = min(k, per - 1)
            out.append((k, e, weights[e * per + a], firsts[a] + (k - a) * total))
    return out


def fetch_tiles(size, place_ref, weights, tiles, firsts, whole_ref, sem):
    copies = []
    rows = size.tile_rows
    for k, e, part, start in weight_rows(size, weights, tiles * rows, firsts):
        pieces = part.shape[0]
        dp = (place_ref[0] ^ k) * 2 + (place_ref[1] ^ e)
        at = pl.ds(pl.multiple_of(dp * pieces, pieces), pieces)
        for t in range(tiles):
            source = part.at[:, pl.ds(start + t * rows, rows)]
            copies.append(pltpu.make_async_copy(source, whole_ref.at[t, at], sem.at[len(copies)]))
    for copy in copies:
        copy.start()
    return copies


def tile_of(ref, t):
    tile = ref[t]
    return tile.reshape(-1, tile.shape[-1])


def own_tokens(near_ref, place_ref, half, z_count):
    y_count = near_ref.shape[0] // z_count
    return jnp.concatenate([near_ref[z * y_count + place_ref[3], :half, :] for z in range(z_count)], axis=0)


def sequence_rows(ref, i, half):
    count = CHUNK // half
    return jnp.concatenate([ref[i * count + j, :half, :] for j in range(count)], axis=0)


def put_pairs(near_ref, far_ref, half, w_k, w_v, kv_ref):
    width = w_k.shape[1]
    count = near_ref.shape[0] * half // CHUNK
    for e, ref in enumerate((near_ref, far_ref)):

        def step(i, carry):
            rows = sequence_rows(ref, i, half)
            at = chunk(i + e * count)
            kv_ref[at, :width] = dot_f32(rows, w_k).astype(BF)
            kv_ref[at, width:] = dot_f32(rows, w_v).astype(BF)
            return carry

        lax.fori_loop(0, count, step, 0)


def grad_rows(place_ref, left_ref, dp_count, e):
    rows = left_ref.shape[0] // dp_count
    out = []
    for k in range(dp_count // 2):
        dp = (place_ref[0] ^ k) * 2 + (place_ref[1] ^ e)
        out.append(left_ref[pl.ds(pl.multiple_of(dp * rows, rows), rows), :])
    return jnp.concatenate(out, axis=0)


def put_grad(target, value, tile, tile_rows):
    x_count, pieces, _, width = target.shape
    rows = value.shape[0] // x_count
    for k in range(x_count):
        part = value[k * rows : (k + 1) * rows].astype(target.dtype)
        target[k, :, tile * tile_rows : (tile + 1) * tile_rows, :] = part.reshape(pieces, tile_rows, width)


def attend_scratch(size, width):
    rows = size.own // size.z_count
    return [
        pltpu.VMEM((size.length, 1), F32),
        pltpu.VMEM((width, rows), F32),
        pltpu.VMEM((width // LANES, GROUP * rows, LANES), BF),
    ]


def first_kernel(
    size,
    visit_ref,
    place_ref,
    near_ref,
    far_ref,
    qseg_ref,
    kseg_ref,
    *refs,
):
    weights, (q_ref, kv_ref, whole_ref, o_ref, lse_ref, seg_ref, acc_ref, qst_ref, sem) = refs[:-9], refs[-9:]
    copies = fetch_tiles(size, place_ref, weights, 3, size.first_one, whole_ref, sem)
    own = own_tokens(near_ref, place_ref, size.half, size.z_count)
    turn_segments(kseg_ref, seg_ref)
    for copy in copies:
        copy.wait()
    q_ref[...] = (dot_f32(own, tile_of(whole_ref, 0)) * (HEAD_DIM**-0.5 * LOG2E)).astype(BF)
    put_pairs(near_ref, far_ref, size.half, tile_of(whole_ref, 1), tile_of(whole_ref, 2), kv_ref)
    attend_part(visit_ref, q_ref, kv_ref, qseg_ref, seg_ref, o_ref, lse_ref, acc_ref, qst_ref)


def lse_shape(size, width):
    return shape((size.z_count * width // LANES, 1, GROUP * size.half), F32)


def first(size, visits, place, weights, near, far, qseg, kseg):
    width = near.shape[2]
    return kernel_call(
        functools.partial(first_kernel, size),
        us=16,
        out_shape=(
            shape((size.own, width)),
            shape((size.length, 2 * width)),
            shape((3, 2 * size.x_count * size.pieces, size.tile_rows, width)),
            shape((size.own, width)),
            lse_shape(size, width),
        ),
        in_specs=[SMEM] * 2 + [VMEM] * 4 + [ANY] * len(weights),
        out_specs=(VMEM,) * 5,
        scratch_shapes=attend_scratch(size, width) + [pltpu.SemaphoreType.DMA((2 * size.x_count * 3,))],
    )(visits, place, near, far, qseg, kseg, *weights)


def second_kernel(
    size,
    visit_ref,
    place_ref,
    near_ref,
    source_near_ref,
    source_far_ref,
    mixed_ref,
    qseg_ref,
    kseg_ref,
    *refs,
):
    weights = refs[:-12]
    q_ref, kv_ref, whole_ref, hat_ref, inv_ref, norm_ref, o_ref, lse_ref, seg_ref, acc_ref, qst_ref, sem = refs[-12:]
    copies = fetch_tiles(size, place_ref, weights, 6, size.first_two, whole_ref, sem)
    own = own_tokens(near_ref, place_ref, size.half, size.z_count)
    turn_segments(kseg_ref, seg_ref)
    for copy in copies:
        copy.wait()
    norm_ref[...] = jnp.transpose(tile_of(whole_ref, 5)[:, :128].astype(F32))[: norm_ref.shape[0]]
    hat, inv = norm_of(own.astype(F32) + dot_f32(mixed_ref[...], tile_of(whole_ref, 0)))
    hat_ref[...] = hat
    inv_ref[...] = inv
    low = (hat * norm_ref[0:1, :] + norm_ref[1:2, :]).astype(BF)
    q_ref[...] = (dot_f32(low, tile_of(whole_ref, 1)) * (HEAD_DIM**-0.5 * LOG2E)).astype(BF)
    put_pairs(source_near_ref, source_far_ref, size.half, tile_of(whole_ref, 2), tile_of(whole_ref, 3), kv_ref)
    attend_part(visit_ref, q_ref, kv_ref, qseg_ref, seg_ref, o_ref, lse_ref, acc_ref, qst_ref)


def second(size, visits, place, weights, near, source_near, source_far, mixed, qseg, kseg):
    width = near.shape[2]
    return kernel_call(
        functools.partial(second_kernel, size),
        us=17,
        out_shape=(
            shape((size.own, width)),
            shape((size.length, 2 * width)),
            shape((6, 2 * size.x_count * size.pieces, size.tile_rows, width)),
            shape((size.own, width), F32),
            shape((size.own, 1), F32),
            shape((8, width), F32),
            shape((size.own, width)),
            lse_shape(size, width),
        ),
        in_specs=[SMEM] * 2 + [VMEM] * 6 + [ANY] * len(weights),
        out_specs=(VMEM,) * 8,
        scratch_shapes=attend_scratch(size, width) + [pltpu.SemaphoreType.DMA((2 * size.x_count * 6,))],
    )(visits, place, near, source_near, source_far, mixed, qseg, kseg, *weights)


def feed_kernel(
    size,
    place_ref,
    mixed_ref,
    whole_two_ref,
    hat_one_ref,
    norm_ref,
    cot_ref,
    *refs,
):
    weights = refs[:-16]
    (
        out_ref,
        d_two_ref,
        d_mixed_ref,
        sums_ref,
        low_t_ref,
        dz_ref,
        hid_ref,
        down_ref,
        mixed_t_ref,
        w_in_ref,
        w_out_ref,
        z_ref,
        low_ref,
        hat_two_ref,
        inv_two_ref,
        sem,
    ) = refs[-16:]
    own, width = hat_one_ref.shape
    hidden = z_ref.shape[1]
    tiles = hidden // width
    tile_rows = size.tile_rows
    copies = []
    total = size.feed_rows
    for k, e, part, start in weight_rows(size, weights, total, size.first_three):
        pieces = part.shape[0]
        dp = (place_ref[0] ^ k) * 2 + (place_ref[1] ^ e)
        at = pl.ds(pl.multiple_of(dp * pieces, pieces), pieces)
        for t in range(tiles):
            source = part.at[:, pl.ds(start + t * tile_rows, tile_rows)]
            copies.append(pltpu.make_async_copy(source, w_in_ref.at[t, at], sem.at[len(copies)]))
        source = part.at[:, pl.ds(start + tiles * tile_rows, total - tiles * tile_rows)]
        copies.append(pltpu.make_async_copy(source, w_out_ref.at[at], sem.at[len(copies)]))
    for copy in copies:
        copy.start()
    mixed_t_ref[...] = jnp.transpose(mixed_ref[...])
    sums_ref[...] = jnp.zeros(sums_ref.shape, F32)
    cross_out = whole_two_ref[4]
    for copy in copies:
        copy.wait()
    per_tile = w_out_ref.shape[0] // tiles

    def w_down(t):
        return w_out_ref[t * per_tile : (t + 1) * per_tile].reshape(width, width)

    def forward(i, carry):
        at = chunk(i)
        one = hat_one_ref[at, :] * norm_ref[0:1, :] + norm_ref[1:2, :]
        hat, inv = norm_of(one + dot_f32(mixed_ref[at, :], cross_out))
        hat_two_ref[at, :] = hat
        inv_two_ref[at, :] = inv
        two = hat * norm_ref[2:3, :] + norm_ref[3:4, :]
        low = two.astype(BF)
        low_ref[at, :] = low
        total = two
        for t in range(tiles):
            cols = slice(t * width, (t + 1) * width)
            z = dot_f32(low, tile_of(w_in_ref, t))
            z_ref[at, cols] = z
            turn = jnp.tanh(GELU_A * (z + GELU_B * (z * z * z)))
            hid = (0.5 * z * (1.0 + turn)).astype(BF)
            hid_ref[at, cols] = hid
            total = total + dot_f32(hid, w_down(t))
        hat, inv = norm_of(total)
        gain = norm_ref[4:5, :]
        out_ref[at, :] = (hat * gain + norm_ref[5:6, :]).astype(BF)
        upstream = sequence_rows(cot_ref, i, size.half).astype(F32)
        sums_ref[4:5, :] += jnp.sum(upstream * hat, axis=0, keepdims=True)
        sums_ref[5:6, :] += jnp.sum(upstream, axis=0, keepdims=True)
        down = norm_pull(upstream, hat, inv, gain)
        low_down = down.astype(BF)
        down_ref[at, :] = low_down
        back = down
        for t in range(tiles):
            cols = slice(t * width, (t + 1) * width)
            d_hid = dot_nt(low_down, w_down(t))
            z = z_ref[at, cols]
            turn = jnp.tanh(GELU_A * (z + GELU_B * (z * z * z)))
            slope = 0.5 * (1.0 + turn) + (0.5 * GELU_A) * z * (1.0 - turn * turn) * (1.0 + (3.0 * GELU_B) * z * z)
            dz = (d_hid * slope).astype(BF)
            dz_ref[at, cols] = dz
            back = back + dot_nt(dz, tile_of(w_in_ref, t))
        hat, inv = hat_two_ref[at, :], inv_two_ref[at, :]
        sums_ref[2:3, :] += jnp.sum(back * hat, axis=0, keepdims=True)
        sums_ref[3:4, :] += jnp.sum(back, axis=0, keepdims=True)
        d_two = norm_pull(back, hat, inv, norm_ref[2:3, :])
        d_two_ref[at, :] = d_two
        d_mixed_ref[at, :] = dot_nt(d_two.astype(BF), cross_out).astype(BF)
        return carry

    lax.fori_loop(0, own // CHUNK, forward, 0)
    low_t_ref[...] = jnp.transpose(low_ref[...])


def feed(size, place, weights, mixed, whole_two, hat_one, norms, cot):
    own, width = hat_one.shape
    hidden = size.hidden
    devices = 2 * size.x_count * size.pieces
    return kernel_call(
        functools.partial(feed_kernel, size),
        us=12,
        out_shape=(
            shape((own, width)),
            shape((own, width), F32),
            shape((own, width)),
            shape((8, width), F32),
            shape((width, own)),
            shape((own, hidden)),
            shape((own, hidden)),
            shape((own, width)),
            shape((width, own)),
        ),
        in_specs=[SMEM] + [VMEM] * 5 + [ANY] * len(weights),
        out_specs=(VMEM,) * 9,
        scratch_shapes=[
            pltpu.VMEM((hidden // width, devices, size.tile_rows, width), BF),
            pltpu.VMEM((devices, hidden // devices, width), BF),
            pltpu.VMEM((own, hidden), F32),
            pltpu.VMEM((own, width), BF),
            pltpu.VMEM((own, width), F32),
            pltpu.VMEM((own, 1), F32),
            pltpu.SemaphoreType.DMA((2 * size.x_count * (hidden // width + 1),)),
        ],
    )(place, mixed, whole_two, hat_one, norms, cot, *weights)


def feed_grads_kernel(
    size, e, place_ref, low_t_ref, dz_ref, hid_ref, down_ref, mixed_t_ref, d_two_ref, target
):
    width = low_t_ref.shape[0]
    hidden = dz_ref.shape[1]
    tiles = hidden // width
    lefts = grad_rows(place_ref, low_t_ref, 2 * size.x_count, e)
    for t in range(tiles):
        put_grad(target, dot_f32(lefts, dz_ref[:, t * width : (t + 1) * width]), t, size.tile_rows)
    value = dot_f32(grad_rows(place_ref, mixed_t_ref, 2 * size.x_count, e), d_two_ref[...].astype(BF))
    put_grad(target, value, tiles, size.tile_rows)
    rows = hidden // (2 * size.x_count)
    for k in range(size.x_count):
        dp = (place_ref[0] ^ k) * 2 + (place_ref[1] ^ e)
        cols = pl.ds(pl.multiple_of(dp * rows, rows), rows)
        value = dot_f32(jnp.transpose(hid_ref[:, cols]), down_ref[...]).astype(target.dtype)
        target[k, :, (tiles + 1) * size.tile_rows :, :] = value.reshape(size.pieces, rows // size.pieces, width)


def feed_grads(size, e, place, low_t, dz, hid, down, mixed_t, d_two):
    width = low_t.shape[0]
    tiles = size.hidden // width
    rows = (tiles + 1) * size.tile_rows + size.hidden // (2 * size.x_count * size.pieces)
    return kernel_call(
        functools.partial(feed_grads_kernel, size, e),
        out_shape=shape((size.x_count, size.pieces, rows, width)),
        in_specs=[SMEM] + [VMEM] * 6,
        out_specs=VMEM,
    )(place, low_t, dz, hid, down, mixed_t, d_two)


def back_pairs(size, d_kv_ref, w_k, w_v, kept_ref, send_ref):
    width = w_k.shape[1]
    count = size.length // (2 * CHUNK)
    for e, target in enumerate((kept_ref, send_ref)):

        def step(i, carry):
            at = chunk(i + e * count)
            value = dot_nt(d_kv_ref[at, :width], w_k) + dot_nt(d_kv_ref[at, width:], w_v)
            target[chunk(i), :] = value.astype(target.dtype)
            return carry

        lax.fori_loop(0, count, step, 0)


def turn_rows(size, near_ref, far_ref, left_ref):
    count = size.length // (2 * CHUNK)
    for e, ref in enumerate((near_ref, far_ref)):

        def step(i, carry):
            left_ref[:, chunk(i + e * count)] = jnp.transpose(sequence_rows(ref, i, size.half))
            return carry

        lax.fori_loop(0, count, step, 0)


def back_scratch(size, width):
    rows = size.own // size.z_count
    return [
        pltpu.VMEM((size.length, 1), F32),
        pltpu.VMEM((size.length, 2 * width), F32),
        pltpu.VMEM((width, rows), F32),
        pltpu.VMEM((width // LANES, GROUP * rows, LANES), BF),
        pltpu.VMEM((width // LANES, GROUP * rows, LANES), BF),
        pltpu.VMEM((width // LANES, 1, GROUP * rows), F32),
    ]


def third_kernel(
    size,
    visit_ref,
    place_ref,
    q_ref,
    do_ref,
    o_ref,
    lse_ref,
    kv_ref,
    qseg_ref,
    kseg_ref,
    near_ref,
    far_ref,
    whole_ref,
    hat_ref,
    inv_ref,
    norm_ref,
    d_two_ref,
    sums_in_ref,
    mixed_self_ref,
    kept_rows_ref,
    send_rows_ref,
    kept_ref,
    send_ref,
    d_one_ref,
    d_mixed_ref,
    seg_ref,
    sum_ref,
    dqt_ref,
    qst_ref,
    dst_ref,
    delta_ref,
    d_q_ref,
    d_kv_ref,
    left_ref,
    self_t_ref,
    low_t_ref,
    cols_ref,
):
    width = hat_ref.shape[1]
    dp_count = 2 * size.x_count
    turn_segments(kseg_ref, seg_ref)
    attend_back_part(
        visit_ref,
        q_ref,
        do_ref,
        o_ref,
        lse_ref,
        kv_ref,
        qseg_ref,
        seg_ref,
        d_q_ref,
        d_kv_ref,
        sum_ref,
        dqt_ref,
        qst_ref,
        dst_ref,
        delta_ref,
    )
    hat, inv, gain = hat_ref[...], inv_ref[...], norm_ref[0:1, :]
    upstream = d_two_ref[...] + dot_nt(d_q_ref[...], whole_ref[1])
    gain_sum = jnp.sum(upstream * hat, axis=0, keepdims=True)
    shift_sum = jnp.sum(upstream, axis=0, keepdims=True)
    d_one = norm_pull(upstream, hat, inv, gain)
    d_one_ref[...] = d_one
    low_one = d_one.astype(BF)
    d_mixed_ref[...] = dot_nt(low_one, whole_ref[0]).astype(BF)
    low_t_ref[...] = jnp.transpose((hat * gain + norm_ref[1:2, :]).astype(BF))
    back_pairs(size, d_kv_ref, whole_ref[2], whole_ref[3], kept_rows_ref, send_rows_ref)
    self_t_ref[...] = jnp.transpose(mixed_self_ref[...])
    pad = jnp.zeros((128 - sums_in_ref.shape[0], width), F32)
    cols_ref[...] = jnp.zeros(cols_ref.shape, F32)
    cols_ref[:, :128] = jnp.transpose(jnp.concatenate([gain_sum, shift_sum, sums_in_ref[2:, :], pad], axis=0))
    turn_rows(size, near_ref, far_ref, left_ref)
    for e, target in enumerate((kept_ref, send_ref)):
        put_grad(target, dot_f32(grad_rows(place_ref, self_t_ref, dp_count, e), low_one), 0, size.tile_rows)
        put_grad(target, dot_f32(grad_rows(place_ref, low_t_ref, dp_count, e), d_q_ref[...]), 1, size.tile_rows)
        lefts = grad_rows(place_ref, left_ref, dp_count, e)
        for t in range(2):
            put_grad(target, dot_f32(lefts, d_kv_ref[:, t * width : (t + 1) * width]), 2 + t, size.tile_rows)
        put_grad(target, grad_rows(place_ref, cols_ref, dp_count, e), 4, size.tile_rows)


def third(
    size, visits, place, q, do, o, lse, kv, qseg, kseg, near, far, whole, hat, inv, norms, d_two, sums, mixed_self
):
    own, width = hat.shape
    group = (size.x_count, size.pieces, 5 * size.tile_rows, width)
    return kernel_call(
        functools.partial(third_kernel, size),
        us=30,
        out_shape=(
            shape((size.length // 2, width)),
            shape((size.length // 2, width)),
            shape(group),
            shape(group),
            shape((own, width), F32),
            shape((own, width)),
        ),
        in_specs=[SMEM] * 2 + [VMEM] * 16,
        out_specs=(VMEM,) * 6,
        scratch_shapes=back_scratch(size, width)
        + [
            pltpu.VMEM((own, width), BF),
            pltpu.VMEM((size.length, 2 * width), BF),
            pltpu.VMEM((width, size.length), BF),
            pltpu.VMEM((width, own), BF),
            pltpu.VMEM((width, own), BF),
            pltpu.VMEM((width, width), F32),
        ],
    )(visits, place, q, do, o, lse, kv, qseg, kseg, near, far, whole, hat, inv, norms, d_two, sums, mixed_self)


def fourth_kernel(
    size,
    visit_ref,
    place_ref,
    q_ref,
    do_ref,
    o_ref,
    lse_ref,
    kv_ref,
    qseg_ref,
    kseg_ref,
    whole_ref,
    d_one_ref,
    near_ref,
    far_ref,
    kept_rows_ref,
    send_rows_ref,
    kept_ref,
    send_ref,
    seg_ref,
    sum_ref,
    dqt_ref,
    qst_ref,
    dst_ref,
    delta_ref,
    d_q_ref,
    d_kv_ref,
    left_ref,
    own_t_ref,
):
    turn_segments(kseg_ref, seg_ref)
    attend_back_part(
        visit_ref,
        q_ref,
        do_ref,
        o_ref,
        lse_ref,
        kv_ref,
        qseg_ref,
        seg_ref,
        d_q_ref,
        d_kv_ref,
        sum_ref,
        dqt_ref,
        qst_ref,
        dst_ref,
        delta_ref,
    )
    back_pairs(size, d_kv_ref, whole_ref[1], whole_ref[2], kept_rows_ref, send_rows_ref)
    mine = d_one_ref[...] + dot_nt(d_q_ref[...], whole_ref[0])
    half = size.half
    y_count = size.length // (2 * half * size.z_count)
    for z in range(size.z_count):
        at = pl.ds(pl.multiple_of((z * y_count + place_ref[3]) * half, half), half)
        total = kept_rows_ref[at, :].astype(F32) + mine[z * half : (z + 1) * half]
        kept_rows_ref[at, :] = total.astype(kept_rows_ref.dtype)
    width = d_one_ref.shape[1]
    dp_count = 2 * size.x_count
    turn_rows(size, near_ref, far_ref, left_ref)
    own_t_ref[...] = jnp.transpose(own_tokens(near_ref, place_ref, half, size.z_count))
    for e, target in enumerate((kept_ref, send_ref)):
        put_grad(target, dot_f32(grad_rows(place_ref, own_t_ref, dp_count, e), d_q_ref[...]), 0, size.tile_rows)
        lefts = grad_rows(place_ref, left_ref, dp_count, e)
        for t in range(2):
            put_grad(target, dot_f32(lefts, d_kv_ref[:, t * width : (t + 1) * width]), 1 + t, size.tile_rows)


def fourth(size, visits, place, q, do, o, lse, kv, qseg, kseg, whole, d_one, near, far):
    own, width = d_one.shape
    group = (size.x_count, size.pieces, 3 * size.tile_rows, width)
    return kernel_call(
        functools.partial(fourth_kernel, size),
        us=27,
        out_shape=(shape((size.length // 2, width)), shape((size.length // 2, width)), shape(group), shape(group)),
        in_specs=[SMEM] * 2 + [VMEM] * 11,
        out_specs=(VMEM,) * 4,
        scratch_shapes=back_scratch(size, width)
        + [
            pltpu.VMEM((own, width), BF),
            pltpu.VMEM((size.length, 2 * width), BF),
            pltpu.VMEM((width, size.length), BF),
            pltpu.VMEM((width, own), BF),
        ],
    )(visits, place, q, do, o, lse, kv, qseg, kseg, whole, d_one, near, far)


def together(*values):
    return lax.optimization_barrier(values)


def unxor(parts, place):
    if len(parts) == 2:
        return jnp.where(place == 0, jnp.stack(parts), jnp.stack(parts[::-1]))
    out = jnp.zeros((len(parts),) + parts[0].shape, parts[0].dtype)
    for k, part in enumerate(parts):
        out = lax.dynamic_update_index_in_dim(out, part, place ^ k, 0)
    return out


def body(
    inputs,
    encoder,
    tgt_seg,
    src_len,
    cotangent,
    self_in,
    self_out,
    cross_q,
    cross_kv,
    cross_out,
    ffn_in,
    ffn_out,
    norm_params,
):
    held, local_rows, width = inputs.shape
    half = local_rows // 2
    dp_count, seq_count = lax.axis_size("dp"), lax.axis_size("seq")
    length = local_rows * seq_count
    x_count = dp_count // 2
    z_count = 2 * held
    y_count = seq_count // z_count
    dp_place, seq_place = lax.axis_index("dp"), lax.axis_index("seq")
    x_place, c_place = dp_place // 2, dp_place % 2
    z_place, y_place = seq_place // y_count, seq_place % y_count
    place = jnp.stack([x_place, c_place, z_place, y_place]).astype(jnp.int32)
    rows = self_in.shape[0]
    fine = rows % 16 == 0
    pieces = seq_count if fine else 1
    tile_rows = rows * seq_count // pieces

    def over_core(v):
        return lax.ppermute(v, "dp", [(i, i ^ 1) for i in range(dp_count)])

    def over_x(v, k):
        return v if k == 0 else lax.ppermute(v, "dp", [(i, i ^ (2 * k)) for i in range(dp_count)])

    def over_y(v, k):
        return v if k == 0 else lax.ppermute(v, "seq", [(i, i ^ k) for i in range(seq_count)])

    def over_z(v, k):
        return v if k == 0 else lax.ppermute(v, "seq", [(i, i ^ (k * y_count)) for i in range(seq_count)])

    def pick(v, at, axis=0):
        return lax.dynamic_index_in_dim(v, at, axis, keepdims=False)

    def by_core(mine, other, axis=0):
        return jnp.where(
            c_place == 0, jnp.concatenate([mine, other], axis=axis), jnp.concatenate([other, mine], axis=axis)
        )

    def exchange(v):
        return lax.all_to_all(v, "seq", 0, 0, tiled=True)

    def exchange_z(v):
        groups = [[z * y_count + y for z in range(z_count)] for y in range(y_count)]
        return lax.all_to_all(v, "seq", 0, 0, tiled=True, axis_index_groups=groups)

    def tiles_of(v):
        return v.reshape(rows, -1, width).transpose(1, 0, 2).reshape(-1, width)

    def y_gather(v):
        return y_order(y_moves(v))

    def y_moves(v):
        return [over_y(v, k) for k in range(y_count)]

    def y_order(moves):
        return unxor(moves, y_place).swapaxes(0, 1).reshape((seq_count,) + moves[0].shape[1:])

    def with_weights(blocks, weights):
        weights = weights.reshape(-1, width)
        return jnp.concatenate([blocks, jnp.broadcast_to(weights, (z_count,) + weights.shape)], axis=1)

    def coarse_parts(v, outer):
        whole = lax.all_gather(v, ("dp", "seq"), axis=0).reshape((x_count, 2, seq_count) + v.shape)
        inner = whole[:, :, :, : v.shape[0] - outer].reshape(x_count, 2, seq_count, -1, rows, width)
        inner = inner.swapaxes(2, 3).reshape(x_count, 2, -1, width)
        whole = jnp.concatenate([inner, whole[:, :, :, v.shape[0] - outer :].reshape(x_count, 2, -1, width)], axis=2)
        out = []
        for e in range(2):
            mine = pick(whole, c_place ^ e, 1)
            out.append(jnp.concatenate([pick(mine, x_place ^ k) for k in range(x_count)])[None])
        return out

    def x_moves(kept, came):
        out = [(kept[0].astype(F32) + came[0]).astype(BF)]
        return out + [over_x((kept[k].astype(F32) + came[k]).astype(BF), k) for k in range(1, x_count)]

    def total(values):
        out = values[0].astype(F32)
        for v in values[1:]:
            out = out + v
        return out.astype(BF)

    def by_owner(v, outer):
        if fine:
            return v
        inner = v[0, : v.shape[1] - outer].reshape(-1, seq_count, rows, width).swapaxes(0, 1)
        inner = inner.reshape(seq_count, -1, width)
        return jnp.concatenate([inner, v[0, v.shape[1] - outer :].reshape(seq_count, -1, width)], axis=1)

    def y_parts(v):
        v = v.reshape((z_count, y_count) + v.shape[1:])
        return [over_y(pick(v, y_place ^ k, 1), k) for k in range(y_count)]

    def z_parts(v):
        return [over_z(pick(v, z_place ^ k), k) for k in range(z_count)]

    def untiled(v):
        return v.reshape(-1, rows, width).transpose(1, 0, 2).reshape(rows, -1)

    def home(v):
        v = v.astype(BF).reshape(2, held, half, width)
        mine, other = pick(v, c_place), over_core(pick(v, 1 - c_place))
        mine, other = mine[:, None], other[:, None]
        return by_core(mine, other, 1).reshape(held, local_rows, width).astype(F32)

    notes = jnp.concatenate([tgt_seg, src_len], axis=1)
    notes = pick(by_core(notes, over_core(notes)), z_place)
    target_all, lengths = notes[:length], notes[length:]
    docs = lengths.shape[0]
    upto = lax.broadcasted_iota(jnp.int32, (docs, docs), 0) <= lax.broadcasted_iota(jnp.int32, (docs, docs), 1)
    ends = jnp.sum(jnp.where(upto, lengths[:, None], 0), axis=0, dtype=jnp.int32)
    positions = jnp.arange(length, dtype=jnp.int32)
    source_all = jnp.sum((positions[:, None] >= ends[None, :]).astype(jnp.int32), axis=1, dtype=jnp.int32)
    qseg = pick(target_all.reshape(z_count, y_count * 2, half), y_place * 2 + c_place, 1)
    keys = 2 * half

    def in_order(segments):
        pairs = segments.reshape(-1, 2, half)
        return jnp.where(c_place == 0, pairs, pairs[:, ::-1]).reshape(-1, 1, keys)

    def visits(segments):
        low = jnp.sum((segments[None, :] < qseg[:, :1]).astype(jnp.int32), axis=1, dtype=jnp.int32)
        high = jnp.sum((segments[None, :] <= qseg[:, -1:]).astype(jnp.int32), axis=1, dtype=jnp.int32)
        table = jnp.stack([low // keys, (high + keys - 1) // keys])
        return jnp.pad(table, ((0, 0), (0, length // keys - z_count)))

    self_kseg, cross_kseg = in_order(target_all), in_order(source_all)
    self_visits, cross_visits = visits(target_all), visits(source_all)

    hidden = ffn_in.shape[1]
    outer = ffn_out.shape[0]
    norm_wide = jnp.pad(norm_params, ((0, 0), (0, width - norm_params.shape[1])))
    first_tiles = tiles_of(self_in)
    rest_tiles = tiles_of(jnp.concatenate([self_out, cross_q, cross_kv, cross_out, norm_wide, ffn_in], axis=1))
    rest_tiles = jnp.concatenate([rest_tiles, ffn_out], axis=0)
    mid = 6 * rows
    size = Size(
        half=half,
        length=length,
        own=z_count * half,
        z_count=z_count,
        x_count=x_count,
        pieces=pieces,
        tile_rows=tile_rows,
        hidden=hidden,
        feed_rows=hidden // width * tile_rows + outer * seq_count // pieces,
        first_one=(half,) if fine else (0,),
        first_two=(half,) if fine else (0,),
        first_three=(0,),
    )
    qseg = qseg[:, None, :]
    streams = jnp.stack([inputs, encoder, cotangent]).reshape(3, held, 2, half, width)
    mine = pick(streams, c_place, 2)
    other = over_core(pick(streams, 1 - c_place, 2))
    streams = by_core(mine, other, 1)
    x_blocks, source_blocks, cot = streams[0], streams[1], streams[2]
    if fine:
        x_blocks = with_weights(x_blocks, jnp.stack([over_x(first_tiles, k) for k in range(x_count)]))
        rest = jnp.stack([over_x(rest_tiles, k) for k in range(x_count)])
        source_blocks = with_weights(source_blocks, rest[:, :mid])
        cot = with_weights(cot, rest[:, mid:])
    x_near = exchange_z(x_blocks)
    x_near, source_blocks = together(x_near, source_blocks)
    x_moves_y = y_moves(x_near)
    source_near = exchange_z(source_blocks)
    x_near = y_order(x_moves_y)
    x_far = over_core(x_near)
    x_near, x_far, source_near, cot = together(x_near, x_far, source_near, cot)
    source_moves = y_moves(source_near)
    cot = exchange_z(cot)
    weights = (x_near, x_far) if fine else coarse_parts(first_tiles, 0)

    queries, pairs, whole_one, mixed_self, self_lse = first(
        size, self_visits, place, weights, x_near, x_far, qseg, self_kseg
    )
    whole_one = whole_one.reshape(3, width, width)
    mixed_self, cot, *source_moves = together(mixed_self, cot, *source_moves)
    source_near = y_order(source_moves)
    source_far = over_core(source_near)
    if fine:
        w3_moves = y_moves(cot[:, half:])
        weights = (source_near, source_far)
    else:
        weights = coarse_parts(rest_tiles[:mid], 0)
    queries_c, pairs_c, whole_two, hat_one, inv_one, norms, mixed_cross, cross_lse = second(
        size, cross_visits, place, weights, x_near, source_near, source_far, mixed_self, qseg, cross_kseg
    )
    whole_two = whole_two.reshape(6, width, width)
    if fine:
        mixed_cross, *w3_moves = together(mixed_cross, *w3_moves)
        w3 = y_order(w3_moves)
        weights = (w3, over_core(w3))
    else:
        weights = coarse_parts(rest_tiles[mid:], outer)
    out_low, d_two, d_mixed_c, sums, low_t, dz, hid, down, mixed_ct = feed(
        size, place, weights, mixed_cross, whole_two, hat_one, norms, cot
    )

    f_send = feed_grads(size, 1, place, low_t, dz, hid, down, mixed_ct, d_two)
    f_came = over_core(f_send)
    low_t, f_send, out_low = together(low_t, f_send, out_low)
    f_kept = feed_grads(size, 0, place, low_t, dz, hid, down, mixed_ct, d_two)
    out_parts = exchange_z(out_low.reshape(z_count, half, width))
    d_mixed_c, f_kept, f_came = together(d_mixed_c, f_kept, f_came)
    f_moves = x_moves(f_kept, f_came)
    d_mixed_c, f_first = together(d_mixed_c, f_moves[0])
    s_kept, s_send, c_kept, c_send, d_one, d_mixed = third(
        size,
        cross_visits,
        place,
        queries_c,
        d_mixed_c,
        mixed_cross,
        cross_lse,
        pairs_c,
        qseg,
        cross_kseg,
        source_near,
        source_far,
        whole_two,
        hat_one,
        inv_one,
        norms,
        d_two,
        sums,
        mixed_self,
    )
    s_kept, s_send, c_kept, c_send, d_one, d_mixed, out_parts, f_first, *f_moves = together(
        s_kept, s_send, c_kept, c_send, d_one, d_mixed, out_parts, f_first, *f_moves[1:]
    )
    s_came, c_came = over_core(s_send), over_core(c_send)
    f_sum = by_owner(total([f_first, *f_moves]), hidden // dp_count)
    f_sum, s_came, c_came = together(f_sum, s_came, c_came)
    s_sum = total([s_kept, s_came]).reshape(seq_count, half, width)
    fs_moves = y_parts(jnp.concatenate([f_sum, s_sum], axis=1))
    c_moves = x_moves(c_kept, c_came)
    d_mixed, fs_first, c_first = together(d_mixed, fs_moves[0], c_moves[0])
    x_kept, x_send, i_kept, i_send = fourth(
        size,
        self_visits,
        place,
        queries,
        d_mixed,
        mixed_self,
        self_lse,
        pairs,
        qseg,
        self_kseg,
        whole_one,
        d_one,
        x_near,
        x_far,
    )
    extra = len(fs_moves) - 1
    x_kept, x_send, i_kept, i_send, fs_first, c_first, out_parts, *moves = together(
        x_kept, x_send, i_kept, i_send, fs_first, c_first, out_parts, *fs_moves[1:], *c_moves[1:]
    )
    x_came, i_came = over_core(x_send), over_core(i_send)
    fs_parts = z_parts(total([fs_first, *moves[:extra]]))
    x_came, i_came, fs_first = together(x_came, i_came, fs_parts[0])
    x_moves_y = y_parts(total([x_kept, x_came]).reshape(seq_count, half, width))
    x_first, i_came, i_kept = together(x_moves_y[0], i_came, i_kept)
    i_moves = x_moves(i_kept, i_came)
    c_sum = by_owner(total([c_first, *moves[extra:]]), 0)
    i_first, c_sum, *x_moves_y = together(i_moves[0], c_sum, x_first, *x_moves_y[1:])
    x_parts = exchange_z(total(x_moves_y))
    i_sum = by_owner(total([i_first, *i_moves[1:]]), 0)
    w_moves = y_parts(jnp.concatenate([c_sum, i_sum], axis=1))
    w_first, out_parts, fs_first, *fs_parts = together(w_moves[0], out_parts, fs_first, *fs_parts[1:])
    fs_parts = [fs_first] + fs_parts
    grad_source = home(unxor([v[-half:] for v in fs_parts], z_place))
    out_tokens = home(out_parts)
    f_own = sum((v[:-half].astype(F32) for v in fs_parts[1:]), fs_parts[0][:-half].astype(F32))
    w_parts = z_parts(total([w_first, *w_moves[1:]]))
    w_first, x_parts = together(w_parts[0], x_parts)
    w_own = sum(w_parts[1:], w_first.astype(F32))
    c_own, i_own = w_own[: 5 * rows], w_own[5 * rows :]
    grad_tokens = home(x_parts)
    f_in = hidden // width * rows
    c_own = c_own.reshape(5, rows, width)
    return (
        out_tokens,
        grad_tokens,
        grad_source,
        untiled(i_own),
        c_own[0],
        c_own[1],
        untiled(c_own[2:4]),
        f_own[f_in : f_in + rows],
        untiled(f_own[:f_in]),
        f_own[f_in + rows :],
        c_own[4][:, : norm_params.shape[1]],
    )


def solution(mesh):
    tokens, rows = P("dp", "seq", None), P(("dp", "seq"), None)
    return jax.shard_map(
        body,
        mesh=mesh,
        in_specs=(tokens, tokens, P("dp", None), P("dp", None), tokens) + (rows,) * 8,
        out_specs=(tokens,) * 3 + (rows,) * 8,
        check_vma=False,
    )
```

```python
import dataclasses
import functools
import math

import jax
import jax.numpy as jnp
from jax import lax
from jax.experimental import pallas as pl
from jax.experimental.pallas import tpu as pltpu
from jax.sharding import PartitionSpec as P

HEAD_DIM = 64
GROUP = 4
LANES = GROUP * HEAD_DIM
PACE = 1.15e9 * 0.1
WIDE = 60
CHUNK = 256
LOG2E = 1.4426950408889634
LN2 = 0.6931471805599453
GELU_A = 0.7978845608028654
GELU_B = 0.044715
BF = jnp.bfloat16
F32 = jnp.float32
SMEM = pl.BlockSpec(memory_space=pltpu.SMEM)
VMEM = pl.BlockSpec(memory_space=pltpu.VMEM)
ANY = pl.BlockSpec(memory_space=pl.ANY)
NOW, LATER = "now", "later"


def dot_f32(left, right):
    return jnp.dot(left, right, preferred_element_type=F32)


def dot_nt(left, right):
    return lax.dot_general(left, right, (((1,), (1,)), ((), ())), preferred_element_type=F32)


def padded_bytes(dims, dtype):
    dims = (1,) * (2 - len(dims)) + tuple(dims)
    lead = math.prod(dims[:-2])
    return lead * (-(-dims[-2] // 16) * 16) * (-(-dims[-1] // 128) * 128) * jnp.dtype(dtype).itemsize


def kernel_call(kernel, *, out_shape, in_specs, out_specs, scratch_shapes=(), spare=3, us=2):
    def call(*operands):
        need = spare * 2**20
        for operand, spec in zip(operands, in_specs):
            need += padded_bytes(operand.shape, operand.dtype) if spec is VMEM else 0
        for result in jax.tree.leaves(out_shape):
            need += padded_bytes(result.shape, result.dtype)
        for scratch in scratch_shapes:
            if getattr(scratch, "memory_space", None) == pltpu.VMEM:
                need += padded_bytes(scratch.shape, scratch.dtype)
        return pl.pallas_call(
            kernel,
            out_shape=out_shape,
            in_specs=in_specs,
            out_specs=out_specs,
            scratch_shapes=scratch_shapes,
            compiler_params=pltpu.CompilerParams(vmem_limit_bytes=need),
            cost_estimate=pl.CostEstimate(flops=int(us * PACE), bytes_accessed=2**10, transcendentals=0),
        )(*operands)

    return call


class Moves:
    def __init__(self, now, late, out):
        self.now, self.late, self.out, self.begun = now, late, out, set()

    def begin(self):
        for copy in self.now:
            copy.wait()

    def ready(self):
        for copy in self.late:
            copy.wait()

    def done(self, *results):
        for i in results:
            self.out[i].start()
            self.begun.add(i)

    def finish(self):
        self.done(*(i for i in range(len(self.out)) if i not in self.begun))
        for copy in self.out:
            copy.wait()


def run_kernel(kernel, *, out_shape, kinds, scratch_shapes=(), us=2):
    def call(*operands):
        moved = [i for i, kind in enumerate(kinds) if kind in (NOW, LATER)]
        count, outs, own = len(kinds), len(out_shape), len(scratch_shapes)

        def wrapped(*refs):
            ins, results, scratch = list(refs[:count]), refs[count : count + outs], refs[count + outs :]
            mine, scratch = scratch[:own], scratch[own:]
            slots, scratch = scratch[: len(moved)], scratch[len(moved) :]
            made, (in_sem, out_sem) = scratch[:outs], scratch[outs:]
            now, late = [], []
            for n, i in enumerate(moved):
                copy = pltpu.make_async_copy(ins[i], slots[n], in_sem.at[n])
                copy.start()
                (now if kinds[i] == NOW else late).append(copy)
                ins[i] = slots[n]
            moves = Moves(now, late, [pltpu.make_async_copy(a, b, out_sem.at[n]) for n, (a, b) in enumerate(zip(made, results))])
            kernel(*ins, *made, *mine, moves=moves)
            moves.finish()

        return pl.pallas_call(
            wrapped,
            out_shape=out_shape,
            in_specs=[SMEM if kind is SMEM else ANY for kind in kinds],
            out_specs=(ANY,) * outs,
            scratch_shapes=list(scratch_shapes)
            + [pltpu.VMEM(operands[i].shape, operands[i].dtype) for i in moved]
            + [pltpu.VMEM(v.shape, v.dtype) for v in out_shape]
            + [pltpu.SemaphoreType.DMA((len(moved),)), pltpu.SemaphoreType.DMA((outs,))],
            compiler_params=pltpu.CompilerParams(vmem_limit_bytes=WIDE * 2**20),
            cost_estimate=pl.CostEstimate(flops=int(us * PACE), bytes_accessed=2**10, transcendentals=0),
        )(*operands)

    return call


def shape(dims, dtype=BF):
    return jax.ShapeDtypeStruct(dims, dtype)


def chunk(i):
    return pl.ds(pl.multiple_of(i * CHUNK, CHUNK), CHUNK)


@dataclasses.dataclass(frozen=True)
class Size:
    half: int
    length: int
    own: int
    z_count: int
    x_count: int
    pieces: int
    tile_rows: int
    hidden: int
    feed_rows: int
    first_one: tuple
    first_two: tuple
    first_three: tuple


def stack_heads(tile):
    head = lax.broadcasted_iota(jnp.int32, tile.shape, 1) // HEAD_DIM
    zero = jnp.zeros_like(tile)
    return jnp.concatenate([jnp.where(head == h, tile, zero) for h in range(GROUP)], axis=0)


def row_of(column):
    return jnp.transpose(jnp.broadcast_to(column, (column.shape[0], 128)))[0:1, :]


def key_rows(b, keys, total):
    half = keys // 2
    at = pl.multiple_of(b * half, half)
    return pl.ds(at, half), pl.ds(pl.multiple_of(at + total // 2, half), half)


def both_rows(ref, spots, cols):
    return jnp.concatenate([ref[spot, cols] for spot in spots], axis=0)


def turn_segments(kseg_ref, seg_ref):
    count, _, keys = kseg_ref.shape
    for b in range(count):
        row = kseg_ref[b].astype(F32)
        seg_ref[b * keys : (b + 1) * keys, :] = jnp.transpose(jnp.broadcast_to(row, (128, keys)))[:, :1]


def attend_part(visit_ref, q_ref, kv_ref, qseg_ref, seg_ref, o_ref, lse_ref, acc_ref, qst_ref):
    width = q_ref.shape[1]
    blocks = qseg_ref.shape[0]
    rows = q_ref.shape[0] // blocks
    total = kv_ref.shape[0]
    keys = total // visit_ref.shape[1]
    groups = width // LANES

    def block(k, carry):
        lo, hi = visit_ref[0, k], visit_ref[1, k]
        q_rows = pl.ds(pl.multiple_of(k * rows, rows), rows)
        qseg = jnp.concatenate([qseg_ref[k].astype(F32)] * GROUP, axis=1)
        for g in range(groups):
            qst_ref[g] = stack_heads(q_ref[q_rows, g * LANES : (g + 1) * LANES])
        acc_ref[...] = jnp.zeros(acc_ref.shape, F32)

        def step(b, carry):
            spots = key_rows(b, keys, total)
            same = seg_ref[pl.ds(pl.multiple_of(b * keys, keys), keys), :] == qseg
            scores = [
                dot_nt(both_rows(kv_ref, spots, slice(g * LANES, (g + 1) * LANES)), qst_ref[g]) for g in range(groups)
            ]
            out, lows, fades = [], [], []
            for g in range(groups):
                top, tot = carry[g]
                masked = jnp.where(same, scores[g], -1e30)
                new = jnp.maximum(top, jnp.max(masked, axis=0, keepdims=True))
                soft = jnp.exp2(masked - new)
                fade = jnp.exp2(top - new)
                out.append((new, tot * fade + jnp.sum(soft, axis=0, keepdims=True)))
                lows.append(soft.astype(BF))
                fades.append(fade)
            for g in range(groups):
                turned = jnp.transpose(both_rows(kv_ref, spots, slice(width + g * LANES, width + (g + 1) * LANES)))
                for h in range(GROUP):
                    at = g * LANES + h * HEAD_DIM
                    cols = slice(h * rows, (h + 1) * rows)
                    values = turned[h * HEAD_DIM : (h + 1) * HEAD_DIM]
                    acc_ref[at : at + HEAD_DIM] = acc_ref[at : at + HEAD_DIM] * fades[g][:, cols] + dot_f32(
                        values, lows[g][:, cols]
                    )
            return tuple(out)

        start = (jnp.full((1, GROUP * rows), -3e38, F32), jnp.zeros((1, GROUP * rows), F32))
        end = lax.fori_loop(lo, hi, step, (start,) * groups)
        for g in range(groups):
            top, tot = end[g]
            inv = 1.0 / tot
            mixed = [
                acc_ref[g * LANES + h * HEAD_DIM : g * LANES + (h + 1) * HEAD_DIM] * inv[:, h * rows : (h + 1) * rows]
                for h in range(GROUP)
            ]
            o_ref[q_rows, g * LANES : (g + 1) * LANES] = jnp.transpose(jnp.concatenate(mixed, axis=0)).astype(BF)
            lse_ref[k * groups + g] = top + jnp.log2(tot)
        return carry

    lax.fori_loop(0, blocks, block, 0)


def attend_back_part(
    visit_ref,
    q_ref,
    do_ref,
    o_ref,
    lse_ref,
    kv_ref,
    qseg_ref,
    seg_ref,
    dq_ref,
    dkv_ref,
    sum_ref,
    dqt_ref,
    qst_ref,
    dst_ref,
    delta_ref,
):
    width = q_ref.shape[1]
    blocks = qseg_ref.shape[0]
    rows = q_ref.shape[0] // blocks
    total = kv_ref.shape[0]
    keys = total // visit_ref.shape[1]
    groups = width // LANES
    def block(k, carry):
        lo, hi = visit_ref[0, k], visit_ref[1, k]
        q_rows = pl.ds(pl.multiple_of(k * rows, rows), rows)
        qseg = jnp.concatenate([qseg_ref[k].astype(F32)] * GROUP, axis=1)
        for g in range(groups):
            cols = slice(g * LANES, (g + 1) * LANES)
            qst_ref[g] = stack_heads(q_ref[q_rows, cols])
            d_mixed = do_ref[q_rows, cols]
            dst_ref[g] = stack_heads(d_mixed)
            prod = d_mixed.astype(F32) * o_ref[q_rows, cols].astype(F32)
            delta_ref[g] = row_of(jnp.sum(stack_heads(prod), axis=1, keepdims=True))
        dqt_ref[...] = jnp.zeros(dqt_ref.shape, F32)

        def step(b, carry):
            spots = key_rows(b, keys, total)
            same = seg_ref[pl.ds(pl.multiple_of(b * keys, keys), keys), :] == qseg
            k_cols = [slice(g * LANES, (g + 1) * LANES) for g in range(groups)]
            v_cols = [slice(width + g * LANES, width + (g + 1) * LANES) for g in range(groups)]
            scores = [dot_nt(both_rows(kv_ref, spots, k_cols[g]), qst_ref[g]) for g in range(groups)]
            d_soft = [dot_nt(both_rows(kv_ref, spots, v_cols[g]), dst_ref[g]) for g in range(groups)]
            softs, d_scores = [], []
            for g in range(groups):
                soft = jnp.where(same, jnp.exp2(scores[g] - lse_ref[k * groups + g]), 0.0)
                d_scores.append((soft * (d_soft[g] - delta_ref[g])).astype(BF))
                softs.append(soft.astype(BF))
            for g in range(groups):
                d_keys, d_values = dot_f32(d_scores[g], qst_ref[g]), dot_f32(softs[g], dst_ref[g])
                for e, spot in enumerate(spots):
                    part = slice(e * keys // 2, (e + 1) * keys // 2)
                    sum_ref[spot, k_cols[g]] += d_keys[part]
                    sum_ref[spot, v_cols[g]] += d_values[part]
                turned = jnp.transpose(both_rows(kv_ref, spots, k_cols[g]))
                for h in range(GROUP):
                    at = slice(g * LANES + h * HEAD_DIM, g * LANES + (h + 1) * HEAD_DIM)
                    keys_t = turned[h * HEAD_DIM : (h + 1) * HEAD_DIM]
                    dqt_ref[at] += dot_f32(keys_t, d_scores[g][:, h * rows : (h + 1) * rows])
            return carry

        lax.fori_loop(lo, hi, step, 0)
        for g in range(groups):
            cols = slice(g * LANES, (g + 1) * LANES)
            dq_ref[q_rows, cols] = (jnp.transpose(dqt_ref[cols]) * HEAD_DIM**-0.5).astype(BF)
        return carry

    lax.fori_loop(0, blocks, block, 0)
    dkv_ref[:, :width] = (sum_ref[:, :width] * LN2).astype(BF)
    dkv_ref[:, width:] = sum_ref[:, width:].astype(BF)


def norm_of(resid):
    centered = resid - jnp.mean(resid, axis=-1, keepdims=True)
    inv = lax.rsqrt(jnp.mean(centered * centered, axis=-1, keepdims=True) + 1e-05)
    return centered * inv, inv


def norm_pull(upstream, hat, inv, gain):
    scaled = upstream * gain
    return inv * (
        scaled - jnp.mean(scaled, axis=-1, keepdims=True) - hat * jnp.mean(scaled * hat, axis=-1, keepdims=True)
    )


def weight_rows(size, weights, total, firsts):
    out = []
    per = len(weights) // 2
    for e in range(2):
        for k in range(size.x_count):
            a = min(k, per - 1)
            out.append((k, e, weights[e * per + a], firsts[a] + (k - a) * total))
    return out


def fetch_tiles(size, place_ref, weights, tiles, firsts, whole_ref, sem):
    copies = []
    rows = size.tile_rows
    for k, e, part, start in weight_rows(size, weights, tiles * rows, firsts):
        pieces = part.shape[0]
        dp = (place_ref[0] ^ k) * 2 + (place_ref[1] ^ e)
        at = pl.ds(pl.multiple_of(dp * pieces, pieces), pieces)
        for t in range(tiles):
            source = part.at[:, pl.ds(start + t * rows, rows)]
            copies.append(pltpu.make_async_copy(source, whole_ref.at[t, at], sem.at[len(copies)]))
    for copy in copies:
        copy.start()
    return copies


def tile_of(ref, t):
    tile = ref[t]
    return tile.reshape(-1, tile.shape[-1])


def own_tokens(near_ref, place_ref, half, z_count):
    y_count = near_ref.shape[0] // z_count
    return jnp.concatenate([near_ref[z * y_count + place_ref[3], :half, :] for z in range(z_count)], axis=0)


def sequence_rows(ref, i, half):
    count = CHUNK // half
    return jnp.concatenate([ref[i * count + j, :half, :] for j in range(count)], axis=0)


def put_pairs(near_ref, far_ref, half, w_k, w_v, kv_ref):
    width = w_k.shape[1]
    count = near_ref.shape[0] * half // CHUNK
    for e, ref in enumerate((near_ref, far_ref)):

        def step(i, carry):
            rows = sequence_rows(ref, i, half)
            at = chunk(i + e * count)
            kv_ref[at, :width] = dot_f32(rows, w_k).astype(BF)
            kv_ref[at, width:] = dot_f32(rows, w_v).astype(BF)
            return carry

        lax.fori_loop(0, count, step, 0)


def grad_rows(place_ref, left_ref, dp_count, e):
    rows = left_ref.shape[0] // dp_count
    out = []
    for k in range(dp_count // 2):
        dp = (place_ref[0] ^ k) * 2 + (place_ref[1] ^ e)
        out.append(left_ref[pl.ds(pl.multiple_of(dp * rows, rows), rows), :])
    return jnp.concatenate(out, axis=0)


def put_grad(target, value, tile, tile_rows):
    x_count, pieces, _, width = target.shape
    rows = value.shape[0] // x_count
    for k in range(x_count):
        part = value[k * rows : (k + 1) * rows].astype(target.dtype)
        target[k, :, tile * tile_rows : (tile + 1) * tile_rows, :] = part.reshape(pieces, tile_rows, width)


def attend_scratch(size, width):
    rows = size.own // size.z_count
    return [
        pltpu.VMEM((size.length, 1), F32),
        pltpu.VMEM((width, rows), F32),
        pltpu.VMEM((width // LANES, GROUP * rows, LANES), BF),
    ]


def first_kernel(
    size,
    visit_ref,
    place_ref,
    near_ref,
    far_ref,
    qseg_ref,
    kseg_ref,
    *refs,
    moves,
):
    weights, (q_ref, kv_ref, whole_ref, o_ref, lse_ref, seg_ref, acc_ref, qst_ref, sem) = refs[:-9], refs[-9:]
    copies = fetch_tiles(size, place_ref, weights, 3, size.first_one, whole_ref, sem)
    moves.begin()
    own = own_tokens(near_ref, place_ref, size.half, size.z_count)
    turn_segments(kseg_ref, seg_ref)
    for copy in copies:
        copy.wait()
    q_ref[...] = (dot_f32(own, tile_of(whole_ref, 0)) * (HEAD_DIM**-0.5 * LOG2E)).astype(BF)
    put_pairs(near_ref, far_ref, size.half, tile_of(whole_ref, 1), tile_of(whole_ref, 2), kv_ref)
    moves.done(0, 1, 2)
    attend_part(visit_ref, q_ref, kv_ref, qseg_ref, seg_ref, o_ref, lse_ref, acc_ref, qst_ref)


def lse_shape(size, width):
    return shape((size.z_count * width // LANES, 1, GROUP * size.half), F32)


def first(size, visits, place, weights, near, far, qseg, kseg):
    width = near.shape[2]
    return run_kernel(
        functools.partial(first_kernel, size),
        us=16,
        out_shape=(
            shape((size.own, width)),
            shape((size.length, 2 * width)),
            shape((3, 2 * size.x_count * size.pieces, size.tile_rows, width)),
            shape((size.own, width)),
            lse_shape(size, width),
        ),
        kinds=[SMEM] * 2 + [NOW] * 4 + [ANY] * len(weights),
        scratch_shapes=attend_scratch(size, width) + [pltpu.SemaphoreType.DMA((2 * size.x_count * 3,))],
    )(visits, place, near, far, qseg, kseg, *weights)


def second_kernel(
    size,
    visit_ref,
    place_ref,
    near_ref,
    source_near_ref,
    source_far_ref,
    mixed_ref,
    qseg_ref,
    kseg_ref,
    *refs,
    moves,
):
    weights = refs[:-12]
    q_ref, kv_ref, whole_ref, hat_ref, inv_ref, norm_ref, o_ref, lse_ref, seg_ref, acc_ref, qst_ref, sem = refs[-12:]
    copies = fetch_tiles(size, place_ref, weights, 6, size.first_two, whole_ref, sem)
    moves.begin()
    own = own_tokens(near_ref, place_ref, size.half, size.z_count)
    turn_segments(kseg_ref, seg_ref)
    for copy in copies:
        copy.wait()
    norm_ref[...] = jnp.transpose(tile_of(whole_ref, 5)[:, :128].astype(F32))[: norm_ref.shape[0]]
    hat, inv = norm_of(own.astype(F32) + dot_f32(mixed_ref[...], tile_of(whole_ref, 0)))
    hat_ref[...] = hat
    inv_ref[...] = inv
    low = (hat * norm_ref[0:1, :] + norm_ref[1:2, :]).astype(BF)
    q_ref[...] = (dot_f32(low, tile_of(whole_ref, 1)) * (HEAD_DIM**-0.5 * LOG2E)).astype(BF)
    moves.ready()
    put_pairs(source_near_ref, source_far_ref, size.half, tile_of(whole_ref, 2), tile_of(whole_ref, 3), kv_ref)
    moves.done(0, 1, 2, 3, 4, 5)
    attend_part(visit_ref, q_ref, kv_ref, qseg_ref, seg_ref, o_ref, lse_ref, acc_ref, qst_ref)


def second(size, visits, place, weights, near, source_near, source_far, mixed, qseg, kseg):
    width = near.shape[2]
    return run_kernel(
        functools.partial(second_kernel, size),
        us=17,
        out_shape=(
            shape((size.own, width)),
            shape((size.length, 2 * width)),
            shape((6, 2 * size.x_count * size.pieces, size.tile_rows, width)),
            shape((size.own, width), F32),
            shape((size.own, 1), F32),
            shape((8, width), F32),
            shape((size.own, width)),
            lse_shape(size, width),
        ),
        kinds=[SMEM] * 2 + [NOW, LATER, LATER, NOW, NOW, NOW] + [ANY] * len(weights),
        scratch_shapes=attend_scratch(size, width) + [pltpu.SemaphoreType.DMA((2 * size.x_count * 6,))],
    )(visits, place, near, source_near, source_far, mixed, qseg, kseg, *weights)


def feed_kernel(
    size,
    place_ref,
    mixed_ref,
    whole_two_ref,
    hat_one_ref,
    norm_ref,
    cot_ref,
    *refs,
):
    weights = refs[:-16]
    (
        out_ref,
        d_two_ref,
        d_mixed_ref,
        sums_ref,
        low_t_ref,
        dz_ref,
        hid_ref,
        down_ref,
        mixed_t_ref,
        w_in_ref,
        w_out_ref,
        z_ref,
        low_ref,
        hat_two_ref,
        inv_two_ref,
        sem,
    ) = refs[-16:]
    own, width = hat_one_ref.shape
    hidden = z_ref.shape[1]
    tiles = hidden // width
    tile_rows = size.tile_rows
    copies = []
    total = size.feed_rows
    for k, e, part, start in weight_rows(size, weights, total, size.first_three):
        pieces = part.shape[0]
        dp = (place_ref[0] ^ k) * 2 + (place_ref[1] ^ e)
        at = pl.ds(pl.multiple_of(dp * pieces, pieces), pieces)
        for t in range(tiles):
            source = part.at[:, pl.ds(start + t * tile_rows, tile_rows)]
            copies.append(pltpu.make_async_copy(source, w_in_ref.at[t, at], sem.at[len(copies)]))
        source = part.at[:, pl.ds(start + tiles * tile_rows, total - tiles * tile_rows)]
        copies.append(pltpu.make_async_copy(source, w_out_ref.at[at], sem.at[len(copies)]))
    for copy in copies:
        copy.start()
    mixed_t_ref[...] = jnp.transpose(mixed_ref[...])
    sums_ref[...] = jnp.zeros(sums_ref.shape, F32)
    cross_out = whole_two_ref[4]
    for copy in copies:
        copy.wait()
    per_tile = w_out_ref.shape[0] // tiles

    def w_down(t):
        return w_out_ref[t * per_tile : (t + 1) * per_tile].reshape(width, width)

    def forward(i, carry):
        at = chunk(i)
        one = hat_one_ref[at, :] * norm_ref[0:1, :] + norm_ref[1:2, :]
        hat, inv = norm_of(one + dot_f32(mixed_ref[at, :], cross_out))
        hat_two_ref[at, :] = hat
        inv_two_ref[at, :] = inv
        two = hat * norm_ref[2:3, :] + norm_ref[3:4, :]
        low = two.astype(BF)
        low_ref[at, :] = low
        total = two
        for t in range(tiles):
            cols = slice(t * width, (t + 1) * width)
            z = dot_f32(low, tile_of(w_in_ref, t))
            z_ref[at, cols] = z
            turn = jnp.tanh(GELU_A * (z + GELU_B * (z * z * z)))
            hid = (0.5 * z * (1.0 + turn)).astype(BF)
            hid_ref[at, cols] = hid
            total = total + dot_f32(hid, w_down(t))
        hat, inv = norm_of(total)
        gain = norm_ref[4:5, :]
        out_ref[at, :] = (hat * gain + norm_ref[5:6, :]).astype(BF)
        upstream = sequence_rows(cot_ref, i, size.half).astype(F32)
        sums_ref[4:5, :] += jnp.sum(upstream * hat, axis=0, keepdims=True)
        sums_ref[5:6, :] += jnp.sum(upstream, axis=0, keepdims=True)
        down = norm_pull(upstream, hat, inv, gain)
        low_down = down.astype(BF)
        down_ref[at, :] = low_down
        back = down
        for t in range(tiles):
            cols = slice(t * width, (t + 1) * width)
            d_hid = dot_nt(low_down, w_down(t))
            z = z_ref[at, cols]
            turn = jnp.tanh(GELU_A * (z + GELU_B * (z * z * z)))
            slope = 0.5 * (1.0 + turn) + (0.5 * GELU_A) * z * (1.0 - turn * turn) * (1.0 + (3.0 * GELU_B) * z * z)
            dz = (d_hid * slope).astype(BF)
            dz_ref[at, cols] = dz
            back = back + dot_nt(dz, tile_of(w_in_ref, t))
        hat, inv = hat_two_ref[at, :], inv_two_ref[at, :]
        sums_ref[2:3, :] += jnp.sum(back * hat, axis=0, keepdims=True)
        sums_ref[3:4, :] += jnp.sum(back, axis=0, keepdims=True)
        d_two = norm_pull(back, hat, inv, norm_ref[2:3, :])
        d_two_ref[at, :] = d_two
        d_mixed_ref[at, :] = dot_nt(d_two.astype(BF), cross_out).astype(BF)
        return carry

    lax.fori_loop(0, own // CHUNK, forward, 0)
    low_t_ref[...] = jnp.transpose(low_ref[...])


def feed(size, place, weights, mixed, whole_two, hat_one, norms, cot):
    own, width = hat_one.shape
    hidden = size.hidden
    devices = 2 * size.x_count * size.pieces
    return kernel_call(
        functools.partial(feed_kernel, size),
        us=12,
        out_shape=(
            shape((own, width)),
            shape((own, width), F32),
            shape((own, width)),
            shape((8, width), F32),
            shape((width, own)),
            shape((own, hidden)),
            shape((own, hidden)),
            shape((own, width)),
            shape((width, own)),
        ),
        in_specs=[SMEM] + [VMEM] * 5 + [ANY] * len(weights),
        out_specs=(VMEM,) * 9,
        scratch_shapes=[
            pltpu.VMEM((hidden // width, devices, size.tile_rows, width), BF),
            pltpu.VMEM((devices, hidden // devices, width), BF),
            pltpu.VMEM((own, hidden), F32),
            pltpu.VMEM((own, width), BF),
            pltpu.VMEM((own, width), F32),
            pltpu.VMEM((own, 1), F32),
            pltpu.SemaphoreType.DMA((2 * size.x_count * (hidden // width + 1),)),
        ],
    )(place, mixed, whole_two, hat_one, norms, cot, *weights)


def feed_grads_kernel(
    size, e, place_ref, low_t_ref, dz_ref, hid_ref, down_ref, mixed_t_ref, d_two_ref, target
):
    width = low_t_ref.shape[0]
    hidden = dz_ref.shape[1]
    tiles = hidden // width
    lefts = grad_rows(place_ref, low_t_ref, 2 * size.x_count, e)
    for t in range(tiles):
        put_grad(target, dot_f32(lefts, dz_ref[:, t * width : (t + 1) * width]), t, size.tile_rows)
    value = dot_f32(grad_rows(place_ref, mixed_t_ref, 2 * size.x_count, e), d_two_ref[...].astype(BF))
    put_grad(target, value, tiles, size.tile_rows)
    rows = hidden // (2 * size.x_count)
    for k in range(size.x_count):
        dp = (place_ref[0] ^ k) * 2 + (place_ref[1] ^ e)
        cols = pl.ds(pl.multiple_of(dp * rows, rows), rows)
        value = dot_f32(jnp.transpose(hid_ref[:, cols]), down_ref[...]).astype(target.dtype)
        target[k, :, (tiles + 1) * size.tile_rows :, :] = value.reshape(size.pieces, rows // size.pieces, width)


def feed_grads(size, e, place, low_t, dz, hid, down, mixed_t, d_two):
    width = low_t.shape[0]
    tiles = size.hidden // width
    rows = (tiles + 1) * size.tile_rows + size.hidden // (2 * size.x_count * size.pieces)
    return kernel_call(
        functools.partial(feed_grads_kernel, size, e),
        out_shape=shape((size.x_count, size.pieces, rows, width)),
        in_specs=[SMEM] + [VMEM] * 6,
        out_specs=VMEM,
    )(place, low_t, dz, hid, down, mixed_t, d_two)


def back_pairs(size, d_kv_ref, w_k, w_v, kept_ref, send_ref):
    width = w_k.shape[1]
    count = size.length // (2 * CHUNK)
    for e, target in enumerate((kept_ref, send_ref)):

        def step(i, carry):
            at = chunk(i + e * count)
            value = dot_nt(d_kv_ref[at, :width], w_k) + dot_nt(d_kv_ref[at, width:], w_v)
            target[chunk(i), :] = value.astype(target.dtype)
            return carry

        lax.fori_loop(0, count, step, 0)


def turn_rows(size, near_ref, far_ref, left_ref):
    count = size.length // (2 * CHUNK)
    for e, ref in enumerate((near_ref, far_ref)):

        def step(i, carry):
            left_ref[:, chunk(i + e * count)] = jnp.transpose(sequence_rows(ref, i, size.half))
            return carry

        lax.fori_loop(0, count, step, 0)


def back_scratch(size, width):
    rows = size.own // size.z_count
    return [
        pltpu.VMEM((size.length, 1), F32),
        pltpu.VMEM((size.length, 2 * width), F32),
        pltpu.VMEM((width, rows), F32),
        pltpu.VMEM((width // LANES, GROUP * rows, LANES), BF),
        pltpu.VMEM((width // LANES, GROUP * rows, LANES), BF),
        pltpu.VMEM((width // LANES, 1, GROUP * rows), F32),
    ]


def third_kernel(
    size,
    visit_ref,
    place_ref,
    q_ref,
    do_ref,
    o_ref,
    lse_ref,
    kv_ref,
    qseg_ref,
    kseg_ref,
    near_ref,
    far_ref,
    whole_ref,
    hat_ref,
    inv_ref,
    norm_ref,
    d_two_ref,
    sums_in_ref,
    mixed_self_ref,
    kept_rows_ref,
    send_rows_ref,
    kept_ref,
    send_ref,
    d_one_ref,
    d_mixed_ref,
    seg_ref,
    sum_ref,
    dqt_ref,
    qst_ref,
    dst_ref,
    delta_ref,
    d_q_ref,
    d_kv_ref,
    left_ref,
    self_t_ref,
    low_t_ref,
    cols_ref,
    moves,
):
    width = hat_ref.shape[1]
    dp_count = 2 * size.x_count
    sum_ref[...] = jnp.zeros(sum_ref.shape, F32)
    moves.begin()
    turn_segments(kseg_ref, seg_ref)
    attend_back_part(
        visit_ref,
        q_ref,
        do_ref,
        o_ref,
        lse_ref,
        kv_ref,
        qseg_ref,
        seg_ref,
        d_q_ref,
        d_kv_ref,
        sum_ref,
        dqt_ref,
        qst_ref,
        dst_ref,
        delta_ref,
    )
    moves.ready()
    hat, inv, gain = hat_ref[...], inv_ref[...], norm_ref[0:1, :]
    upstream = d_two_ref[...] + dot_nt(d_q_ref[...], whole_ref[1])
    gain_sum = jnp.sum(upstream * hat, axis=0, keepdims=True)
    shift_sum = jnp.sum(upstream, axis=0, keepdims=True)
    d_one = norm_pull(upstream, hat, inv, gain)
    d_one_ref[...] = d_one
    low_one = d_one.astype(BF)
    d_mixed_ref[...] = dot_nt(low_one, whole_ref[0]).astype(BF)
    low_t_ref[...] = jnp.transpose((hat * gain + norm_ref[1:2, :]).astype(BF))
    back_pairs(size, d_kv_ref, whole_ref[2], whole_ref[3], kept_rows_ref, send_rows_ref)
    moves.done(0, 1, 4, 5)
    self_t_ref[...] = jnp.transpose(mixed_self_ref[...])
    pad = jnp.zeros((128 - sums_in_ref.shape[0], width), F32)
    cols_ref[...] = jnp.zeros(cols_ref.shape, F32)
    cols_ref[:, :128] = jnp.transpose(jnp.concatenate([gain_sum, shift_sum, sums_in_ref[2:, :], pad], axis=0))
    turn_rows(size, near_ref, far_ref, left_ref)
    for e, target in enumerate((kept_ref, send_ref)):
        put_grad(target, dot_f32(grad_rows(place_ref, self_t_ref, dp_count, e), low_one), 0, size.tile_rows)
        put_grad(target, dot_f32(grad_rows(place_ref, low_t_ref, dp_count, e), d_q_ref[...]), 1, size.tile_rows)
        lefts = grad_rows(place_ref, left_ref, dp_count, e)
        for t in range(2):
            put_grad(target, dot_f32(lefts, d_kv_ref[:, t * width : (t + 1) * width]), 2 + t, size.tile_rows)
        put_grad(target, grad_rows(place_ref, cols_ref, dp_count, e), 4, size.tile_rows)


def third(
    size, visits, place, q, do, o, lse, kv, qseg, kseg, near, far, whole, hat, inv, norms, d_two, sums, mixed_self
):
    own, width = hat.shape
    group = (size.x_count, size.pieces, 5 * size.tile_rows, width)
    return run_kernel(
        functools.partial(third_kernel, size),
        us=30,
        out_shape=(
            shape((size.length // 2, width)),
            shape((size.length // 2, width)),
            shape(group),
            shape(group),
            shape((own, width), F32),
            shape((own, width)),
        ),
        kinds=[SMEM] * 2 + [NOW] * 7 + [LATER] * 9,
        scratch_shapes=back_scratch(size, width)
        + [
            pltpu.VMEM((own, width), BF),
            pltpu.VMEM((size.length, 2 * width), BF),
            pltpu.VMEM((width, size.length), BF),
            pltpu.VMEM((width, own), BF),
            pltpu.VMEM((width, own), BF),
            pltpu.VMEM((width, width), F32),
        ],
    )(visits, place, q, do, o, lse, kv, qseg, kseg, near, far, whole, hat, inv, norms, d_two, sums, mixed_self)


def fourth_kernel(
    size,
    visit_ref,
    place_ref,
    q_ref,
    do_ref,
    o_ref,
    lse_ref,
    kv_ref,
    qseg_ref,
    kseg_ref,
    whole_ref,
    d_one_ref,
    near_ref,
    far_ref,
    kept_rows_ref,
    send_rows_ref,
    kept_ref,
    send_ref,
    seg_ref,
    sum_ref,
    dqt_ref,
    qst_ref,
    dst_ref,
    delta_ref,
    d_q_ref,
    d_kv_ref,
    left_ref,
    own_t_ref,
    moves,
):
    sum_ref[...] = jnp.zeros(sum_ref.shape, F32)
    moves.begin()
    turn_segments(kseg_ref, seg_ref)
    attend_back_part(
        visit_ref,
        q_ref,
        do_ref,
        o_ref,
        lse_ref,
        kv_ref,
        qseg_ref,
        seg_ref,
        d_q_ref,
        d_kv_ref,
        sum_ref,
        dqt_ref,
        qst_ref,
        dst_ref,
        delta_ref,
    )
    moves.ready()
    back_pairs(size, d_kv_ref, whole_ref[1], whole_ref[2], kept_rows_ref, send_rows_ref)
    mine = d_one_ref[...] + dot_nt(d_q_ref[...], whole_ref[0])
    half = size.half
    y_count = size.length // (2 * half * size.z_count)
    for z in range(size.z_count):
        at = pl.ds(pl.multiple_of((z * y_count + place_ref[3]) * half, half), half)
        total = kept_rows_ref[at, :].astype(F32) + mine[z * half : (z + 1) * half]
        kept_rows_ref[at, :] = total.astype(kept_rows_ref.dtype)
    moves.done(0, 1)
    width = d_one_ref.shape[1]
    dp_count = 2 * size.x_count
    turn_rows(size, near_ref, far_ref, left_ref)
    own_t_ref[...] = jnp.transpose(own_tokens(near_ref, place_ref, half, size.z_count))
    for e, target in enumerate((kept_ref, send_ref)):
        put_grad(target, dot_f32(grad_rows(place_ref, own_t_ref, dp_count, e), d_q_ref[...]), 0, size.tile_rows)
        lefts = grad_rows(place_ref, left_ref, dp_count, e)
        for t in range(2):
            put_grad(target, dot_f32(lefts, d_kv_ref[:, t * width : (t + 1) * width]), 1 + t, size.tile_rows)


def fourth(size, visits, place, q, do, o, lse, kv, qseg, kseg, whole, d_one, near, far):
    own, width = d_one.shape
    group = (size.x_count, size.pieces, 3 * size.tile_rows, width)
    return run_kernel(
        functools.partial(fourth_kernel, size),
        us=27,
        out_shape=(shape((size.length // 2, width)), shape((size.length // 2, width)), shape(group), shape(group)),
        kinds=[SMEM] * 2 + [NOW] * 7 + [LATER] * 4,
        scratch_shapes=back_scratch(size, width)
        + [
            pltpu.VMEM((own, width), BF),
            pltpu.VMEM((size.length, 2 * width), BF),
            pltpu.VMEM((width, size.length), BF),
            pltpu.VMEM((width, own), BF),
        ],
    )(visits, place, q, do, o, lse, kv, qseg, kseg, whole, d_one, near, far)


def together(*values):
    return lax.optimization_barrier(values)


def unxor(parts, place):
    if len(parts) == 2:
        return jnp.where(place == 0, jnp.stack(parts), jnp.stack(parts[::-1]))
    out = jnp.zeros((len(parts),) + parts[0].shape, parts[0].dtype)
    for k, part in enumerate(parts):
        out = lax.dynamic_update_index_in_dim(out, part, place ^ k, 0)
    return out


def body(
    inputs,
    encoder,
    tgt_seg,
    src_len,
    cotangent,
    self_in,
    self_out,
    cross_q,
    cross_kv,
    cross_out,
    ffn_in,
    ffn_out,
    norm_params,
):
    held, local_rows, width = inputs.shape
    half = local_rows // 2
    dp_count, seq_count = lax.axis_size("dp"), lax.axis_size("seq")
    length = local_rows * seq_count
    x_count = dp_count // 2
    z_count = 2 * held
    y_count = seq_count // z_count
    dp_place, seq_place = lax.axis_index("dp"), lax.axis_index("seq")
    x_place, c_place = dp_place // 2, dp_place % 2
    z_place, y_place = seq_place // y_count, seq_place % y_count
    place = jnp.stack([x_place, c_place, z_place, y_place]).astype(jnp.int32)
    rows = self_in.shape[0]
    fine = rows % 16 == 0
    pieces = seq_count if fine else 1
    tile_rows = rows * seq_count // pieces

    def over_core(v):
        return lax.ppermute(v, "dp", [(i, i ^ 1) for i in range(dp_count)])

    def over_x(v, k):
        return v if k == 0 else lax.ppermute(v, "dp", [(i, i ^ (2 * k)) for i in range(dp_count)])

    def over_y(v, k):
        return v if k == 0 else lax.ppermute(v, "seq", [(i, i ^ k) for i in range(seq_count)])

    def over_z(v, k):
        return v if k == 0 else lax.ppermute(v, "seq", [(i, i ^ (k * y_count)) for i in range(seq_count)])

    def pick(v, at, axis=0):
        return lax.dynamic_index_in_dim(v, at, axis, keepdims=False)

    def by_core(mine, other, axis=0):
        return jnp.where(
            c_place == 0, jnp.concatenate([mine, other], axis=axis), jnp.concatenate([other, mine], axis=axis)
        )

    def exchange(v):
        return lax.all_to_all(v, "seq", 0, 0, tiled=True)

    def exchange_z(v):
        groups = [[z * y_count + y for z in range(z_count)] for y in range(y_count)]
        return lax.all_to_all(v, "seq", 0, 0, tiled=True, axis_index_groups=groups)

    def tiles_of(v):
        return v.reshape(rows, -1, width).transpose(1, 0, 2).reshape(-1, width)

    def y_gather(v):
        return y_order(y_moves(v))

    def y_moves(v):
        return [over_y(v, k) for k in range(y_count)]

    def y_order(moves):
        return unxor(moves, y_place).swapaxes(0, 1).reshape((seq_count,) + moves[0].shape[1:])

    def with_weights(blocks, weights):
        weights = weights.reshape(-1, width)
        return jnp.concatenate([blocks, jnp.broadcast_to(weights, (z_count,) + weights.shape)], axis=1)

    def coarse_parts(v, outer):
        whole = lax.all_gather(v, ("dp", "seq"), axis=0).reshape((x_count, 2, seq_count) + v.shape)
        inner = whole[:, :, :, : v.shape[0] - outer].reshape(x_count, 2, seq_count, -1, rows, width)
        inner = inner.swapaxes(2, 3).reshape(x_count, 2, -1, width)
        whole = jnp.concatenate([inner, whole[:, :, :, v.shape[0] - outer :].reshape(x_count, 2, -1, width)], axis=2)
        out = []
        for e in range(2):
            mine = pick(whole, c_place ^ e, 1)
            out.append(jnp.concatenate([pick(mine, x_place ^ k) for k in range(x_count)])[None])
        return out

    def x_moves(kept, came):
        out = [(kept[0].astype(F32) + came[0]).astype(BF)]
        return out + [over_x((kept[k].astype(F32) + came[k]).astype(BF), k) for k in range(1, x_count)]

    def total(values):
        out = values[0].astype(F32)
        for v in values[1:]:
            out = out + v
        return out.astype(BF)

    def by_owner(v, outer):
        if fine:
            return v
        inner = v[0, : v.shape[1] - outer].reshape(-1, seq_count, rows, width).swapaxes(0, 1)
        inner = inner.reshape(seq_count, -1, width)
        return jnp.concatenate([inner, v[0, v.shape[1] - outer :].reshape(seq_count, -1, width)], axis=1)

    def y_parts(v):
        v = v.reshape((z_count, y_count) + v.shape[1:])
        return [over_y(pick(v, y_place ^ k, 1), k) for k in range(y_count)]

    def z_parts(v):
        return [over_z(pick(v, z_place ^ k), k) for k in range(z_count)]

    def untiled(v):
        return v.reshape(-1, rows, width).transpose(1, 0, 2).reshape(rows, -1)

    def home(v):
        v = v.astype(BF).reshape(2, held, half, width)
        mine, other = pick(v, c_place), over_core(pick(v, 1 - c_place))
        mine, other = mine[:, None], other[:, None]
        return by_core(mine, other, 1).reshape(held, local_rows, width).astype(F32)

    notes = jnp.concatenate([tgt_seg, src_len], axis=1)
    notes = pick(by_core(notes, over_core(notes)), z_place)
    target_all, lengths = notes[:length], notes[length:]
    docs = lengths.shape[0]
    upto = lax.broadcasted_iota(jnp.int32, (docs, docs), 0) <= lax.broadcasted_iota(jnp.int32, (docs, docs), 1)
    ends = jnp.sum(jnp.where(upto, lengths[:, None], 0), axis=0, dtype=jnp.int32)
    positions = jnp.arange(length, dtype=jnp.int32)
    source_all = jnp.sum((positions[:, None] >= ends[None, :]).astype(jnp.int32), axis=1, dtype=jnp.int32)
    qseg = pick(target_all.reshape(z_count, y_count * 2, half), y_place * 2 + c_place, 1)
    keys = 2 * half

    def in_order(segments):
        pairs = segments.reshape(-1, 2, half)
        return jnp.where(c_place == 0, pairs, pairs[:, ::-1]).reshape(-1, 1, keys)

    def visits(segments):
        low = jnp.sum((segments[None, :] < qseg[:, :1]).astype(jnp.int32), axis=1, dtype=jnp.int32)
        high = jnp.sum((segments[None, :] <= qseg[:, -1:]).astype(jnp.int32), axis=1, dtype=jnp.int32)
        table = jnp.stack([low // keys, (high + keys - 1) // keys])
        return jnp.pad(table, ((0, 0), (0, length // keys - z_count)))

    self_kseg, cross_kseg = in_order(target_all), in_order(source_all)
    self_visits, cross_visits = visits(target_all), visits(source_all)

    hidden = ffn_in.shape[1]
    outer = ffn_out.shape[0]
    norm_wide = jnp.pad(norm_params, ((0, 0), (0, width - norm_params.shape[1])))
    first_tiles = tiles_of(self_in)
    rest_tiles = tiles_of(jnp.concatenate([self_out, cross_q, cross_kv, cross_out, norm_wide, ffn_in], axis=1))
    rest_tiles = jnp.concatenate([rest_tiles, ffn_out], axis=0)
    mid = 6 * rows
    size = Size(
        half=half,
        length=length,
        own=z_count * half,
        z_count=z_count,
        x_count=x_count,
        pieces=pieces,
        tile_rows=tile_rows,
        hidden=hidden,
        feed_rows=hidden // width * tile_rows + outer * seq_count // pieces,
        first_one=(half,) if fine else (0,),
        first_two=(half,) if fine else (0,),
        first_three=(0,),
    )
    qseg = qseg[:, None, :]
    streams = jnp.stack([inputs, encoder, cotangent]).reshape(3, held, 2, half, width)
    mine = pick(streams, c_place, 2)
    other = over_core(pick(streams, 1 - c_place, 2))
    streams = by_core(mine, other, 1)
    x_blocks, source_blocks, cot = streams[0], streams[1], streams[2]
    if fine:
        x_blocks = with_weights(x_blocks, jnp.stack([over_x(first_tiles, k) for k in range(x_count)]))
        rest = jnp.stack([over_x(rest_tiles, k) for k in range(x_count)])
        source_blocks = with_weights(source_blocks, rest[:, :mid])
        cot = with_weights(cot, rest[:, mid:])
    x_near = exchange_z(x_blocks)
    x_near, source_blocks = together(x_near, source_blocks)
    x_moves_y = y_moves(x_near)
    source_near = exchange_z(source_blocks)
    x_near = y_order(x_moves_y)
    x_far = over_core(x_near)
    x_near, x_far, source_near, cot = together(x_near, x_far, source_near, cot)
    source_moves = y_moves(source_near)
    cot = exchange_z(cot)
    weights = (x_near, x_far) if fine else coarse_parts(first_tiles, 0)

    queries, pairs, whole_one, mixed_self, self_lse = first(
        size, self_visits, place, weights, x_near, x_far, qseg, self_kseg
    )
    whole_one = whole_one.reshape(3, width, width)
    mixed_self, cot, *source_moves = together(mixed_self, cot, *source_moves)
    source_near = y_order(source_moves)
    source_far = over_core(source_near)
    if fine:
        w3_moves = y_moves(cot[:, half:])
        weights = (source_near, source_far)
    else:
        weights = coarse_parts(rest_tiles[:mid], 0)
    queries_c, pairs_c, whole_two, hat_one, inv_one, norms, mixed_cross, cross_lse = second(
        size, cross_visits, place, weights, x_near, source_near, source_far, mixed_self, qseg, cross_kseg
    )
    whole_two = whole_two.reshape(6, width, width)
    if fine:
        mixed_cross, *w3_moves = together(mixed_cross, *w3_moves)
        w3 = y_order(w3_moves)
        weights = (w3, over_core(w3))
    else:
        weights = coarse_parts(rest_tiles[mid:], outer)
    out_low, d_two, d_mixed_c, sums, low_t, dz, hid, down, mixed_ct = feed(
        size, place, weights, mixed_cross, whole_two, hat_one, norms, cot
    )

    f_send = feed_grads(size, 1, place, low_t, dz, hid, down, mixed_ct, d_two)
    f_came = over_core(f_send)
    low_t, f_send, out_low = together(low_t, f_send, out_low)
    f_kept = feed_grads(size, 0, place, low_t, dz, hid, down, mixed_ct, d_two)
    out_parts = exchange_z(out_low.reshape(z_count, half, width))
    d_mixed_c, f_kept, f_came = together(d_mixed_c, f_kept, f_came)
    f_moves = x_moves(f_kept, f_came)
    d_mixed_c, f_first = together(d_mixed_c, f_moves[0])
    s_kept, s_send, c_kept, c_send, d_one, d_mixed = third(
        size,
        cross_visits,
        place,
        queries_c,
        d_mixed_c,
        mixed_cross,
        cross_lse,
        pairs_c,
        qseg,
        cross_kseg,
        source_near,
        source_far,
        whole_two,
        hat_one,
        inv_one,
        norms,
        d_two,
        sums,
        mixed_self,
    )
    s_kept, s_send, c_kept, c_send, d_one, d_mixed, out_parts, f_first, *f_moves = together(
        s_kept, s_send, c_kept, c_send, d_one, d_mixed, out_parts, f_first, *f_moves[1:]
    )
    s_came, c_came = over_core(s_send), over_core(c_send)
    f_sum = by_owner(total([f_first, *f_moves]), hidden // dp_count)
    f_sum, s_came, c_came = together(f_sum, s_came, c_came)
    s_sum = total([s_kept, s_came]).reshape(seq_count, half, width)
    fs_moves = y_parts(jnp.concatenate([f_sum, s_sum], axis=1))
    c_moves = x_moves(c_kept, c_came)
    d_mixed, fs_first, c_first = together(d_mixed, fs_moves[0], c_moves[0])
    x_kept, x_send, i_kept, i_send = fourth(
        size,
        self_visits,
        place,
        queries,
        d_mixed,
        mixed_self,
        self_lse,
        pairs,
        qseg,
        self_kseg,
        whole_one,
        d_one,
        x_near,
        x_far,
    )
    extra = len(fs_moves) - 1
    x_kept, x_send, i_kept, i_send, fs_first, c_first, out_parts, *moves = together(
        x_kept, x_send, i_kept, i_send, fs_first, c_first, out_parts, *fs_moves[1:], *c_moves[1:]
    )
    x_came, i_came = over_core(x_send), over_core(i_send)
    fs_parts = z_parts(total([fs_first, *moves[:extra]]))
    x_came, i_came, fs_first = together(x_came, i_came, fs_parts[0])
    x_moves_y = y_parts(total([x_kept, x_came]).reshape(seq_count, half, width))
    x_first, i_came, i_kept = together(x_moves_y[0], i_came, i_kept)
    i_moves = x_moves(i_kept, i_came)
    c_sum = by_owner(total([c_first, *moves[extra:]]), 0)
    i_first, c_sum, *x_moves_y = together(i_moves[0], c_sum, x_first, *x_moves_y[1:])
    x_parts = exchange_z(total(x_moves_y))
    i_sum = by_owner(total([i_first, *i_moves[1:]]), 0)
    w_moves = y_parts(jnp.concatenate([c_sum, i_sum], axis=1))
    w_first, out_parts, fs_first, *fs_parts = together(w_moves[0], out_parts, fs_first, *fs_parts[1:])
    fs_parts = [fs_first] + fs_parts
    grad_source = home(unxor([v[-half:] for v in fs_parts], z_place))
    out_tokens = home(out_parts)
    f_own = sum((v[:-half].astype(F32) for v in fs_parts[1:]), fs_parts[0][:-half].astype(F32))
    w_parts = z_parts(total([w_first, *w_moves[1:]]))
    w_first, x_parts = together(w_parts[0], x_parts)
    w_own = sum(w_parts[1:], w_first.astype(F32))
    c_own, i_own = w_own[: 5 * rows], w_own[5 * rows :]
    grad_tokens = home(x_parts)
    f_in = hidden // width * rows
    c_own = c_own.reshape(5, rows, width)
    return (
        out_tokens,
        grad_tokens,
        grad_source,
        untiled(i_own),
        c_own[0],
        c_own[1],
        untiled(c_own[2:4]),
        f_own[f_in : f_in + rows],
        untiled(f_own[:f_in]),
        f_own[f_in + rows :],
        c_own[4][:, : norm_params.shape[1]],
    )


def solution(mesh):
    tokens, rows = P("dp", "seq", None), P(("dp", "seq"), None)
    return jax.shard_map(
        body,
        mesh=mesh,
        in_specs=(tokens, tokens, P("dp", None), P("dp", None), tokens) + (rows,) * 8,
        out_specs=(tokens,) * 3 + (rows,) * 8,
        check_vma=False,
    )
```

```python
import dataclasses
import functools
import math

import jax
import jax.numpy as jnp
from jax import lax
from jax.experimental import pallas as pl
from jax.experimental.pallas import tpu as pltpu
from jax.sharding import PartitionSpec as P

HEAD_DIM = 64
GROUP = 4
LANES = GROUP * HEAD_DIM
PACE = 1.15e9 * 0.1
WIDE = 60
CHUNK = 256
LOG2E = 1.4426950408889634
LN2 = 0.6931471805599453
GELU_A = 0.7978845608028654
GELU_B = 0.044715
BF = jnp.bfloat16
F32 = jnp.float32
SMEM = pl.BlockSpec(memory_space=pltpu.SMEM)
VMEM = pl.BlockSpec(memory_space=pltpu.VMEM)
ANY = pl.BlockSpec(memory_space=pl.ANY)
NOW, LATER = "now", "later"


def dot_f32(left, right):
    return jnp.dot(left, right, preferred_element_type=F32)


def dot_nt(left, right):
    return lax.dot_general(left, right, (((1,), (1,)), ((), ())), preferred_element_type=F32)


def padded_bytes(dims, dtype):
    dims = (1,) * (2 - len(dims)) + tuple(dims)
    lead = math.prod(dims[:-2])
    return lead * (-(-dims[-2] // 16) * 16) * (-(-dims[-1] // 128) * 128) * jnp.dtype(dtype).itemsize


def kernel_call(kernel, *, out_shape, in_specs, out_specs, scratch_shapes=(), spare=3, us=2):
    def call(*operands):
        need = spare * 2**20
        for operand, spec in zip(operands, in_specs):
            need += padded_bytes(operand.shape, operand.dtype) if spec is VMEM else 0
        for result in jax.tree.leaves(out_shape):
            need += padded_bytes(result.shape, result.dtype)
        for scratch in scratch_shapes:
            if getattr(scratch, "memory_space", None) == pltpu.VMEM:
                need += padded_bytes(scratch.shape, scratch.dtype)
        return pl.pallas_call(
            kernel,
            out_shape=out_shape,
            in_specs=in_specs,
            out_specs=out_specs,
            scratch_shapes=scratch_shapes,
            compiler_params=pltpu.CompilerParams(vmem_limit_bytes=need),
            cost_estimate=pl.CostEstimate(flops=int(us * PACE), bytes_accessed=2**10, transcendentals=0),
        )(*operands)

    return call


class Moves:
    def __init__(self, now, late, out):
        self.now, self.late, self.out, self.begun = now, late, out, set()

    def begin(self):
        for copy in self.now:
            copy.wait()

    def ready(self):
        for copy in self.late:
            copy.wait()

    def done(self, *results):
        for i in results:
            self.out[i].start()
            self.begun.add(i)

    def finish(self):
        self.done(*(i for i in range(len(self.out)) if i not in self.begun))
        for copy in self.out:
            copy.wait()


def run_kernel(kernel, *, out_shape, kinds, scratch_shapes=(), us=2):
    def call(*operands):
        moved = [i for i, kind in enumerate(kinds) if kind in (NOW, LATER)]
        count, outs, own = len(kinds), len(out_shape), len(scratch_shapes)

        def wrapped(*refs):
            ins, results, scratch = list(refs[:count]), refs[count : count + outs], refs[count + outs :]
            mine, scratch = scratch[:own], scratch[own:]
            slots, scratch = scratch[: len(moved)], scratch[len(moved) :]
            made, (in_sem, out_sem) = scratch[:outs], scratch[outs:]
            now, late = [], []
            for n, i in enumerate(moved):
                copy = pltpu.make_async_copy(ins[i], slots[n], in_sem.at[n])
                copy.start()
                (now if kinds[i] == NOW else late).append(copy)
                ins[i] = slots[n]
            moves = Moves(now, late, [pltpu.make_async_copy(a, b, out_sem.at[n]) for n, (a, b) in enumerate(zip(made, results))])
            kernel(*ins, *made, *mine, moves=moves)
            moves.finish()

        return pl.pallas_call(
            wrapped,
            out_shape=out_shape,
            in_specs=[SMEM if kind is SMEM else ANY for kind in kinds],
            out_specs=(ANY,) * outs,
            scratch_shapes=list(scratch_shapes)
            + [pltpu.VMEM(operands[i].shape, operands[i].dtype) for i in moved]
            + [pltpu.VMEM(v.shape, v.dtype) for v in out_shape]
            + [pltpu.SemaphoreType.DMA((len(moved),)), pltpu.SemaphoreType.DMA((outs,))],
            compiler_params=pltpu.CompilerParams(vmem_limit_bytes=WIDE * 2**20),
            cost_estimate=pl.CostEstimate(flops=int(us * PACE), bytes_accessed=2**10, transcendentals=0),
        )(*operands)

    return call


def shape(dims, dtype=BF):
    return jax.ShapeDtypeStruct(dims, dtype)


def chunk(i):
    return pl.ds(pl.multiple_of(i * CHUNK, CHUNK), CHUNK)


@dataclasses.dataclass(frozen=True)
class Size:
    half: int
    length: int
    own: int
    z_count: int
    x_count: int
    pieces: int
    tile_rows: int
    hidden: int
    feed_rows: int
    first_one: tuple
    first_two: tuple
    first_three: tuple


def stack_heads(tile):
    head = lax.broadcasted_iota(jnp.int32, tile.shape, 1) // HEAD_DIM
    zero = jnp.zeros_like(tile)
    return jnp.concatenate([jnp.where(head == h, tile, zero) for h in range(GROUP)], axis=0)


def row_of(column):
    return jnp.transpose(jnp.broadcast_to(column, (column.shape[0], 128)))[0:1, :]


def key_rows(b, keys, total):
    half = keys // 2
    at = pl.multiple_of(b * half, half)
    return pl.ds(at, half), pl.ds(pl.multiple_of(at + total // 2, half), half)


def both_rows(ref, spots, cols):
    return jnp.concatenate([ref[spot, cols] for spot in spots], axis=0)


def turn_segments(kseg_ref, seg_ref):
    count, _, keys = kseg_ref.shape
    for b in range(count):
        row = kseg_ref[b].astype(F32)
        seg_ref[b * keys : (b + 1) * keys, :] = jnp.transpose(jnp.broadcast_to(row, (128, keys)))[:, :1]


def attend_part(visit_ref, q_ref, kv_ref, qseg_ref, seg_ref, o_ref, lse_ref, acc_ref, qst_ref):
    width = q_ref.shape[1]
    blocks = qseg_ref.shape[0]
    rows = q_ref.shape[0] // blocks
    total = kv_ref.shape[0]
    keys = total // visit_ref.shape[1]
    groups = width // LANES

    def block(k, carry):
        lo, hi = visit_ref[0, k], visit_ref[1, k]
        q_rows = pl.ds(pl.multiple_of(k * rows, rows), rows)
        qseg = jnp.concatenate([qseg_ref[k].astype(F32)] * GROUP, axis=1)
        for g in range(groups):
            qst_ref[g] = stack_heads(q_ref[q_rows, g * LANES : (g + 1) * LANES])
        acc_ref[...] = jnp.zeros(acc_ref.shape, F32)

        def step(b, carry):
            spots = key_rows(b, keys, total)
            same = seg_ref[pl.ds(pl.multiple_of(b * keys, keys), keys), :] == qseg
            scores = [
                dot_nt(both_rows(kv_ref, spots, slice(g * LANES, (g + 1) * LANES)), qst_ref[g]) for g in range(groups)
            ]
            out, lows, fades = [], [], []
            for g in range(groups):
                top, tot = carry[g]
                masked = jnp.where(same, scores[g], -1e30)
                new = jnp.maximum(top, jnp.max(masked, axis=0, keepdims=True))
                soft = jnp.exp2(masked - new)
                fade = jnp.exp2(top - new)
                out.append((new, tot * fade + jnp.sum(soft, axis=0, keepdims=True)))
                lows.append(soft.astype(BF))
                fades.append(fade)
            for g in range(groups):
                turned = jnp.transpose(both_rows(kv_ref, spots, slice(width + g * LANES, width + (g + 1) * LANES)))
                for h in range(GROUP):
                    at = g * LANES + h * HEAD_DIM
                    cols = slice(h * rows, (h + 1) * rows)
                    values = turned[h * HEAD_DIM : (h + 1) * HEAD_DIM]
                    acc_ref[at : at + HEAD_DIM] = acc_ref[at : at + HEAD_DIM] * fades[g][:, cols] + dot_f32(
                        values, lows[g][:, cols]
                    )
            return tuple(out)

        start = (jnp.full((1, GROUP * rows), -3e38, F32), jnp.zeros((1, GROUP * rows), F32))
        end = lax.fori_loop(lo, hi, step, (start,) * groups)
        for g in range(groups):
            top, tot = end[g]
            inv = 1.0 / tot
            mixed = [
                acc_ref[g * LANES + h * HEAD_DIM : g * LANES + (h + 1) * HEAD_DIM] * inv[:, h * rows : (h + 1) * rows]
                for h in range(GROUP)
            ]
            o_ref[q_rows, g * LANES : (g + 1) * LANES] = jnp.transpose(jnp.concatenate(mixed, axis=0)).astype(BF)
            lse_ref[k * groups + g] = top + jnp.log2(tot)
        return carry

    lax.fori_loop(0, blocks, block, 0)


def attend_back_part(
    visit_ref,
    q_ref,
    do_ref,
    o_ref,
    lse_ref,
    kv_ref,
    qseg_ref,
    seg_ref,
    dq_ref,
    dkv_ref,
    sum_ref,
    dqt_ref,
    qst_ref,
    dst_ref,
    delta_ref,
):
    width = q_ref.shape[1]
    blocks = qseg_ref.shape[0]
    rows = q_ref.shape[0] // blocks
    total = kv_ref.shape[0]
    keys = total // visit_ref.shape[1]
    groups = width // LANES
    def block(k, carry):
        lo, hi = visit_ref[0, k], visit_ref[1, k]
        q_rows = pl.ds(pl.multiple_of(k * rows, rows), rows)
        qseg = jnp.concatenate([qseg_ref[k].astype(F32)] * GROUP, axis=1)
        for g in range(groups):
            cols = slice(g * LANES, (g + 1) * LANES)
            qst_ref[g] = stack_heads(q_ref[q_rows, cols])
            d_mixed = do_ref[q_rows, cols]
            dst_ref[g] = stack_heads(d_mixed)
            prod = d_mixed.astype(F32) * o_ref[q_rows, cols].astype(F32)
            delta_ref[g] = row_of(jnp.sum(stack_heads(prod), axis=1, keepdims=True))
        dqt_ref[...] = jnp.zeros(dqt_ref.shape, F32)

        def step(b, carry):
            spots = key_rows(b, keys, total)
            same = seg_ref[pl.ds(pl.multiple_of(b * keys, keys), keys), :] == qseg
            k_cols = [slice(g * LANES, (g + 1) * LANES) for g in range(groups)]
            v_cols = [slice(width + g * LANES, width + (g + 1) * LANES) for g in range(groups)]
            scores = [dot_nt(both_rows(kv_ref, spots, k_cols[g]), qst_ref[g]) for g in range(groups)]
            d_soft = [dot_nt(both_rows(kv_ref, spots, v_cols[g]), dst_ref[g]) for g in range(groups)]
            softs, d_scores = [], []
            for g in range(groups):
                soft = jnp.where(same, jnp.exp2(scores[g] - lse_ref[k * groups + g]), 0.0)
                d_scores.append((soft * (d_soft[g] - delta_ref[g])).astype(BF))
                softs.append(soft.astype(BF))
            for g in range(groups):
                d_keys, d_values = dot_f32(d_scores[g], qst_ref[g]), dot_f32(softs[g], dst_ref[g])
                for e, spot in enumerate(spots):
                    part = slice(e * keys // 2, (e + 1) * keys // 2)
                    sum_ref[spot, k_cols[g]] += d_keys[part]
                    sum_ref[spot, v_cols[g]] += d_values[part]
                turned = jnp.transpose(both_rows(kv_ref, spots, k_cols[g]))
                for h in range(GROUP):
                    at = slice(g * LANES + h * HEAD_DIM, g * LANES + (h + 1) * HEAD_DIM)
                    keys_t = turned[h * HEAD_DIM : (h + 1) * HEAD_DIM]
                    dqt_ref[at] += dot_f32(keys_t, d_scores[g][:, h * rows : (h + 1) * rows])
            return carry

        lax.fori_loop(lo, hi, step, 0)
        for g in range(groups):
            cols = slice(g * LANES, (g + 1) * LANES)
            dq_ref[q_rows, cols] = (jnp.transpose(dqt_ref[cols]) * HEAD_DIM**-0.5).astype(BF)
        return carry

    lax.fori_loop(0, blocks, block, 0)
    dkv_ref[:, :width] = (sum_ref[:, :width] * LN2).astype(BF)
    dkv_ref[:, width:] = sum_ref[:, width:].astype(BF)


def norm_of(resid):
    centered = resid - jnp.mean(resid, axis=-1, keepdims=True)
    inv = lax.rsqrt(jnp.mean(centered * centered, axis=-1, keepdims=True) + 1e-05)
    return centered * inv, inv


def norm_pull(upstream, hat, inv, gain):
    scaled = upstream * gain
    return inv * (
        scaled - jnp.mean(scaled, axis=-1, keepdims=True) - hat * jnp.mean(scaled * hat, axis=-1, keepdims=True)
    )


def weight_rows(size, weights, total, firsts):
    out = []
    per = len(weights) // 2
    for e in range(2):
        for k in range(size.x_count):
            a = min(k, per - 1)
            out.append((k, e, weights[e * per + a], firsts[a] + (k - a) * total))
    return out


def fetch_tiles(size, place_ref, weights, tiles, firsts, whole_ref, sem):
    copies = []
    rows = size.tile_rows
    for k, e, part, start in weight_rows(size, weights, tiles * rows, firsts):
        pieces = part.shape[0]
        dp = (place_ref[0] ^ k) * 2 + (place_ref[1] ^ e)
        at = pl.ds(pl.multiple_of(dp * pieces, pieces), pieces)
        for t in range(tiles):
            source = part.at[:, pl.ds(start + t * rows, rows)]
            copies.append(pltpu.make_async_copy(source, whole_ref.at[t, at], sem.at[len(copies)]))
    for copy in copies:
        copy.start()
    return copies


def tile_of(ref, t):
    tile = ref[t]
    return tile.reshape(-1, tile.shape[-1])


def own_tokens(near_ref, place_ref, half, z_count):
    y_count = near_ref.shape[0] // z_count
    return jnp.concatenate([near_ref[z * y_count + place_ref[3], :half, :] for z in range(z_count)], axis=0)


def sequence_rows(ref, i, half):
    count = CHUNK // half
    return jnp.concatenate([ref[i * count + j, :half, :] for j in range(count)], axis=0)


def put_pairs(near_ref, far_ref, half, w_k, w_v, kv_ref):
    width = w_k.shape[1]
    count = near_ref.shape[0] * half // CHUNK
    for e, ref in enumerate((near_ref, far_ref)):

        def step(i, carry):
            rows = sequence_rows(ref, i, half)
            at = chunk(i + e * count)
            kv_ref[at, :width] = dot_f32(rows, w_k).astype(BF)
            kv_ref[at, width:] = dot_f32(rows, w_v).astype(BF)
            return carry

        lax.fori_loop(0, count, step, 0)


def grad_rows(place_ref, left_ref, dp_count, e):
    rows = left_ref.shape[0] // dp_count
    out = []
    for k in range(dp_count // 2):
        dp = (place_ref[0] ^ k) * 2 + (place_ref[1] ^ e)
        out.append(left_ref[pl.ds(pl.multiple_of(dp * rows, rows), rows), :])
    return jnp.concatenate(out, axis=0)


def put_grad(target, value, tile, tile_rows):
    x_count, pieces, _, width = target.shape
    rows = value.shape[0] // x_count
    for k in range(x_count):
        part = value[k * rows : (k + 1) * rows].astype(target.dtype)
        target[k, :, tile * tile_rows : (tile + 1) * tile_rows, :] = part.reshape(pieces, tile_rows, width)


def attend_scratch(size, width):
    rows = size.own // size.z_count
    return [
        pltpu.VMEM((size.length, 1), F32),
        pltpu.VMEM((width, rows), F32),
        pltpu.VMEM((width // LANES, GROUP * rows, LANES), BF),
    ]


def first_kernel(
    size,
    visit_ref,
    place_ref,
    near_ref,
    far_ref,
    qseg_ref,
    kseg_ref,
    *refs,
    moves,
):
    weights, (q_ref, kv_ref, whole_ref, o_ref, lse_ref, seg_ref, acc_ref, qst_ref, sem) = refs[:-9], refs[-9:]
    copies = fetch_tiles(size, place_ref, weights, 3, size.first_one, whole_ref, sem)
    moves.begin()
    own = own_tokens(near_ref, place_ref, size.half, size.z_count)
    turn_segments(kseg_ref, seg_ref)
    for copy in copies:
        copy.wait()
    q_ref[...] = (dot_f32(own, tile_of(whole_ref, 0)) * (HEAD_DIM**-0.5 * LOG2E)).astype(BF)
    put_pairs(near_ref, far_ref, size.half, tile_of(whole_ref, 1), tile_of(whole_ref, 2), kv_ref)
    moves.done(0, 1, 2)
    attend_part(visit_ref, q_ref, kv_ref, qseg_ref, seg_ref, o_ref, lse_ref, acc_ref, qst_ref)


def lse_shape(size, width):
    return shape((size.z_count * width // LANES, 1, GROUP * size.half), F32)


def first(size, visits, place, weights, near, far, qseg, kseg):
    width = near.shape[2]
    return run_kernel(
        functools.partial(first_kernel, size),
        us=16,
        out_shape=(
            shape((size.own, width)),
            shape((size.length, 2 * width)),
            shape((3, 2 * size.x_count * size.pieces, size.tile_rows, width)),
            shape((size.own, width)),
            lse_shape(size, width),
        ),
        kinds=[SMEM] * 2 + [NOW] * 4 + [ANY] * len(weights),
        scratch_shapes=attend_scratch(size, width) + [pltpu.SemaphoreType.DMA((2 * size.x_count * 3,))],
    )(visits, place, near, far, qseg, kseg, *weights)


def second_kernel(
    size,
    visit_ref,
    place_ref,
    near_ref,
    source_near_ref,
    source_far_ref,
    mixed_ref,
    qseg_ref,
    kseg_ref,
    *refs,
    moves,
):
    weights = refs[:-12]
    q_ref, kv_ref, whole_ref, hat_ref, inv_ref, norm_ref, o_ref, lse_ref, seg_ref, acc_ref, qst_ref, sem = refs[-12:]
    copies = fetch_tiles(size, place_ref, weights, 6, size.first_two, whole_ref, sem)
    moves.begin()
    own = own_tokens(near_ref, place_ref, size.half, size.z_count)
    turn_segments(kseg_ref, seg_ref)
    for copy in copies:
        copy.wait()
    norm_ref[...] = jnp.transpose(tile_of(whole_ref, 5)[:, :128].astype(F32))[: norm_ref.shape[0]]
    hat, inv = norm_of(own.astype(F32) + dot_f32(mixed_ref[...], tile_of(whole_ref, 0)))
    hat_ref[...] = hat
    inv_ref[...] = inv
    low = (hat * norm_ref[0:1, :] + norm_ref[1:2, :]).astype(BF)
    q_ref[...] = (dot_f32(low, tile_of(whole_ref, 1)) * (HEAD_DIM**-0.5 * LOG2E)).astype(BF)
    moves.ready()
    put_pairs(source_near_ref, source_far_ref, size.half, tile_of(whole_ref, 2), tile_of(whole_ref, 3), kv_ref)
    moves.done(0, 1, 2, 3, 4, 5)
    attend_part(visit_ref, q_ref, kv_ref, qseg_ref, seg_ref, o_ref, lse_ref, acc_ref, qst_ref)


def second(size, visits, place, weights, near, source_near, source_far, mixed, qseg, kseg):
    width = near.shape[2]
    return run_kernel(
        functools.partial(second_kernel, size),
        us=17,
        out_shape=(
            shape((size.own, width)),
            shape((size.length, 2 * width)),
            shape((6, 2 * size.x_count * size.pieces, size.tile_rows, width)),
            shape((size.own, width), F32),
            shape((size.own, 1), F32),
            shape((8, width), F32),
            shape((size.own, width)),
            lse_shape(size, width),
        ),
        kinds=[SMEM] * 2 + [NOW, LATER, LATER, NOW, NOW, NOW] + [ANY] * len(weights),
        scratch_shapes=attend_scratch(size, width) + [pltpu.SemaphoreType.DMA((2 * size.x_count * 6,))],
    )(visits, place, near, source_near, source_far, mixed, qseg, kseg, *weights)


def feed_kernel(
    size,
    place_ref,
    mixed_ref,
    whole_two_ref,
    hat_one_ref,
    norm_ref,
    cot_ref,
    *refs,
):
    weights = refs[:-16]
    (
        out_ref,
        d_two_ref,
        d_mixed_ref,
        sums_ref,
        low_t_ref,
        dz_ref,
        hid_ref,
        down_ref,
        mixed_t_ref,
        w_in_ref,
        w_out_ref,
        z_ref,
        low_ref,
        hat_two_ref,
        inv_two_ref,
        sem,
    ) = refs[-16:]
    own, width = hat_one_ref.shape
    hidden = z_ref.shape[1]
    tiles = hidden // width
    tile_rows = size.tile_rows
    copies = []
    total = size.feed_rows
    for k, e, part, start in weight_rows(size, weights, total, size.first_three):
        pieces = part.shape[0]
        dp = (place_ref[0] ^ k) * 2 + (place_ref[1] ^ e)
        at = pl.ds(pl.multiple_of(dp * pieces, pieces), pieces)
        for t in range(tiles):
            source = part.at[:, pl.ds(start + t * tile_rows, tile_rows)]
            copies.append(pltpu.make_async_copy(source, w_in_ref.at[t, at], sem.at[len(copies)]))
        source = part.at[:, pl.ds(start + tiles * tile_rows, total - tiles * tile_rows)]
        copies.append(pltpu.make_async_copy(source, w_out_ref.at[at], sem.at[len(copies)]))
    for copy in copies:
        copy.start()
    mixed_t_ref[...] = jnp.transpose(mixed_ref[...])
    sums_ref[...] = jnp.zeros(sums_ref.shape, F32)
    cross_out = whole_two_ref[4]
    for copy in copies:
        copy.wait()
    per_tile = w_out_ref.shape[0] // tiles

    def w_down(t):
        return w_out_ref[t * per_tile : (t + 1) * per_tile].reshape(width, width)

    def forward(i, carry):
        at = chunk(i)
        one = hat_one_ref[at, :] * norm_ref[0:1, :] + norm_ref[1:2, :]
        hat, inv = norm_of(one + dot_f32(mixed_ref[at, :], cross_out))
        hat_two_ref[at, :] = hat
        inv_two_ref[at, :] = inv
        two = hat * norm_ref[2:3, :] + norm_ref[3:4, :]
        low = two.astype(BF)
        low_ref[at, :] = low
        total = two
        for t in range(tiles):
            cols = slice(t * width, (t + 1) * width)
            z = dot_f32(low, tile_of(w_in_ref, t))
            z_ref[at, cols] = z
            turn = jnp.tanh(GELU_A * (z + GELU_B * (z * z * z)))
            hid = (0.5 * z * (1.0 + turn)).astype(BF)
            hid_ref[at, cols] = hid
            total = total + dot_f32(hid, w_down(t))
        hat, inv = norm_of(total)
        gain = norm_ref[4:5, :]
        out_ref[at, :] = (hat * gain + norm_ref[5:6, :]).astype(BF)
        upstream = sequence_rows(cot_ref, i, size.half).astype(F32)
        sums_ref[4:5, :] += jnp.sum(upstream * hat, axis=0, keepdims=True)
        sums_ref[5:6, :] += jnp.sum(upstream, axis=0, keepdims=True)
        down = norm_pull(upstream, hat, inv, gain)
        low_down = down.astype(BF)
        down_ref[at, :] = low_down
        back = down
        for t in range(tiles):
            cols = slice(t * width, (t + 1) * width)
            d_hid = dot_nt(low_down, w_down(t))
            z = z_ref[at, cols]
            turn = jnp.tanh(GELU_A * (z + GELU_B * (z * z * z)))
            slope = 0.5 * (1.0 + turn) + (0.5 * GELU_A) * z * (1.0 - turn * turn) * (1.0 + (3.0 * GELU_B) * z * z)
            dz = (d_hid * slope).astype(BF)
            dz_ref[at, cols] = dz
            back = back + dot_nt(dz, tile_of(w_in_ref, t))
        hat, inv = hat_two_ref[at, :], inv_two_ref[at, :]
        sums_ref[2:3, :] += jnp.sum(back * hat, axis=0, keepdims=True)
        sums_ref[3:4, :] += jnp.sum(back, axis=0, keepdims=True)
        d_two = norm_pull(back, hat, inv, norm_ref[2:3, :])
        d_two_ref[at, :] = d_two
        d_mixed_ref[at, :] = dot_nt(d_two.astype(BF), cross_out).astype(BF)
        return carry

    lax.fori_loop(0, own // CHUNK, forward, 0)
    low_t_ref[...] = jnp.transpose(low_ref[...])


def feed(size, place, weights, mixed, whole_two, hat_one, norms, cot):
    own, width = hat_one.shape
    hidden = size.hidden
    devices = 2 * size.x_count * size.pieces
    return kernel_call(
        functools.partial(feed_kernel, size),
        us=12,
        out_shape=(
            shape((own, width)),
            shape((own, width), F32),
            shape((own, width)),
            shape((8, width), F32),
            shape((width, own)),
            shape((own, hidden)),
            shape((own, hidden)),
            shape((own, width)),
            shape((width, own)),
        ),
        in_specs=[SMEM] + [VMEM] * 5 + [ANY] * len(weights),
        out_specs=(VMEM,) * 9,
        scratch_shapes=[
            pltpu.VMEM((hidden // width, devices, size.tile_rows, width), BF),
            pltpu.VMEM((devices, hidden // devices, width), BF),
            pltpu.VMEM((own, hidden), F32),
            pltpu.VMEM((own, width), BF),
            pltpu.VMEM((own, width), F32),
            pltpu.VMEM((own, 1), F32),
            pltpu.SemaphoreType.DMA((2 * size.x_count * (hidden // width + 1),)),
        ],
    )(place, mixed, whole_two, hat_one, norms, cot, *weights)


def feed_grads_kernel(
    size, e, place_ref, low_t_ref, dz_ref, hid_ref, down_ref, mixed_t_ref, d_two_ref, target
):
    width = low_t_ref.shape[0]
    hidden = dz_ref.shape[1]
    tiles = hidden // width
    lefts = grad_rows(place_ref, low_t_ref, 2 * size.x_count, e)
    for t in range(tiles):
        put_grad(target, dot_f32(lefts, dz_ref[:, t * width : (t + 1) * width]), t, size.tile_rows)
    value = dot_f32(grad_rows(place_ref, mixed_t_ref, 2 * size.x_count, e), d_two_ref[...].astype(BF))
    put_grad(target, value, tiles, size.tile_rows)
    rows = hidden // (2 * size.x_count)
    for k in range(size.x_count):
        dp = (place_ref[0] ^ k) * 2 + (place_ref[1] ^ e)
        cols = pl.ds(pl.multiple_of(dp * rows, rows), rows)
        value = dot_f32(jnp.transpose(hid_ref[:, cols]), down_ref[...]).astype(target.dtype)
        target[k, :, (tiles + 1) * size.tile_rows :, :] = value.reshape(size.pieces, rows // size.pieces, width)


def feed_grads(size, e, place, low_t, dz, hid, down, mixed_t, d_two):
    width = low_t.shape[0]
    tiles = size.hidden // width
    rows = (tiles + 1) * size.tile_rows + size.hidden // (2 * size.x_count * size.pieces)
    return kernel_call(
        functools.partial(feed_grads_kernel, size, e),
        out_shape=shape((size.x_count, size.pieces, rows, width)),
        in_specs=[SMEM] + [VMEM] * 6,
        out_specs=VMEM,
    )(place, low_t, dz, hid, down, mixed_t, d_two)


def back_pairs(size, d_kv_ref, w_k, w_v, kept_ref, send_ref):
    width = w_k.shape[1]
    count = size.length // (2 * CHUNK)
    for e, target in enumerate((kept_ref, send_ref)):

        def step(i, carry):
            at = chunk(i + e * count)
            value = dot_nt(d_kv_ref[at, :width], w_k) + dot_nt(d_kv_ref[at, width:], w_v)
            target[chunk(i), :] = value.astype(target.dtype)
            return carry

        lax.fori_loop(0, count, step, 0)


def turn_rows(size, near_ref, far_ref, left_ref):
    count = size.length // (2 * CHUNK)
    for e, ref in enumerate((near_ref, far_ref)):

        def step(i, carry):
            left_ref[:, chunk(i + e * count)] = jnp.transpose(sequence_rows(ref, i, size.half))
            return carry

        lax.fori_loop(0, count, step, 0)


def back_scratch(size, width):
    rows = size.own // size.z_count
    return [
        pltpu.VMEM((size.length, 1), F32),
        pltpu.VMEM((size.length, 2 * width), F32),
        pltpu.VMEM((width, rows), F32),
        pltpu.VMEM((width // LANES, GROUP * rows, LANES), BF),
        pltpu.VMEM((width // LANES, GROUP * rows, LANES), BF),
        pltpu.VMEM((width // LANES, 1, GROUP * rows), F32),
    ]


def third_kernel(
    size,
    visit_ref,
    place_ref,
    q_ref,
    do_ref,
    o_ref,
    lse_ref,
    kv_ref,
    qseg_ref,
    kseg_ref,
    near_ref,
    far_ref,
    whole_ref,
    hat_ref,
    inv_ref,
    norm_ref,
    d_two_ref,
    sums_in_ref,
    mixed_self_ref,
    kept_rows_ref,
    send_rows_ref,
    kept_ref,
    send_ref,
    d_one_ref,
    d_mixed_ref,
    seg_ref,
    sum_ref,
    dqt_ref,
    qst_ref,
    dst_ref,
    delta_ref,
    d_q_ref,
    d_kv_ref,
    left_ref,
    self_t_ref,
    low_t_ref,
    cols_ref,
    moves,
):
    width = hat_ref.shape[1]
    dp_count = 2 * size.x_count
    sum_ref[...] = jnp.zeros(sum_ref.shape, F32)
    moves.begin()
    turn_segments(kseg_ref, seg_ref)
    attend_back_part(
        visit_ref,
        q_ref,
        do_ref,
        o_ref,
        lse_ref,
        kv_ref,
        qseg_ref,
        seg_ref,
        d_q_ref,
        d_kv_ref,
        sum_ref,
        dqt_ref,
        qst_ref,
        dst_ref,
        delta_ref,
    )
    moves.ready()
    hat, inv, gain = hat_ref[...], inv_ref[...], norm_ref[0:1, :]
    upstream = d_two_ref[...] + dot_nt(d_q_ref[...], whole_ref[1])
    gain_sum = jnp.sum(upstream * hat, axis=0, keepdims=True)
    shift_sum = jnp.sum(upstream, axis=0, keepdims=True)
    d_one = norm_pull(upstream, hat, inv, gain)
    d_one_ref[...] = d_one
    low_one = d_one.astype(BF)
    d_mixed_ref[...] = dot_nt(low_one, whole_ref[0]).astype(BF)
    low_t_ref[...] = jnp.transpose((hat * gain + norm_ref[1:2, :]).astype(BF))
    back_pairs(size, d_kv_ref, whole_ref[2], whole_ref[3], kept_rows_ref, send_rows_ref)
    moves.done(0, 1, 4, 5)
    self_t_ref[...] = jnp.transpose(mixed_self_ref[...])
    pad = jnp.zeros((128 - sums_in_ref.shape[0], width), F32)
    cols_ref[...] = jnp.zeros(cols_ref.shape, F32)
    cols_ref[:, :128] = jnp.transpose(jnp.concatenate([gain_sum, shift_sum, sums_in_ref[2:, :], pad], axis=0))
    turn_rows(size, near_ref, far_ref, left_ref)
    for e, target in enumerate((kept_ref, send_ref)):
        put_grad(target, dot_f32(grad_rows(place_ref, self_t_ref, dp_count, e), low_one), 0, size.tile_rows)
        put_grad(target, dot_f32(grad_rows(place_ref, low_t_ref, dp_count, e), d_q_ref[...]), 1, size.tile_rows)
        lefts = grad_rows(place_ref, left_ref, dp_count, e)
        for t in range(2):
            put_grad(target, dot_f32(lefts, d_kv_ref[:, t * width : (t + 1) * width]), 2 + t, size.tile_rows)
        put_grad(target, grad_rows(place_ref, cols_ref, dp_count, e), 4, size.tile_rows)


def third(
    size, visits, place, q, do, o, lse, kv, qseg, kseg, near, far, whole, hat, inv, norms, d_two, sums, mixed_self
):
    own, width = hat.shape
    group = (size.x_count, size.pieces, 5 * size.tile_rows, width)
    return run_kernel(
        functools.partial(third_kernel, size),
        us=30,
        out_shape=(
            shape((size.length // 2, width)),
            shape((size.length // 2, width)),
            shape(group),
            shape(group),
            shape((own, width), F32),
            shape((own, width)),
        ),
        kinds=[SMEM] * 2 + [NOW] * 7 + [LATER] * 9,
        scratch_shapes=back_scratch(size, width)
        + [
            pltpu.VMEM((own, width), BF),
            pltpu.VMEM((size.length, 2 * width), BF),
            pltpu.VMEM((width, size.length), BF),
            pltpu.VMEM((width, own), BF),
            pltpu.VMEM((width, own), BF),
            pltpu.VMEM((width, width), F32),
        ],
    )(visits, place, q, do, o, lse, kv, qseg, kseg, near, far, whole, hat, inv, norms, d_two, sums, mixed_self)


def fourth_kernel(
    size,
    visit_ref,
    place_ref,
    q_ref,
    do_ref,
    o_ref,
    lse_ref,
    kv_ref,
    qseg_ref,
    kseg_ref,
    whole_ref,
    d_one_ref,
    near_ref,
    far_ref,
    kept_rows_ref,
    send_rows_ref,
    kept_ref,
    send_ref,
    seg_ref,
    sum_ref,
    dqt_ref,
    qst_ref,
    dst_ref,
    delta_ref,
    d_q_ref,
    d_kv_ref,
    left_ref,
    own_t_ref,
    moves,
):
    sum_ref[...] = jnp.zeros(sum_ref.shape, F32)
    moves.begin()
    turn_segments(kseg_ref, seg_ref)
    attend_back_part(
        visit_ref,
        q_ref,
        do_ref,
        o_ref,
        lse_ref,
        kv_ref,
        qseg_ref,
        seg_ref,
        d_q_ref,
        d_kv_ref,
        sum_ref,
        dqt_ref,
        qst_ref,
        dst_ref,
        delta_ref,
    )
    moves.ready()
    back_pairs(size, d_kv_ref, whole_ref[1], whole_ref[2], kept_rows_ref, send_rows_ref)
    mine = d_one_ref[...] + dot_nt(d_q_ref[...], whole_ref[0])
    half = size.half
    y_count = size.length // (2 * half * size.z_count)
    for z in range(size.z_count):
        at = pl.ds(pl.multiple_of((z * y_count + place_ref[3]) * half, half), half)
        total = kept_rows_ref[at, :].astype(F32) + mine[z * half : (z + 1) * half]
        kept_rows_ref[at, :] = total.astype(kept_rows_ref.dtype)
    moves.done(0, 1)
    width = d_one_ref.shape[1]
    dp_count = 2 * size.x_count
    turn_rows(size, near_ref, far_ref, left_ref)
    own_t_ref[...] = jnp.transpose(own_tokens(near_ref, place_ref, half, size.z_count))
    for e, target in enumerate((kept_ref, send_ref)):
        put_grad(target, dot_f32(grad_rows(place_ref, own_t_ref, dp_count, e), d_q_ref[...]), 0, size.tile_rows)
        lefts = grad_rows(place_ref, left_ref, dp_count, e)
        for t in range(2):
            put_grad(target, dot_f32(lefts, d_kv_ref[:, t * width : (t + 1) * width]), 1 + t, size.tile_rows)


def fourth(size, visits, place, q, do, o, lse, kv, qseg, kseg, whole, d_one, near, far):
    own, width = d_one.shape
    group = (size.x_count, size.pieces, 3 * size.tile_rows, width)
    return run_kernel(
        functools.partial(fourth_kernel, size),
        us=27,
        out_shape=(shape((size.length // 2, width)), shape((size.length // 2, width)), shape(group), shape(group)),
        kinds=[SMEM] * 2 + [NOW] * 7 + [LATER] * 4,
        scratch_shapes=back_scratch(size, width)
        + [
            pltpu.VMEM((own, width), BF),
            pltpu.VMEM((size.length, 2 * width), BF),
            pltpu.VMEM((width, size.length), BF),
            pltpu.VMEM((width, own), BF),
        ],
    )(visits, place, q, do, o, lse, kv, qseg, kseg, whole, d_one, near, far)


def together(*values):
    return lax.optimization_barrier(values)


def unxor(parts, place):
    if len(parts) == 2:
        return jnp.where(place == 0, jnp.stack(parts), jnp.stack(parts[::-1]))
    out = jnp.zeros((len(parts),) + parts[0].shape, parts[0].dtype)
    for k, part in enumerate(parts):
        out = lax.dynamic_update_index_in_dim(out, part, place ^ k, 0)
    return out


def body(
    inputs,
    encoder,
    tgt_seg,
    src_len,
    cotangent,
    self_in,
    self_out,
    cross_q,
    cross_kv,
    cross_out,
    ffn_in,
    ffn_out,
    norm_params,
):
    held, local_rows, width = inputs.shape
    half = local_rows // 2
    dp_count, seq_count = lax.axis_size("dp"), lax.axis_size("seq")
    length = local_rows * seq_count
    x_count = dp_count // 2
    z_count = 2 * held
    y_count = seq_count // z_count
    dp_place, seq_place = lax.axis_index("dp"), lax.axis_index("seq")
    x_place, c_place = dp_place // 2, dp_place % 2
    z_place, y_place = seq_place // y_count, seq_place % y_count
    place = jnp.stack([x_place, c_place, z_place, y_place]).astype(jnp.int32)
    rows = self_in.shape[0]
    fine = rows % 16 == 0
    pieces = seq_count if fine else 1
    tile_rows = rows * seq_count // pieces

    def over_core(v):
        return lax.ppermute(v, "dp", [(i, i ^ 1) for i in range(dp_count)])

    def over_x(v, k):
        return v if k == 0 else lax.ppermute(v, "dp", [(i, i ^ (2 * k)) for i in range(dp_count)])

    def over_y(v, k):
        return v if k == 0 else lax.ppermute(v, "seq", [(i, i ^ k) for i in range(seq_count)])

    def over_z(v, k):
        return v if k == 0 else lax.ppermute(v, "seq", [(i, i ^ (k * y_count)) for i in range(seq_count)])

    def pick(v, at, axis=0):
        return lax.dynamic_index_in_dim(v, at, axis, keepdims=False)

    def by_core(mine, other, axis=0):
        return jnp.where(
            c_place == 0, jnp.concatenate([mine, other], axis=axis), jnp.concatenate([other, mine], axis=axis)
        )

    def exchange(v):
        return lax.all_to_all(v, "seq", 0, 0, tiled=True)

    def exchange_z(v):
        groups = [[z * y_count + y for z in range(z_count)] for y in range(y_count)]
        return lax.all_to_all(v, "seq", 0, 0, tiled=True, axis_index_groups=groups)

    def tiles_of(v):
        return v.reshape(rows, -1, width).transpose(1, 0, 2).reshape(-1, width)

    def y_gather(v):
        return y_order(y_moves(v))

    def y_moves(v):
        return [over_y(v, k) for k in range(y_count)]

    def y_order(moves):
        return unxor(moves, y_place).swapaxes(0, 1).reshape((seq_count,) + moves[0].shape[1:])

    def with_weights(blocks, weights):
        weights = weights.reshape(-1, width)
        return jnp.concatenate([blocks, jnp.broadcast_to(weights, (z_count,) + weights.shape)], axis=1)

    def coarse_parts(v, outer):
        whole = lax.all_gather(v, ("dp", "seq"), axis=0).reshape((x_count, 2, seq_count) + v.shape)
        inner = whole[:, :, :, : v.shape[0] - outer].reshape(x_count, 2, seq_count, -1, rows, width)
        inner = inner.swapaxes(2, 3).reshape(x_count, 2, -1, width)
        whole = jnp.concatenate([inner, whole[:, :, :, v.shape[0] - outer :].reshape(x_count, 2, -1, width)], axis=2)
        out = []
        for e in range(2):
            mine = pick(whole, c_place ^ e, 1)
            out.append(jnp.concatenate([pick(mine, x_place ^ k) for k in range(x_count)])[None])
        return out

    def x_moves(kept, came):
        out = [(kept[0].astype(F32) + came[0]).astype(BF)]
        return out + [over_x((kept[k].astype(F32) + came[k]).astype(BF), k) for k in range(1, x_count)]

    def total(values):
        out = values[0].astype(F32)
        for v in values[1:]:
            out = out + v
        return out.astype(BF)

    def by_owner(v, outer):
        if fine:
            return v
        inner = v[0, : v.shape[1] - outer].reshape(-1, seq_count, rows, width).swapaxes(0, 1)
        inner = inner.reshape(seq_count, -1, width)
        return jnp.concatenate([inner, v[0, v.shape[1] - outer :].reshape(seq_count, -1, width)], axis=1)

    def y_parts(v):
        v = v.reshape((z_count, y_count) + v.shape[1:])
        return [over_y(pick(v, y_place ^ k, 1), k) for k in range(y_count)]

    def z_parts(v):
        return [over_z(pick(v, z_place ^ k), k) for k in range(z_count)]

    def untiled(v):
        return v.reshape(-1, rows, width).transpose(1, 0, 2).reshape(rows, -1)

    def home(v):
        v = v.astype(BF).reshape(2, held, half, width)
        mine, other = pick(v, c_place), over_core(pick(v, 1 - c_place))
        mine, other = mine[:, None], other[:, None]
        return by_core(mine, other, 1).reshape(held, local_rows, width).astype(F32)

    notes = jnp.concatenate([tgt_seg, src_len], axis=1)
    notes = pick(by_core(notes, over_core(notes)), z_place)
    target_all, lengths = notes[:length], notes[length:]
    docs = lengths.shape[0]
    upto = lax.broadcasted_iota(jnp.int32, (docs, docs), 0) <= lax.broadcasted_iota(jnp.int32, (docs, docs), 1)
    ends = jnp.sum(jnp.where(upto, lengths[:, None], 0), axis=0, dtype=jnp.int32)
    positions = jnp.arange(length, dtype=jnp.int32)
    source_all = jnp.sum((positions[:, None] >= ends[None, :]).astype(jnp.int32), axis=1, dtype=jnp.int32)
    qseg = pick(target_all.reshape(z_count, y_count * 2, half), y_place * 2 + c_place, 1)
    keys = 2 * half

    def in_order(segments):
        pairs = segments.reshape(-1, 2, half)
        return jnp.where(c_place == 0, pairs, pairs[:, ::-1]).reshape(-1, 1, keys)

    def visits(segments):
        low = jnp.sum((segments[None, :] < qseg[:, :1]).astype(jnp.int32), axis=1, dtype=jnp.int32)
        high = jnp.sum((segments[None, :] <= qseg[:, -1:]).astype(jnp.int32), axis=1, dtype=jnp.int32)
        table = jnp.stack([low // keys, (high + keys - 1) // keys])
        return jnp.pad(table, ((0, 0), (0, length // keys - z_count)))

    self_kseg, cross_kseg = in_order(target_all), in_order(source_all)
    self_visits, cross_visits = visits(target_all), visits(source_all)

    hidden = ffn_in.shape[1]
    outer = ffn_out.shape[0]
    norm_wide = jnp.pad(norm_params, ((0, 0), (0, width - norm_params.shape[1])))
    first_tiles = tiles_of(self_in)
    rest_tiles = tiles_of(jnp.concatenate([self_out, cross_q, cross_kv, cross_out, norm_wide, ffn_in], axis=1))
    rest_tiles = jnp.concatenate([rest_tiles, ffn_out], axis=0)
    mid = 6 * rows
    size = Size(
        half=half,
        length=length,
        own=z_count * half,
        z_count=z_count,
        x_count=x_count,
        pieces=pieces,
        tile_rows=tile_rows,
        hidden=hidden,
        feed_rows=hidden // width * tile_rows + outer * seq_count // pieces,
        first_one=(half,) if fine else (0,),
        first_two=(half,) if fine else (0,),
        first_three=(0,),
    )
    qseg = qseg[:, None, :]
    streams = jnp.stack([inputs, encoder, cotangent]).reshape(3, held, 2, half, width)
    mine = pick(streams, c_place, 2)
    other = over_core(pick(streams, 1 - c_place, 2))
    streams = by_core(mine, other, 1)
    x_blocks, source_blocks, cot = streams[0], streams[1], streams[2]
    if fine:
        x_blocks = with_weights(x_blocks, jnp.stack([over_x(first_tiles, k) for k in range(x_count)]))
        rest = jnp.stack([over_x(rest_tiles, k) for k in range(x_count)])
        source_blocks = with_weights(source_blocks, rest[:, :mid])
        cot = with_weights(cot, rest[:, mid:])
    x_near = exchange_z(x_blocks)
    x_near, source_blocks = together(x_near, source_blocks)
    x_moves_y = y_moves(x_near)
    source_near = exchange_z(source_blocks)
    x_near = y_order(x_moves_y)
    x_far = over_core(x_near)
    x_near, x_far, source_near, cot = together(x_near, x_far, source_near, cot)
    source_moves = y_moves(source_near)
    cot = exchange_z(cot)
    weights = (x_near, x_far) if fine else coarse_parts(first_tiles, 0)

    queries, pairs, whole_one, mixed_self, self_lse = first(
        size, self_visits, place, weights, x_near, x_far, qseg, self_kseg
    )
    whole_one = whole_one.reshape(3, width, width)
    mixed_self, cot, *source_moves = together(mixed_self, cot, *source_moves)
    source_near = y_order(source_moves)
    source_far = over_core(source_near)
    if fine:
        w3_moves = y_moves(cot[:, half:])
        weights = (source_near, source_far)
    else:
        weights = coarse_parts(rest_tiles[:mid], 0)
    queries_c, pairs_c, whole_two, hat_one, inv_one, norms, mixed_cross, cross_lse = second(
        size, cross_visits, place, weights, x_near, source_near, source_far, mixed_self, qseg, cross_kseg
    )
    whole_two = whole_two.reshape(6, width, width)
    if fine:
        mixed_cross, *w3_moves = together(mixed_cross, *w3_moves)
        w3 = y_order(w3_moves)
        weights = (w3, over_core(w3))
    else:
        weights = coarse_parts(rest_tiles[mid:], outer)
    out_low, d_two, d_mixed_c, sums, low_t, dz, hid, down, mixed_ct = feed(
        size, place, weights, mixed_cross, whole_two, hat_one, norms, cot
    )

    f_send = feed_grads(size, 1, place, low_t, dz, hid, down, mixed_ct, d_two)
    f_came = over_core(f_send)
    low_t, f_send, out_low = together(low_t, f_send, out_low)
    f_kept = feed_grads(size, 0, place, low_t, dz, hid, down, mixed_ct, d_two)
    out_parts = exchange_z(out_low.reshape(z_count, half, width))
    d_mixed_c, f_kept, f_came = together(d_mixed_c, f_kept, f_came)
    f_moves = x_moves(f_kept, f_came)
    d_mixed_c, f_first = together(d_mixed_c, f_moves[0])
    s_kept, s_send, c_kept, c_send, d_one, d_mixed = third(
        size,
        cross_visits,
        place,
        queries_c,
        d_mixed_c,
        mixed_cross,
        cross_lse,
        pairs_c,
        qseg,
        cross_kseg,
        source_near,
        source_far,
        whole_two,
        hat_one,
        inv_one,
        norms,
        d_two,
        sums,
        mixed_self,
    )
    s_kept, s_send, c_kept, c_send, d_one, d_mixed, out_parts, f_first, *f_moves = together(
        s_kept, s_send, c_kept, c_send, d_one, d_mixed, out_parts, f_first, *f_moves[1:]
    )
    s_came, c_came = over_core(s_send), over_core(c_send)
    f_sum = by_owner(total([f_first, *f_moves]), hidden // dp_count)
    f_sum, s_came, c_came = together(f_sum, s_came, c_came)
    s_sum = total([s_kept, s_came]).reshape(seq_count, half, width)
    fs_moves = y_parts(jnp.concatenate([f_sum, s_sum], axis=1))
    c_moves = x_moves(c_kept, c_came)
    d_mixed, fs_first, c_first = together(d_mixed, fs_moves[0], c_moves[0])
    x_kept, x_send, i_kept, i_send = fourth(
        size,
        self_visits,
        place,
        queries,
        d_mixed,
        mixed_self,
        self_lse,
        pairs,
        qseg,
        self_kseg,
        whole_one,
        d_one,
        x_near,
        x_far,
    )
    extra = len(fs_moves) - 1
    x_kept, x_send, i_kept, i_send, fs_first, c_first, out_parts, *moves = together(
        x_kept, x_send, i_kept, i_send, fs_first, c_first, out_parts, *fs_moves[1:], *c_moves[1:]
    )
    x_came, i_came = over_core(x_send), over_core(i_send)
    fs_sum = total([fs_first, *moves[:extra]])
    fs_got = exchange_z(fs_sum)
    x_came, i_came, fs_sum = together(x_came, i_came, fs_sum)
    x_moves_y = y_parts(total([x_kept, x_came]).reshape(seq_count, half, width))
    x_first, i_came, i_kept = together(x_moves_y[0], i_came, i_kept)
    i_moves = x_moves(i_kept, i_came)
    c_sum = by_owner(total([c_first, *moves[extra:]]), 0)
    i_first, c_sum, *x_moves_y = together(i_moves[0], c_sum, x_first, *x_moves_y[1:])
    x_parts = z_parts(total(x_moves_y))
    i_sum = by_owner(total([i_first, *i_moves[1:]]), 0)
    w_moves = y_parts(jnp.concatenate([c_sum, i_sum], axis=1))
    w_first, out_parts, fs_got = together(w_moves[0], out_parts, fs_got)
    grad_source = home(fs_got[:, -half:])
    out_tokens = home(out_parts)
    f_own = jnp.sum(fs_got[:, :-half].astype(F32), axis=0)
    w_parts = z_parts(total([w_first, *w_moves[1:]]))
    w_first = w_parts[0]
    w_own = sum(w_parts[1:], w_first.astype(F32))
    c_own, i_own = w_own[: 5 * rows], w_own[5 * rows :]
    grad_tokens = home(unxor(x_parts, z_place))
    f_in = hidden // width * rows
    c_own = c_own.reshape(5, rows, width)
    return (
        out_tokens,
        grad_tokens,
        grad_source,
        untiled(i_own),
        c_own[0],
        c_own[1],
        untiled(c_own[2:4]),
        f_own[f_in : f_in + rows],
        untiled(f_own[:f_in]),
        f_own[f_in + rows :],
        c_own[4][:, : norm_params.shape[1]],
    )


def solution(mesh):
    tokens, rows = P("dp", "seq", None), P(("dp", "seq"), None)
    return jax.shard_map(
        body,
        mesh=mesh,
        in_specs=(tokens, tokens, P("dp", None), P("dp", None), tokens) + (rows,) * 8,
        out_specs=(tokens,) * 3 + (rows,) * 8,
        check_vma=False,
    )
```

```python
import dataclasses
import functools
import math

import jax
import jax.numpy as jnp
from jax import lax
from jax.experimental import pallas as pl
from jax.experimental.pallas import tpu as pltpu
from jax.sharding import PartitionSpec as P

HEAD_DIM = 64
GROUP = 4
LANES = GROUP * HEAD_DIM
PACE = 1.15e9 * 0.1
WIDE = 60
CHUNK = 256
LOG2E = 1.4426950408889634
LN2 = 0.6931471805599453
GELU_A = 0.7978845608028654
GELU_B = 0.044715
BF = jnp.bfloat16
F32 = jnp.float32
SMEM = pl.BlockSpec(memory_space=pltpu.SMEM)
VMEM = pl.BlockSpec(memory_space=pltpu.VMEM)
ANY = pl.BlockSpec(memory_space=pl.ANY)
NOW, LATER = "now", "later"


def dot_f32(left, right):
    return jnp.dot(left, right, preferred_element_type=F32)


def dot_nt(left, right):
    return lax.dot_general(left, right, (((1,), (1,)), ((), ())), preferred_element_type=F32)


def padded_bytes(dims, dtype):
    dims = (1,) * (2 - len(dims)) + tuple(dims)
    lead = math.prod(dims[:-2])
    return lead * (-(-dims[-2] // 16) * 16) * (-(-dims[-1] // 128) * 128) * jnp.dtype(dtype).itemsize


def kernel_call(kernel, *, out_shape, in_specs, out_specs, scratch_shapes=(), spare=3, us=2):
    def call(*operands):
        need = spare * 2**20
        for operand, spec in zip(operands, in_specs):
            need += padded_bytes(operand.shape, operand.dtype) if spec is VMEM else 0
        for result in jax.tree.leaves(out_shape):
            need += padded_bytes(result.shape, result.dtype)
        for scratch in scratch_shapes:
            if getattr(scratch, "memory_space", None) == pltpu.VMEM:
                need += padded_bytes(scratch.shape, scratch.dtype)
        return pl.pallas_call(
            kernel,
            out_shape=out_shape,
            in_specs=in_specs,
            out_specs=out_specs,
            scratch_shapes=scratch_shapes,
            compiler_params=pltpu.CompilerParams(vmem_limit_bytes=need),
            cost_estimate=pl.CostEstimate(flops=int(us * PACE), bytes_accessed=2**10, transcendentals=0),
        )(*operands)

    return call


class Moves:
    def __init__(self, now, late, out):
        self.now, self.late, self.out, self.begun = now, late, out, set()

    def begin(self):
        for copy in self.now:
            copy.wait()

    def ready(self):
        for copy in self.late:
            copy.wait()

    def done(self, *results):
        for i in results:
            self.out[i].start()
            self.begun.add(i)

    def finish(self):
        self.done(*(i for i in range(len(self.out)) if i not in self.begun))
        for copy in self.out:
            copy.wait()


def run_kernel(kernel, *, out_shape, kinds, scratch_shapes=(), us=2):
    def call(*operands):
        moved = [i for i, kind in enumerate(kinds) if kind in (NOW, LATER)]
        count, outs, own = len(kinds), len(out_shape), len(scratch_shapes)

        def wrapped(*refs):
            ins, results, scratch = list(refs[:count]), refs[count : count + outs], refs[count + outs :]
            mine, scratch = scratch[:own], scratch[own:]
            slots, scratch = scratch[: len(moved)], scratch[len(moved) :]
            made, (in_sem, out_sem) = scratch[:outs], scratch[outs:]
            now, late = [], []
            for n, i in enumerate(moved):
                copy = pltpu.make_async_copy(ins[i], slots[n], in_sem.at[n])
                copy.start()
                (now if kinds[i] == NOW else late).append(copy)
                ins[i] = slots[n]
            moves = Moves(now, late, [pltpu.make_async_copy(a, b, out_sem.at[n]) for n, (a, b) in enumerate(zip(made, results))])
            kernel(*ins, *made, *mine, moves=moves)
            moves.finish()

        return pl.pallas_call(
            wrapped,
            out_shape=out_shape,
            in_specs=[SMEM if kind is SMEM else ANY for kind in kinds],
            out_specs=(ANY,) * outs,
            scratch_shapes=list(scratch_shapes)
            + [pltpu.VMEM(operands[i].shape, operands[i].dtype) for i in moved]
            + [pltpu.VMEM(v.shape, v.dtype) for v in out_shape]
            + [pltpu.SemaphoreType.DMA((len(moved),)), pltpu.SemaphoreType.DMA((outs,))],
            compiler_params=pltpu.CompilerParams(vmem_limit_bytes=WIDE * 2**20),
            cost_estimate=pl.CostEstimate(flops=int(us * PACE), bytes_accessed=2**10, transcendentals=0),
        )(*operands)

    return call


def shape(dims, dtype=BF):
    return jax.ShapeDtypeStruct(dims, dtype)


def chunk(i):
    return pl.ds(pl.multiple_of(i * CHUNK, CHUNK), CHUNK)


@dataclasses.dataclass(frozen=True)
class Size:
    half: int
    length: int
    own: int
    z_count: int
    x_count: int
    pieces: int
    tile_rows: int
    hidden: int
    feed_rows: int
    first_one: tuple
    first_two: tuple
    first_three: tuple


def stack_heads(tile):
    head = lax.broadcasted_iota(jnp.int32, tile.shape, 1) // HEAD_DIM
    zero = jnp.zeros_like(tile)
    return jnp.concatenate([jnp.where(head == h, tile, zero) for h in range(GROUP)], axis=0)


def row_of(column):
    return jnp.transpose(jnp.broadcast_to(column, (column.shape[0], 128)))[0:1, :]


def key_rows(b, keys, total):
    half = keys // 2
    at = pl.multiple_of(b * half, half)
    return pl.ds(at, half), pl.ds(pl.multiple_of(at + total // 2, half), half)


def both_rows(ref, spots, cols):
    return jnp.concatenate([ref[spot, cols] for spot in spots], axis=0)


def turn_segments(kseg_ref, seg_ref):
    count, _, keys = kseg_ref.shape
    for b in range(count):
        row = kseg_ref[b].astype(F32)
        seg_ref[b * keys : (b + 1) * keys, :] = jnp.transpose(jnp.broadcast_to(row, (128, keys)))[:, :1]


def attend_part(visit_ref, q_ref, kv_ref, qseg_ref, seg_ref, o_ref, lse_ref, acc_ref, qst_ref):
    width = q_ref.shape[1]
    blocks = qseg_ref.shape[0]
    rows = q_ref.shape[0] // blocks
    total = kv_ref.shape[0]
    keys = total // visit_ref.shape[1]
    groups = width // LANES

    def block(k, carry):
        lo, hi = visit_ref[0, k], visit_ref[1, k]
        q_rows = pl.ds(pl.multiple_of(k * rows, rows), rows)
        qseg = jnp.concatenate([qseg_ref[k].astype(F32)] * GROUP, axis=1)
        for g in range(groups):
            qst_ref[g] = stack_heads(q_ref[q_rows, g * LANES : (g + 1) * LANES])
        acc_ref[...] = jnp.zeros(acc_ref.shape, F32)

        def step(b, carry):
            spots = key_rows(b, keys, total)
            same = seg_ref[pl.ds(pl.multiple_of(b * keys, keys), keys), :] == qseg
            scores = [
                dot_nt(both_rows(kv_ref, spots, slice(g * LANES, (g + 1) * LANES)), qst_ref[g]) for g in range(groups)
            ]
            out, lows, fades = [], [], []
            for g in range(groups):
                top, tot = carry[g]
                masked = jnp.where(same, scores[g], -1e30)
                new = jnp.maximum(top, jnp.max(masked, axis=0, keepdims=True))
                soft = jnp.exp2(masked - new)
                fade = jnp.exp2(top - new)
                out.append((new, tot * fade + jnp.sum(soft, axis=0, keepdims=True)))
                lows.append(soft.astype(BF))
                fades.append(fade)
            for g in range(groups):
                turned = jnp.transpose(both_rows(kv_ref, spots, slice(width + g * LANES, width + (g + 1) * LANES)))
                for h in range(GROUP):
                    at = g * LANES + h * HEAD_DIM
                    cols = slice(h * rows, (h + 1) * rows)
                    values = turned[h * HEAD_DIM : (h + 1) * HEAD_DIM]
                    acc_ref[at : at + HEAD_DIM] = acc_ref[at : at + HEAD_DIM] * fades[g][:, cols] + dot_f32(
                        values, lows[g][:, cols]
                    )
            return tuple(out)

        start = (jnp.full((1, GROUP * rows), -3e38, F32), jnp.zeros((1, GROUP * rows), F32))
        end = lax.fori_loop(lo, hi, step, (start,) * groups)
        for g in range(groups):
            top, tot = end[g]
            inv = 1.0 / tot
            mixed = [
                acc_ref[g * LANES + h * HEAD_DIM : g * LANES + (h + 1) * HEAD_DIM] * inv[:, h * rows : (h + 1) * rows]
                for h in range(GROUP)
            ]
            o_ref[q_rows, g * LANES : (g + 1) * LANES] = jnp.transpose(jnp.concatenate(mixed, axis=0)).astype(BF)
            lse_ref[k * groups + g] = top + jnp.log2(tot)
        return carry

    lax.fori_loop(0, blocks, block, 0)


def attend_back_part(
    visit_ref,
    q_ref,
    do_ref,
    o_ref,
    lse_ref,
    kv_ref,
    qseg_ref,
    seg_ref,
    dq_ref,
    dkv_ref,
    sum_ref,
    dqt_ref,
    qst_ref,
    dst_ref,
    delta_ref,
):
    width = q_ref.shape[1]
    blocks = qseg_ref.shape[0]
    rows = q_ref.shape[0] // blocks
    total = kv_ref.shape[0]
    keys = total // visit_ref.shape[1]
    groups = width // LANES
    def block(k, carry):
        lo, hi = visit_ref[0, k], visit_ref[1, k]
        q_rows = pl.ds(pl.multiple_of(k * rows, rows), rows)
        qseg = jnp.concatenate([qseg_ref[k].astype(F32)] * GROUP, axis=1)
        for g in range(groups):
            cols = slice(g * LANES, (g + 1) * LANES)
            qst_ref[g] = stack_heads(q_ref[q_rows, cols])
            d_mixed = do_ref[q_rows, cols]
            dst_ref[g] = stack_heads(d_mixed)
            prod = d_mixed.astype(F32) * o_ref[q_rows, cols].astype(F32)
            delta_ref[g] = row_of(jnp.sum(stack_heads(prod), axis=1, keepdims=True))
        dqt_ref[...] = jnp.zeros(dqt_ref.shape, F32)

        def step(b, carry):
            spots = key_rows(b, keys, total)
            same = seg_ref[pl.ds(pl.multiple_of(b * keys, keys), keys), :] == qseg
            k_cols = [slice(g * LANES, (g + 1) * LANES) for g in range(groups)]
            v_cols = [slice(width + g * LANES, width + (g + 1) * LANES) for g in range(groups)]
            scores = [dot_nt(both_rows(kv_ref, spots, k_cols[g]), qst_ref[g]) for g in range(groups)]
            d_soft = [dot_nt(both_rows(kv_ref, spots, v_cols[g]), dst_ref[g]) for g in range(groups)]
            softs, d_scores = [], []
            for g in range(groups):
                soft = jnp.where(same, jnp.exp2(scores[g] - lse_ref[k * groups + g]), 0.0)
                d_scores.append((soft * (d_soft[g] - delta_ref[g])).astype(BF))
                softs.append(soft.astype(BF))
            for g in range(groups):
                d_keys, d_values = dot_f32(d_scores[g], qst_ref[g]), dot_f32(softs[g], dst_ref[g])
                for e, spot in enumerate(spots):
                    part = slice(e * keys // 2, (e + 1) * keys // 2)
                    sum_ref[spot, k_cols[g]] += d_keys[part]
                    sum_ref[spot, v_cols[g]] += d_values[part]
                turned = jnp.transpose(both_rows(kv_ref, spots, k_cols[g]))
                for h in range(GROUP):
                    at = slice(g * LANES + h * HEAD_DIM, g * LANES + (h + 1) * HEAD_DIM)
                    keys_t = turned[h * HEAD_DIM : (h + 1) * HEAD_DIM]
                    dqt_ref[at] += dot_f32(keys_t, d_scores[g][:, h * rows : (h + 1) * rows])
            return carry

        lax.fori_loop(lo, hi, step, 0)
        for g in range(groups):
            cols = slice(g * LANES, (g + 1) * LANES)
            dq_ref[q_rows, cols] = (jnp.transpose(dqt_ref[cols]) * HEAD_DIM**-0.5).astype(BF)
        return carry

    lax.fori_loop(0, blocks, block, 0)
    dkv_ref[:, :width] = (sum_ref[:, :width] * LN2).astype(BF)
    dkv_ref[:, width:] = sum_ref[:, width:].astype(BF)


def norm_of(resid):
    centered = resid - jnp.mean(resid, axis=-1, keepdims=True)
    inv = lax.rsqrt(jnp.mean(centered * centered, axis=-1, keepdims=True) + 1e-05)
    return centered * inv, inv


def norm_pull(upstream, hat, inv, gain):
    scaled = upstream * gain
    return inv * (
        scaled - jnp.mean(scaled, axis=-1, keepdims=True) - hat * jnp.mean(scaled * hat, axis=-1, keepdims=True)
    )


def weight_rows(size, weights, total, firsts):
    out = []
    per = len(weights) // 2
    for e in range(2):
        for k in range(size.x_count):
            a = min(k, per - 1)
            out.append((k, e, weights[e * per + a], firsts[a] + (k - a) * total))
    return out


def fetch_tiles(size, place_ref, weights, tiles, firsts, whole_ref, sem):
    copies = []
    rows = size.tile_rows
    for k, e, part, start in weight_rows(size, weights, tiles * rows, firsts):
        pieces = part.shape[0]
        dp = (place_ref[0] ^ k) * 2 + (place_ref[1] ^ e)
        at = pl.ds(pl.multiple_of(dp * pieces, pieces), pieces)
        for t in range(tiles):
            source = part.at[:, pl.ds(start + t * rows, rows)]
            copies.append(pltpu.make_async_copy(source, whole_ref.at[t, at], sem.at[len(copies)]))
    for copy in copies:
        copy.start()
    return copies


def tile_of(ref, t):
    tile = ref[t]
    return tile.reshape(-1, tile.shape[-1])


def own_tokens(near_ref, place_ref, half, z_count):
    y_count = near_ref.shape[0] // z_count
    return jnp.concatenate([near_ref[z * y_count + place_ref[3], :half, :] for z in range(z_count)], axis=0)


def sequence_rows(ref, i, half):
    count = CHUNK // half
    return jnp.concatenate([ref[i * count + j, :half, :] for j in range(count)], axis=0)


def put_pairs(near_ref, far_ref, half, w_k, w_v, kv_ref):
    width = w_k.shape[1]
    count = near_ref.shape[0] * half // CHUNK
    for e, ref in enumerate((near_ref, far_ref)):

        def step(i, carry):
            rows = sequence_rows(ref, i, half)
            at = chunk(i + e * count)
            kv_ref[at, :width] = dot_f32(rows, w_k).astype(BF)
            kv_ref[at, width:] = dot_f32(rows, w_v).astype(BF)
            return carry

        lax.fori_loop(0, count, step, 0)


def grad_rows(place_ref, left_ref, dp_count, e):
    rows = left_ref.shape[0] // dp_count
    out = []
    for k in range(dp_count // 2):
        dp = (place_ref[0] ^ k) * 2 + (place_ref[1] ^ e)
        out.append(left_ref[pl.ds(pl.multiple_of(dp * rows, rows), rows), :])
    return jnp.concatenate(out, axis=0)


def put_grad(target, value, tile, tile_rows):
    x_count, pieces, _, width = target.shape
    rows = value.shape[0] // x_count
    for k in range(x_count):
        part = value[k * rows : (k + 1) * rows].astype(target.dtype)
        target[k, :, tile * tile_rows : (tile + 1) * tile_rows, :] = part.reshape(pieces, tile_rows, width)


def attend_scratch(size, width):
    rows = size.own // size.z_count
    return [
        pltpu.VMEM((size.length, 1), F32),
        pltpu.VMEM((width, rows), F32),
        pltpu.VMEM((width // LANES, GROUP * rows, LANES), BF),
    ]


def first_kernel(
    size,
    visit_ref,
    place_ref,
    near_ref,
    far_ref,
    qseg_ref,
    kseg_ref,
    *refs,
    moves,
):
    weights, (q_ref, kv_ref, whole_ref, o_ref, lse_ref, seg_ref, acc_ref, qst_ref, sem) = refs[:-9], refs[-9:]
    copies = fetch_tiles(size, place_ref, weights, 3, size.first_one, whole_ref, sem)
    moves.begin()
    own = own_tokens(near_ref, place_ref, size.half, size.z_count)
    turn_segments(kseg_ref, seg_ref)
    for copy in copies:
        copy.wait()
    q_ref[...] = (dot_f32(own, tile_of(whole_ref, 0)) * (HEAD_DIM**-0.5 * LOG2E)).astype(BF)
    put_pairs(near_ref, far_ref, size.half, tile_of(whole_ref, 1), tile_of(whole_ref, 2), kv_ref)
    moves.done(0, 1, 2)
    attend_part(visit_ref, q_ref, kv_ref, qseg_ref, seg_ref, o_ref, lse_ref, acc_ref, qst_ref)


def lse_shape(size, width):
    return shape((size.z_count * width // LANES, 1, GROUP * size.half), F32)


def first(size, visits, place, weights, near, far, qseg, kseg):
    width = near.shape[2]
    return run_kernel(
        functools.partial(first_kernel, size),
        us=16,
        out_shape=(
            shape((size.own, width)),
            shape((size.length, 2 * width)),
            shape((3, 2 * size.x_count * size.pieces, size.tile_rows, width)),
            shape((size.own, width)),
            lse_shape(size, width),
        ),
        kinds=[SMEM] * 2 + [NOW] * 4 + [ANY] * len(weights),
        scratch_shapes=attend_scratch(size, width) + [pltpu.SemaphoreType.DMA((2 * size.x_count * 3,))],
    )(visits, place, near, far, qseg, kseg, *weights)


def second_kernel(
    size,
    visit_ref,
    place_ref,
    near_ref,
    source_near_ref,
    source_far_ref,
    mixed_ref,
    qseg_ref,
    kseg_ref,
    *refs,
    moves,
):
    weights = refs[:-12]
    q_ref, kv_ref, whole_ref, hat_ref, inv_ref, norm_ref, o_ref, lse_ref, seg_ref, acc_ref, qst_ref, sem = refs[-12:]
    copies = fetch_tiles(size, place_ref, weights, 6, size.first_two, whole_ref, sem)
    moves.begin()
    own = own_tokens(near_ref, place_ref, size.half, size.z_count)
    turn_segments(kseg_ref, seg_ref)
    for copy in copies:
        copy.wait()
    norm_ref[...] = jnp.transpose(tile_of(whole_ref, 5)[:, :128].astype(F32))[: norm_ref.shape[0]]
    hat, inv = norm_of(own.astype(F32) + dot_f32(mixed_ref[...], tile_of(whole_ref, 0)))
    hat_ref[...] = hat
    inv_ref[...] = inv
    low = (hat * norm_ref[0:1, :] + norm_ref[1:2, :]).astype(BF)
    q_ref[...] = (dot_f32(low, tile_of(whole_ref, 1)) * (HEAD_DIM**-0.5 * LOG2E)).astype(BF)
    moves.ready()
    put_pairs(source_near_ref, source_far_ref, size.half, tile_of(whole_ref, 2), tile_of(whole_ref, 3), kv_ref)
    moves.done(0, 1, 2, 3, 4, 5)
    attend_part(visit_ref, q_ref, kv_ref, qseg_ref, seg_ref, o_ref, lse_ref, acc_ref, qst_ref)


def second(size, visits, place, weights, near, source_near, source_far, mixed, qseg, kseg):
    width = near.shape[2]
    return run_kernel(
        functools.partial(second_kernel, size),
        us=17,
        out_shape=(
            shape((size.own, width)),
            shape((size.length, 2 * width)),
            shape((6, 2 * size.x_count * size.pieces, size.tile_rows, width)),
            shape((size.own, width), F32),
            shape((size.own, 1), F32),
            shape((8, width), F32),
            shape((size.own, width)),
            lse_shape(size, width),
        ),
        kinds=[SMEM] * 2 + [NOW, LATER, LATER, NOW, NOW, NOW] + [ANY] * len(weights),
        scratch_shapes=attend_scratch(size, width) + [pltpu.SemaphoreType.DMA((2 * size.x_count * 6,))],
    )(visits, place, near, source_near, source_far, mixed, qseg, kseg, *weights)


def feed_kernel(
    size,
    place_ref,
    mixed_ref,
    whole_two_ref,
    hat_one_ref,
    norm_ref,
    cot_ref,
    *refs,
):
    weights = refs[:-16]
    (
        out_ref,
        d_two_ref,
        d_mixed_ref,
        sums_ref,
        low_t_ref,
        dz_ref,
        hid_ref,
        down_ref,
        mixed_t_ref,
        w_in_ref,
        w_out_ref,
        z_ref,
        low_ref,
        hat_two_ref,
        inv_two_ref,
        sem,
    ) = refs[-16:]
    own, width = hat_one_ref.shape
    hidden = z_ref.shape[1]
    tiles = hidden // width
    tile_rows = size.tile_rows
    copies = []
    total = size.feed_rows
    for k, e, part, start in weight_rows(size, weights, total, size.first_three):
        pieces = part.shape[0]
        dp = (place_ref[0] ^ k) * 2 + (place_ref[1] ^ e)
        at = pl.ds(pl.multiple_of(dp * pieces, pieces), pieces)
        for t in range(tiles):
            source = part.at[:, pl.ds(start + t * tile_rows, tile_rows)]
            copies.append(pltpu.make_async_copy(source, w_in_ref.at[t, at], sem.at[len(copies)]))
        source = part.at[:, pl.ds(start + tiles * tile_rows, total - tiles * tile_rows)]
        copies.append(pltpu.make_async_copy(source, w_out_ref.at[at], sem.at[len(copies)]))
    for copy in copies:
        copy.start()
    mixed_t_ref[...] = jnp.transpose(mixed_ref[...])
    sums_ref[...] = jnp.zeros(sums_ref.shape, F32)
    cross_out = whole_two_ref[4]
    for copy in copies:
        copy.wait()
    per_tile = w_out_ref.shape[0] // tiles

    def w_down(t):
        return w_out_ref[t * per_tile : (t + 1) * per_tile].reshape(width, width)

    def forward(i, carry):
        at = chunk(i)
        one = hat_one_ref[at, :] * norm_ref[0:1, :] + norm_ref[1:2, :]
        hat, inv = norm_of(one + dot_f32(mixed_ref[at, :], cross_out))
        hat_two_ref[at, :] = hat
        inv_two_ref[at, :] = inv
        two = hat * norm_ref[2:3, :] + norm_ref[3:4, :]
        low = two.astype(BF)
        low_ref[at, :] = low
        total = two
        for t in range(tiles):
            cols = slice(t * width, (t + 1) * width)
            z = dot_f32(low, tile_of(w_in_ref, t))
            z_ref[at, cols] = z
            turn = jnp.tanh(GELU_A * (z + GELU_B * (z * z * z)))
            hid = (0.5 * z * (1.0 + turn)).astype(BF)
            hid_ref[at, cols] = hid
            total = total + dot_f32(hid, w_down(t))
        hat, inv = norm_of(total)
        gain = norm_ref[4:5, :]
        out_ref[at, :] = (hat * gain + norm_ref[5:6, :]).astype(BF)
        upstream = sequence_rows(cot_ref, i, size.half).astype(F32)
        sums_ref[4:5, :] += jnp.sum(upstream * hat, axis=0, keepdims=True)
        sums_ref[5:6, :] += jnp.sum(upstream, axis=0, keepdims=True)
        down = norm_pull(upstream, hat, inv, gain)
        low_down = down.astype(BF)
        down_ref[at, :] = low_down
        back = down
        for t in range(tiles):
            cols = slice(t * width, (t + 1) * width)
            d_hid = dot_nt(low_down, w_down(t))
            z = z_ref[at, cols]
            turn = jnp.tanh(GELU_A * (z + GELU_B * (z * z * z)))
            slope = 0.5 * (1.0 + turn) + (0.5 * GELU_A) * z * (1.0 - turn * turn) * (1.0 + (3.0 * GELU_B) * z * z)
            dz = (d_hid * slope).astype(BF)
            dz_ref[at, cols] = dz
            back = back + dot_nt(dz, tile_of(w_in_ref, t))
        hat, inv = hat_two_ref[at, :], inv_two_ref[at, :]
        sums_ref[2:3, :] += jnp.sum(back * hat, axis=0, keepdims=True)
        sums_ref[3:4, :] += jnp.sum(back, axis=0, keepdims=True)
        d_two = norm_pull(back, hat, inv, norm_ref[2:3, :])
        d_two_ref[at, :] = d_two
        d_mixed_ref[at, :] = dot_nt(d_two.astype(BF), cross_out).astype(BF)
        return carry

    lax.fori_loop(0, own // CHUNK, forward, 0)
    low_t_ref[...] = jnp.transpose(low_ref[...])


def feed(size, place, weights, mixed, whole_two, hat_one, norms, cot):
    own, width = hat_one.shape
    hidden = size.hidden
    devices = 2 * size.x_count * size.pieces
    return kernel_call(
        functools.partial(feed_kernel, size),
        us=12,
        out_shape=(
            shape((own, width)),
            shape((own, width), F32),
            shape((own, width)),
            shape((8, width), F32),
            shape((width, own)),
            shape((own, hidden)),
            shape((own, hidden)),
            shape((own, width)),
            shape((width, own)),
        ),
        in_specs=[SMEM] + [VMEM] * 5 + [ANY] * len(weights),
        out_specs=(VMEM,) * 9,
        scratch_shapes=[
            pltpu.VMEM((hidden // width, devices, size.tile_rows, width), BF),
            pltpu.VMEM((devices, hidden // devices, width), BF),
            pltpu.VMEM((own, hidden), F32),
            pltpu.VMEM((own, width), BF),
            pltpu.VMEM((own, width), F32),
            pltpu.VMEM((own, 1), F32),
            pltpu.SemaphoreType.DMA((2 * size.x_count * (hidden // width + 1),)),
        ],
    )(place, mixed, whole_two, hat_one, norms, cot, *weights)


def feed_grads_kernel(
    size, e, place_ref, low_t_ref, dz_ref, hid_ref, down_ref, mixed_t_ref, d_two_ref, target
):
    width = low_t_ref.shape[0]
    hidden = dz_ref.shape[1]
    tiles = hidden // width
    lefts = grad_rows(place_ref, low_t_ref, 2 * size.x_count, e)
    for t in range(tiles):
        put_grad(target, dot_f32(lefts, dz_ref[:, t * width : (t + 1) * width]), t, size.tile_rows)
    value = dot_f32(grad_rows(place_ref, mixed_t_ref, 2 * size.x_count, e), d_two_ref[...].astype(BF))
    put_grad(target, value, tiles, size.tile_rows)
    rows = hidden // (2 * size.x_count)
    for k in range(size.x_count):
        dp = (place_ref[0] ^ k) * 2 + (place_ref[1] ^ e)
        cols = pl.ds(pl.multiple_of(dp * rows, rows), rows)
        value = dot_f32(jnp.transpose(hid_ref[:, cols]), down_ref[...]).astype(target.dtype)
        target[k, :, (tiles + 1) * size.tile_rows :, :] = value.reshape(size.pieces, rows // size.pieces, width)


def feed_grads(size, e, place, low_t, dz, hid, down, mixed_t, d_two):
    width = low_t.shape[0]
    tiles = size.hidden // width
    rows = (tiles + 1) * size.tile_rows + size.hidden // (2 * size.x_count * size.pieces)
    return kernel_call(
        functools.partial(feed_grads_kernel, size, e),
        out_shape=shape((size.x_count, size.pieces, rows, width)),
        in_specs=[SMEM] + [VMEM] * 6,
        out_specs=VMEM,
    )(place, low_t, dz, hid, down, mixed_t, d_two)


def back_pairs(size, d_kv_ref, w_k, w_v, kept_ref, send_ref):
    width = w_k.shape[1]
    count = size.length // (2 * CHUNK)
    for e, target in enumerate((kept_ref, send_ref)):

        def step(i, carry):
            at = chunk(i + e * count)
            value = dot_nt(d_kv_ref[at, :width], w_k) + dot_nt(d_kv_ref[at, width:], w_v)
            target[chunk(i), :] = value.astype(target.dtype)
            return carry

        lax.fori_loop(0, count, step, 0)


def turn_rows(size, near_ref, far_ref, left_ref):
    count = size.length // (2 * CHUNK)
    for e, ref in enumerate((near_ref, far_ref)):

        def step(i, carry):
            left_ref[:, chunk(i + e * count)] = jnp.transpose(sequence_rows(ref, i, size.half))
            return carry

        lax.fori_loop(0, count, step, 0)


def back_scratch(size, width):
    rows = size.own // size.z_count
    return [
        pltpu.VMEM((size.length, 1), F32),
        pltpu.VMEM((size.length, 2 * width), F32),
        pltpu.VMEM((width, rows), F32),
        pltpu.VMEM((width // LANES, GROUP * rows, LANES), BF),
        pltpu.VMEM((width // LANES, GROUP * rows, LANES), BF),
        pltpu.VMEM((width // LANES, 1, GROUP * rows), F32),
    ]


def third_kernel(
    size,
    visit_ref,
    place_ref,
    q_ref,
    do_ref,
    o_ref,
    lse_ref,
    kv_ref,
    qseg_ref,
    kseg_ref,
    near_ref,
    far_ref,
    whole_ref,
    hat_ref,
    inv_ref,
    norm_ref,
    d_two_ref,
    sums_in_ref,
    mixed_self_ref,
    kept_rows_ref,
    send_rows_ref,
    kept_ref,
    send_ref,
    d_one_ref,
    d_mixed_ref,
    seg_ref,
    sum_ref,
    dqt_ref,
    qst_ref,
    dst_ref,
    delta_ref,
    d_q_ref,
    d_kv_ref,
    left_ref,
    self_t_ref,
    low_t_ref,
    cols_ref,
    moves,
):
    width = hat_ref.shape[1]
    dp_count = 2 * size.x_count
    sum_ref[...] = jnp.zeros(sum_ref.shape, F32)
    moves.begin()
    turn_segments(kseg_ref, seg_ref)
    attend_back_part(
        visit_ref,
        q_ref,
        do_ref,
        o_ref,
        lse_ref,
        kv_ref,
        qseg_ref,
        seg_ref,
        d_q_ref,
        d_kv_ref,
        sum_ref,
        dqt_ref,
        qst_ref,
        dst_ref,
        delta_ref,
    )
    moves.ready()
    hat, inv, gain = hat_ref[...], inv_ref[...], norm_ref[0:1, :]
    upstream = d_two_ref[...] + dot_nt(d_q_ref[...], whole_ref[1])
    gain_sum = jnp.sum(upstream * hat, axis=0, keepdims=True)
    shift_sum = jnp.sum(upstream, axis=0, keepdims=True)
    d_one = norm_pull(upstream, hat, inv, gain)
    d_one_ref[...] = d_one
    low_one = d_one.astype(BF)
    d_mixed_ref[...] = dot_nt(low_one, whole_ref[0]).astype(BF)
    low_t_ref[...] = jnp.transpose((hat * gain + norm_ref[1:2, :]).astype(BF))
    back_pairs(size, d_kv_ref, whole_ref[2], whole_ref[3], kept_rows_ref, send_rows_ref)
    moves.done(0, 1, 4, 5)
    self_t_ref[...] = jnp.transpose(mixed_self_ref[...])
    pad = jnp.zeros((128 - sums_in_ref.shape[0], width), F32)
    cols_ref[...] = jnp.zeros(cols_ref.shape, F32)
    cols_ref[:, :128] = jnp.transpose(jnp.concatenate([gain_sum, shift_sum, sums_in_ref[2:, :], pad], axis=0))
    turn_rows(size, near_ref, far_ref, left_ref)
    for e, target in enumerate((kept_ref, send_ref)):
        put_grad(target, dot_f32(grad_rows(place_ref, self_t_ref, dp_count, e), low_one), 0, size.tile_rows)
        put_grad(target, dot_f32(grad_rows(place_ref, low_t_ref, dp_count, e), d_q_ref[...]), 1, size.tile_rows)
        lefts = grad_rows(place_ref, left_ref, dp_count, e)
        for t in range(2):
            put_grad(target, dot_f32(lefts, d_kv_ref[:, t * width : (t + 1) * width]), 2 + t, size.tile_rows)
        put_grad(target, grad_rows(place_ref, cols_ref, dp_count, e), 4, size.tile_rows)


def third(
    size, visits, place, q, do, o, lse, kv, qseg, kseg, near, far, whole, hat, inv, norms, d_two, sums, mixed_self
):
    own, width = hat.shape
    group = (size.x_count, size.pieces, 5 * size.tile_rows, width)
    return run_kernel(
        functools.partial(third_kernel, size),
        us=30,
        out_shape=(
            shape((size.length // 2, width)),
            shape((size.length // 2, width)),
            shape(group),
            shape(group),
            shape((own, width), F32),
            shape((own, width)),
        ),
        kinds=[SMEM] * 2 + [NOW] * 7 + [LATER] * 9,
        scratch_shapes=back_scratch(size, width)
        + [
            pltpu.VMEM((own, width), BF),
            pltpu.VMEM((size.length, 2 * width), BF),
            pltpu.VMEM((width, size.length), BF),
            pltpu.VMEM((width, own), BF),
            pltpu.VMEM((width, own), BF),
            pltpu.VMEM((width, width), F32),
        ],
    )(visits, place, q, do, o, lse, kv, qseg, kseg, near, far, whole, hat, inv, norms, d_two, sums, mixed_self)


def fourth_kernel(
    size,
    visit_ref,
    place_ref,
    q_ref,
    do_ref,
    o_ref,
    lse_ref,
    kv_ref,
    qseg_ref,
    kseg_ref,
    whole_ref,
    d_one_ref,
    near_ref,
    far_ref,
    kept_rows_ref,
    send_rows_ref,
    kept_ref,
    send_ref,
    seg_ref,
    sum_ref,
    dqt_ref,
    qst_ref,
    dst_ref,
    delta_ref,
    d_q_ref,
    d_kv_ref,
    left_ref,
    own_t_ref,
    moves,
):
    sum_ref[...] = jnp.zeros(sum_ref.shape, F32)
    moves.begin()
    turn_segments(kseg_ref, seg_ref)
    attend_back_part(
        visit_ref,
        q_ref,
        do_ref,
        o_ref,
        lse_ref,
        kv_ref,
        qseg_ref,
        seg_ref,
        d_q_ref,
        d_kv_ref,
        sum_ref,
        dqt_ref,
        qst_ref,
        dst_ref,
        delta_ref,
    )
    moves.ready()
    back_pairs(size, d_kv_ref, whole_ref[1], whole_ref[2], kept_rows_ref, send_rows_ref)
    mine = d_one_ref[...] + dot_nt(d_q_ref[...], whole_ref[0])
    half = size.half
    y_count = size.length // (2 * half * size.z_count)
    for z in range(size.z_count):
        at = pl.ds(pl.multiple_of((z * y_count + place_ref[3]) * half, half), half)
        total = kept_rows_ref[at, :].astype(F32) + mine[z * half : (z + 1) * half]
        kept_rows_ref[at, :] = total.astype(kept_rows_ref.dtype)
    moves.done(0, 1)
    width = d_one_ref.shape[1]
    dp_count = 2 * size.x_count
    turn_rows(size, near_ref, far_ref, left_ref)
    own_t_ref[...] = jnp.transpose(own_tokens(near_ref, place_ref, half, size.z_count))
    for e, target in enumerate((kept_ref, send_ref)):
        put_grad(target, dot_f32(grad_rows(place_ref, own_t_ref, dp_count, e), d_q_ref[...]), 0, size.tile_rows)
        lefts = grad_rows(place_ref, left_ref, dp_count, e)
        for t in range(2):
            put_grad(target, dot_f32(lefts, d_kv_ref[:, t * width : (t + 1) * width]), 1 + t, size.tile_rows)


def fourth(size, visits, place, q, do, o, lse, kv, qseg, kseg, whole, d_one, near, far):
    own, width = d_one.shape
    group = (size.x_count, size.pieces, 3 * size.tile_rows, width)
    return run_kernel(
        functools.partial(fourth_kernel, size),
        us=27,
        out_shape=(shape((size.length // 2, width)), shape((size.length // 2, width)), shape(group), shape(group)),
        kinds=[SMEM] * 2 + [NOW] * 7 + [LATER] * 4,
        scratch_shapes=back_scratch(size, width)
        + [
            pltpu.VMEM((own, width), BF),
            pltpu.VMEM((size.length, 2 * width), BF),
            pltpu.VMEM((width, size.length), BF),
            pltpu.VMEM((width, own), BF),
        ],
    )(visits, place, q, do, o, lse, kv, qseg, kseg, whole, d_one, near, far)


def together(*values):
    return lax.optimization_barrier(values)


def unxor(parts, place):
    if len(parts) == 2:
        return jnp.where(place == 0, jnp.stack(parts), jnp.stack(parts[::-1]))
    out = jnp.zeros((len(parts),) + parts[0].shape, parts[0].dtype)
    for k, part in enumerate(parts):
        out = lax.dynamic_update_index_in_dim(out, part, place ^ k, 0)
    return out


def body(
    inputs,
    encoder,
    tgt_seg,
    src_len,
    cotangent,
    self_in,
    self_out,
    cross_q,
    cross_kv,
    cross_out,
    ffn_in,
    ffn_out,
    norm_params,
):
    held, local_rows, width = inputs.shape
    half = local_rows // 2
    dp_count, seq_count = lax.axis_size("dp"), lax.axis_size("seq")
    length = local_rows * seq_count
    x_count = dp_count // 2
    z_count = 2 * held
    y_count = seq_count // z_count
    dp_place, seq_place = lax.axis_index("dp"), lax.axis_index("seq")
    x_place, c_place = dp_place // 2, dp_place % 2
    z_place, y_place = seq_place // y_count, seq_place % y_count
    place = jnp.stack([x_place, c_place, z_place, y_place]).astype(jnp.int32)
    rows = self_in.shape[0]
    fine = rows % 16 == 0
    pieces = seq_count if fine else 1
    tile_rows = rows * seq_count // pieces

    def over_core(v):
        return lax.ppermute(v, "dp", [(i, i ^ 1) for i in range(dp_count)])

    def over_x(v, k):
        return v if k == 0 else lax.ppermute(v, "dp", [(i, i ^ (2 * k)) for i in range(dp_count)])

    def over_y(v, k):
        return v if k == 0 else lax.ppermute(v, "seq", [(i, i ^ k) for i in range(seq_count)])

    def over_z(v, k):
        return v if k == 0 else lax.ppermute(v, "seq", [(i, i ^ (k * y_count)) for i in range(seq_count)])

    def pick(v, at, axis=0):
        return lax.dynamic_index_in_dim(v, at, axis, keepdims=False)

    def by_core(mine, other, axis=0):
        return jnp.where(
            c_place == 0, jnp.concatenate([mine, other], axis=axis), jnp.concatenate([other, mine], axis=axis)
        )

    def exchange(v):
        return lax.all_to_all(v, "seq", 0, 0, tiled=True)

    def exchange_z(v):
        groups = [[z * y_count + y for z in range(z_count)] for y in range(y_count)]
        return lax.all_to_all(v, "seq", 0, 0, tiled=True, axis_index_groups=groups)

    def tiles_of(v):
        return v.reshape(rows, -1, width).transpose(1, 0, 2).reshape(-1, width)

    def y_gather(v):
        return y_order(y_moves(v))

    def y_moves(v):
        return [over_y(v, k) for k in range(y_count)]

    def y_order(moves):
        return unxor(moves, y_place).swapaxes(0, 1).reshape((seq_count,) + moves[0].shape[1:])

    def with_weights(blocks, weights):
        weights = weights.reshape(-1, width)
        return jnp.concatenate([blocks, jnp.broadcast_to(weights, (z_count,) + weights.shape)], axis=1)

    def coarse_parts(v, outer):
        whole = lax.all_gather(v, ("dp", "seq"), axis=0).reshape((x_count, 2, seq_count) + v.shape)
        inner = whole[:, :, :, : v.shape[0] - outer].reshape(x_count, 2, seq_count, -1, rows, width)
        inner = inner.swapaxes(2, 3).reshape(x_count, 2, -1, width)
        whole = jnp.concatenate([inner, whole[:, :, :, v.shape[0] - outer :].reshape(x_count, 2, -1, width)], axis=2)
        out = []
        for e in range(2):
            mine = pick(whole, c_place ^ e, 1)
            out.append(jnp.concatenate([pick(mine, x_place ^ k) for k in range(x_count)])[None])
        return out

    def x_moves(kept, came):
        out = [(kept[0].astype(F32) + came[0]).astype(BF)]
        return out + [over_x((kept[k].astype(F32) + came[k]).astype(BF), k) for k in range(1, x_count)]

    def total(values):
        out = values[0].astype(F32)
        for v in values[1:]:
            out = out + v
        return out.astype(BF)

    def by_owner(v, outer):
        if fine:
            return v
        inner = v[0, : v.shape[1] - outer].reshape(-1, seq_count, rows, width).swapaxes(0, 1)
        inner = inner.reshape(seq_count, -1, width)
        return jnp.concatenate([inner, v[0, v.shape[1] - outer :].reshape(seq_count, -1, width)], axis=1)

    def y_parts(v):
        v = v.reshape((z_count, y_count) + v.shape[1:])
        return [over_y(pick(v, y_place ^ k, 1), k) for k in range(y_count)]

    def z_parts(v):
        return [over_z(pick(v, z_place ^ k), k) for k in range(z_count)]

    def untiled(v):
        return v.reshape(-1, rows, width).transpose(1, 0, 2).reshape(rows, -1)

    def home(v):
        v = v.astype(BF).reshape(2, held, half, width)
        mine, other = pick(v, c_place), over_core(pick(v, 1 - c_place))
        mine, other = mine[:, None], other[:, None]
        return by_core(mine, other, 1).reshape(held, local_rows, width).astype(F32)

    notes = jnp.concatenate([tgt_seg, src_len], axis=1)
    notes = pick(by_core(notes, over_core(notes)), z_place)
    target_all, lengths = notes[:length], notes[length:]
    docs = lengths.shape[0]
    upto = lax.broadcasted_iota(jnp.int32, (docs, docs), 0) <= lax.broadcasted_iota(jnp.int32, (docs, docs), 1)
    ends = jnp.sum(jnp.where(upto, lengths[:, None], 0), axis=0, dtype=jnp.int32)
    positions = jnp.arange(length, dtype=jnp.int32)
    source_all = jnp.sum((positions[:, None] >= ends[None, :]).astype(jnp.int32), axis=1, dtype=jnp.int32)
    qseg = pick(target_all.reshape(z_count, y_count * 2, half), y_place * 2 + c_place, 1)
    keys = 2 * half

    def in_order(segments):
        pairs = segments.reshape(-1, 2, half)
        return jnp.where(c_place == 0, pairs, pairs[:, ::-1]).reshape(-1, 1, keys)

    def visits(segments):
        low = jnp.sum((segments[None, :] < qseg[:, :1]).astype(jnp.int32), axis=1, dtype=jnp.int32)
        high = jnp.sum((segments[None, :] <= qseg[:, -1:]).astype(jnp.int32), axis=1, dtype=jnp.int32)
        table = jnp.stack([low // keys, (high + keys - 1) // keys])
        return jnp.pad(table, ((0, 0), (0, length // keys - z_count)))

    self_kseg, cross_kseg = in_order(target_all), in_order(source_all)
    self_visits, cross_visits = visits(target_all), visits(source_all)

    hidden = ffn_in.shape[1]
    outer = ffn_out.shape[0]
    norm_wide = jnp.pad(norm_params, ((0, 0), (0, width - norm_params.shape[1])))
    first_tiles = tiles_of(self_in)
    rest_tiles = tiles_of(jnp.concatenate([self_out, cross_q, cross_kv, cross_out, norm_wide, ffn_in], axis=1))
    rest_tiles = jnp.concatenate([rest_tiles, ffn_out], axis=0)
    mid = 6 * rows
    size = Size(
        half=half,
        length=length,
        own=z_count * half,
        z_count=z_count,
        x_count=x_count,
        pieces=pieces,
        tile_rows=tile_rows,
        hidden=hidden,
        feed_rows=hidden // width * tile_rows + outer * seq_count // pieces,
        first_one=(half,) if fine else (0,),
        first_two=(half,) if fine else (0,),
        first_three=(0,),
    )
    qseg = qseg[:, None, :]
    streams = jnp.stack([inputs, encoder, cotangent]).reshape(3, held, 2, half, width)
    mine = pick(streams, c_place, 2)
    other = over_core(pick(streams, 1 - c_place, 2))
    streams = by_core(mine, other, 1)
    x_blocks, source_blocks, cot = streams[0], streams[1], streams[2]
    if fine:
        x_blocks = with_weights(x_blocks, jnp.stack([over_x(first_tiles, k) for k in range(x_count)]))
        rest = jnp.stack([over_x(rest_tiles, k) for k in range(x_count)])
        source_blocks = with_weights(source_blocks, rest[:, :mid])
        cot = with_weights(cot, rest[:, mid:])
    x_near = exchange_z(x_blocks)
    x_near, source_blocks = together(x_near, source_blocks)
    x_moves_y = y_moves(x_near)
    source_near = exchange_z(source_blocks)
    x_near = y_order(x_moves_y)
    x_far = over_core(x_near)
    x_near, x_far, source_near, cot = together(x_near, x_far, source_near, cot)
    source_moves = y_moves(source_near)
    cot = exchange_z(cot)
    weights = (x_near, x_far) if fine else coarse_parts(first_tiles, 0)

    queries, pairs, whole_one, mixed_self, self_lse = first(
        size, self_visits, place, weights, x_near, x_far, qseg, self_kseg
    )
    whole_one = whole_one.reshape(3, width, width)
    mixed_self, cot, *source_moves = together(mixed_self, cot, *source_moves)
    source_near = y_order(source_moves)
    source_far = over_core(source_near)
    if fine:
        w3_moves = y_moves(cot[:, half:])
        weights = (source_near, source_far)
    else:
        weights = coarse_parts(rest_tiles[:mid], 0)
    queries_c, pairs_c, whole_two, hat_one, inv_one, norms, mixed_cross, cross_lse = second(
        size, cross_visits, place, weights, x_near, source_near, source_far, mixed_self, qseg, cross_kseg
    )
    whole_two = whole_two.reshape(6, width, width)
    if fine:
        mixed_cross, *w3_moves = together(mixed_cross, *w3_moves)
        w3 = y_order(w3_moves)
        weights = (w3, over_core(w3))
    else:
        weights = coarse_parts(rest_tiles[mid:], outer)
    out_low, d_two, d_mixed_c, sums, low_t, dz, hid, down, mixed_ct = feed(
        size, place, weights, mixed_cross, whole_two, hat_one, norms, cot
    )

    f_send = feed_grads(size, 1, place, low_t, dz, hid, down, mixed_ct, d_two)
    f_came = over_core(f_send)
    low_t, f_send, out_low = together(low_t, f_send, out_low)
    f_kept = feed_grads(size, 0, place, low_t, dz, hid, down, mixed_ct, d_two)
    out_parts = exchange_z(out_low.reshape(z_count, half, width))
    d_mixed_c, f_kept, f_came = together(d_mixed_c, f_kept, f_came)
    f_moves = x_moves(f_kept, f_came)
    d_mixed_c, f_first = together(d_mixed_c, f_moves[0])
    s_kept, s_send, c_kept, c_send, d_one, d_mixed = third(
        size,
        cross_visits,
        place,
        queries_c,
        d_mixed_c,
        mixed_cross,
        cross_lse,
        pairs_c,
        qseg,
        cross_kseg,
        source_near,
        source_far,
        whole_two,
        hat_one,
        inv_one,
        norms,
        d_two,
        sums,
        mixed_self,
    )
    s_kept, s_send, c_kept, c_send, d_one, d_mixed, out_parts, f_first, *f_moves = together(
        s_kept, s_send, c_kept, c_send, d_one, d_mixed, out_parts, f_first, *f_moves[1:]
    )
    s_came, c_came = over_core(s_send), over_core(c_send)
    f_sum = by_owner(total([f_first, *f_moves]), hidden // dp_count)
    f_sum, s_came, c_came = together(f_sum, s_came, c_came)
    s_sum = total([s_kept, s_came]).reshape(seq_count, half, width)
    fs_moves = y_parts(jnp.concatenate([f_sum, s_sum], axis=1))
    c_moves = x_moves(c_kept, c_came)
    d_mixed, fs_first, c_first = together(d_mixed, fs_moves[0], c_moves[0])
    x_kept, x_send, i_kept, i_send = fourth(
        size,
        self_visits,
        place,
        queries,
        d_mixed,
        mixed_self,
        self_lse,
        pairs,
        qseg,
        self_kseg,
        whole_one,
        d_one,
        x_near,
        x_far,
    )
    extra = len(fs_moves) - 1
    x_kept, x_send, i_kept, i_send, fs_first, c_first, out_parts, *moves = together(
        x_kept, x_send, i_kept, i_send, fs_first, c_first, out_parts, *fs_moves[1:], *c_moves[1:]
    )
    x_came, i_came = over_core(x_send), over_core(i_send)
    fs_sum = total([fs_first, *moves[:extra]])
    fs_got = exchange_z(fs_sum)
    x_came, i_came, fs_sum = together(x_came, i_came, fs_sum)
    x_moves_y = y_parts(total([x_kept, x_came]).reshape(seq_count, half, width))
    x_first, i_came, i_kept = together(x_moves_y[0], i_came, i_kept)
    i_moves = x_moves(i_kept, i_came)
    c_sum = by_owner(total([c_first, *moves[extra:]]), 0)
    out_tokens = home(out_parts)
    out_tokens, i_first, c_sum, *x_moves_y = together(out_tokens, i_moves[0], c_sum, x_first, *x_moves_y[1:])
    x_parts = z_parts(total(x_moves_y))
    i_sum = by_owner(total([i_first, *i_moves[1:]]), 0)
    w_moves = y_parts(jnp.concatenate([c_sum, i_sum], axis=1))
    w_first, fs_got = together(w_moves[0], fs_got)
    grad_source = home(fs_got[:, -half:])
    f_own = jnp.sum(fs_got[:, :-half].astype(F32), axis=0)
    w_parts = z_parts(total([w_first, *w_moves[1:]]))
    w_first = w_parts[0]
    w_own = sum(w_parts[1:], w_first.astype(F32))
    c_own, i_own = w_own[: 5 * rows], w_own[5 * rows :]
    grad_tokens = home(unxor(x_parts, z_place))
    f_in = hidden // width * rows
    c_own = c_own.reshape(5, rows, width)
    return (
        out_tokens,
        grad_tokens,
        grad_source,
        untiled(i_own),
        c_own[0],
        c_own[1],
        untiled(c_own[2:4]),
        f_own[f_in : f_in + rows],
        untiled(f_own[:f_in]),
        f_own[f_in + rows :],
        c_own[4][:, : norm_params.shape[1]],
    )


def solution(mesh):
    tokens, rows = P("dp", "seq", None), P(("dp", "seq"), None)
    return jax.shard_map(
        body,
        mesh=mesh,
        in_specs=(tokens, tokens, P("dp", None), P("dp", None), tokens) + (rows,) * 8,
        out_specs=(tokens,) * 3 + (rows,) * 8,
        check_vma=False,
    )
```
